32 devices in a mesh: dp: 8 (over z, x), mp: 4 (over y, core).
Axes of the slice: x: 2, y: 2, z: 4, core: 2. Of those that a mesh axis runs over, the one named last changes fastest.
Arguments:
- features: bfloat16 [1024, 1536], P('dp', 'mp'), may hold values from -240 to 240
- proj_weight: bfloat16 [1536, 1152], P('mp'), may hold values from -0.15625 to 0.15625
- texts: bfloat16 [1024, 1152], P(('dp', 'mp')), may hold values from -6 to 6
Outputs:
- grad_features: bfloat16 [1024, 1536], P('dp', 'mp')
- grad_weight: float32 [1536, 1152], P('mp')
The draws below stay inside these ranges and needn't reach their ends.
All inputs are finite; a program needn't handle non-finite values.
Results may differ from the reference program's by a relative error of at most 0.011.
Values may be sent and summed in bfloat16 or wider, within the bound.
No kernel may reach another device: no remote copies, remote signals or barrier semaphores. Data moves between devices by JAX's collectives and lax.ppermute only.
A program may use at most 64 MiB of HBM per device.

```python
import math
import jax
import jax.numpy as jnp
from jax import lax

W = 1536
E = 1152
BATCH = 1024


def draw_features(key, part):
    key = jax.random.fold_in(key, 11)
    key_base, key_cols, key_rows = jax.random.split(key, 3)
    columns = jnp.arange(W, dtype=jnp.float32) / (W - 1)
    col_scale = 3.0 ** columns * jax.random.uniform(key_cols, (W,), jnp.float32, 0.7, 1.4)
    row_scale = jnp.exp(jax.random.uniform(key_rows, (BATCH, 1), jnp.float32, 0.0, math.log(10.0)))
    base = jnp.clip(jax.random.normal(key_base, (BATCH, W), jnp.float32), -4.0, 4.0)
    values = base * col_scale[None, :] * row_scale
    return values.astype(jnp.bfloat16)


def block_levels(key, shape, pieces, smallest, top_value):
    gain = 1.0
    for axis_at, blocks in pieces:
        heights = jax.random.uniform(jax.random.fold_in(jax.random.fold_in(key, 6), axis_at), (blocks,), jnp.float32, smallest / len(pieces), top_value / len(pieces))
        gain = gain * jnp.repeat(jnp.exp(heights), shape[axis_at] // blocks).reshape((-1,) + (1,) * (len(shape) - 1 - axis_at))
    return gain


def normal_values(key, dims, scale, limit, cuts=(), kind=jnp.bfloat16):
    level = block_levels(key, dims, cuts, -0.22, 0.18) if cuts else 1.0
    entries = jax.random.normal(key, dims, jnp.float32) * scale * level
    return jnp.minimum(jnp.maximum(entries, -limit), limit).astype(kind)


def setup_inputs(seed: int = 0) -> dict:
    keys = jax.random.split(jax.random.key(seed), 4)
    features = draw_features(jax.random.fold_in(keys[3], 71), 0)
    proj_weight = normal_values(keys[1], (W, E), W ** -0.5, 0.15625, ((0, 4),))
    texts = normal_values(keys[2], (BATCH, E), 1.0, 6.0, ((0, 32),))
    return dict(features=features, proj_weight=proj_weight, texts=texts)


logit_scale = 100.0
logit_bias = -10.0
epsilon = 1e-06

def unit_rows(values):
    return values * lax.rsqrt(lax.optimization_barrier(jnp.sum(values * values, axis=1, keepdims=True)) + epsilon)

def reference(features, proj_weight, texts):
    inputs = features.astype(jnp.float32)
    mean_in = lax.optimization_barrier(jnp.mean(inputs, axis=1, keepdims=True))
    centred = inputs - mean_in
    normed_b = centred.astype(jnp.bfloat16)
    project = jnp.dot(normed_b, proj_weight, preferred_element_type=jnp.float32)
    inv_norm = lax.rsqrt(lax.optimization_barrier(jnp.sum(project * project, axis=1, keepdims=True)) + epsilon)
    unit_img = project * inv_norm
    unit_img_b = unit_img.astype(jnp.bfloat16)
    unit_txt_b = unit_rows(texts.astype(jnp.float32)).astype(jnp.bfloat16)
    total = unit_txt_b.shape[0]
    text_ids = jnp.arange(total, dtype=jnp.int32)
    block = math.gcd(total, 512)

    def one_block(pair):
        rows_b, row_ids = pair
        logits = logit_scale * jnp.dot(rows_b, unit_txt_b.T, preferred_element_type=jnp.float32) + logit_bias
        labels = jnp.where(row_ids[:, None] == text_ids[None, :], 1.0, -1.0).astype(jnp.float32)
        slopes = (-labels * jax.nn.sigmoid(-labels * logits)).astype(jnp.bfloat16)
        return logit_scale * jnp.dot(slopes, unit_txt_b, preferred_element_type=jnp.float32)
    grad_unit = lax.map(one_block, (unit_img_b.reshape(total // block, block, -1), text_ids.reshape(total // block, block)))
    grad_unit = grad_unit.reshape(total, -1)
    grad_proj = inv_norm * (grad_unit - unit_img * lax.optimization_barrier(jnp.sum(unit_img * grad_unit, axis=1, keepdims=True)))
    grad_proj_b = grad_proj.astype(jnp.bfloat16)
    grad_weight = jnp.dot(normed_b.T, grad_proj_b, preferred_element_type=jnp.float32)
    grad_normed = jnp.dot(grad_proj_b, proj_weight.T, preferred_element_type=jnp.float32)
    grad_mean = lax.optimization_barrier(jnp.mean(grad_normed, axis=1, keepdims=True))
    grad_in = grad_normed - grad_mean
    return (grad_in.astype(jnp.bfloat16), grad_weight)
```

```python
import functools

import jax
import jax.numpy as jnp
from jax import lax
from jax.experimental import pallas as pl
from jax.experimental.pallas import tpu as pltpu
from jax.sharding import PartitionSpec as P

logit_scale = 100.0
logit_bias = -10.0
epsilon = 1e-06
LANES = 128
GATHER_BYTES = 8 << 20
VMEM_BYTES = 40 << 20


def unit_rows(values):
    return values * lax.rsqrt(jnp.sum(values * values, axis=1, keepdims=True) + epsilon)


def add_texts(unit_img_b, image_ids, piece, piece_ids):
    unit_txt_b = unit_rows(piece.astype(jnp.float32)).astype(jnp.bfloat16)
    logits = (
        logit_scale * jnp.dot(unit_img_b, unit_txt_b.T, preferred_element_type=jnp.float32)
        + logit_bias
    )
    labels = jnp.where(image_ids[:, None] == piece_ids[None, :], 1.0, -1.0).astype(jnp.float32)
    slopes = (-labels * jax.nn.sigmoid(-labels * logits)).astype(jnp.bfloat16)
    return logit_scale * jnp.dot(slopes, unit_txt_b, preferred_element_type=jnp.float32)


def shards_summed(features, proj_weight, texts):
    local_rows = features.shape[0]
    width_local = features.shape[1]
    mp_count = lax.axis_size("mp")
    full_width = width_local * mp_count
    mp_index = lax.axis_index("mp")
    dp_index = lax.axis_index("dp")
    text_rows = texts.shape[0]
    inputs = features.astype(jnp.float32)
    mean_in = lax.psum(jnp.sum(inputs, axis=1, keepdims=True), "mp") / full_width
    centred = inputs - mean_in
    normed_b = centred.astype(jnp.bfloat16)
    partial_proj = jnp.dot(normed_b, proj_weight, preferred_element_type=jnp.float32)
    project = lax.psum(partial_proj, "mp")
    inv_norm = lax.rsqrt(jnp.sum(project * project, axis=1, keepdims=True) + epsilon)
    unit_img = project * inv_norm
    unit_img_b = unit_img.astype(jnp.bfloat16)
    image_ids = dp_index * local_rows + jnp.arange(local_rows, dtype=jnp.int32)
    piece = lax.all_gather(texts, "dp", axis=0, tiled=True)
    positions = jnp.arange(piece.shape[0], dtype=jnp.int32)
    shard_of = positions // text_rows
    piece_ids = (shard_of * mp_count + mp_index) * text_rows + positions % text_rows
    grad_unit = add_texts(unit_img_b, image_ids, piece, piece_ids)
    grad_unit = lax.psum(grad_unit, "mp")
    grad_proj = inv_norm * (
        grad_unit - unit_img * jnp.sum(unit_img * grad_unit, axis=1, keepdims=True)
    )
    grad_proj_b = grad_proj.astype(jnp.bfloat16)
    weight_part = jnp.dot(normed_b.T, grad_proj_b, preferred_element_type=jnp.float32)
    grad_weight = lax.psum(weight_part, "dp")
    grad_normed = jnp.dot(grad_proj_b, proj_weight.T, preferred_element_type=jnp.float32)
    grad_total = lax.psum(jnp.sum(grad_normed, axis=1, keepdims=True), "mp")
    grad_in = grad_normed - grad_total / full_width
    return (grad_in.astype(jnp.bfloat16), grad_weight)


def split_terms(value, count):
    terms = []
    for _ in range(count):
        term = value.astype(jnp.bfloat16).astype(jnp.float32)
        terms.append(term)
        value = value - term
    return terms


def kernel_call(body, outs, scratch=(), **names):
    return pl.pallas_call(
        body,
        out_shape=outs,
        scratch_shapes=scratch,
        compiler_params=pltpu.CompilerParams(vmem_limit_bytes=VMEM_BYTES),
        **names,
    )


def texts_body(texts_ref, out_ref):
    out_ref[...] = unit_rows(texts_ref[...].astype(jnp.float32)).astype(jnp.bfloat16)


def project_body(rows, features_ref, weight_ref, out_ref, extra_ref):
    embed = weight_ref.shape[1]
    local_rows, width = features_ref.shape
    values = features_ref[...].astype(jnp.float32)
    row_sum = jnp.sum(values, axis=1, keepdims=True)
    centred = (values - row_sum / width).astype(jnp.bfloat16)
    out_ref[:, :embed] = jnp.dot(
        centred, weight_ref[...], preferred_element_type=jnp.float32
    ).astype(jnp.bfloat16)
    column_sum = jnp.sum(weight_ref[...].astype(jnp.float32), axis=0, keepdims=True)
    extra_ref[...] = jnp.zeros_like(extra_ref)
    at = 0
    for term in split_terms(column_sum, 2):
        for i in range(embed // LANES):
            extra_ref[at : at + 1, :] = term[:, i * LANES : (i + 1) * LANES]
            at += 1
    row = lax.broadcasted_iota(jnp.int32, (local_rows, LANES), 0)
    lane = lax.broadcasted_iota(jnp.int32, (local_rows, LANES), 1)
    sum_row = jnp.sum(jnp.where(row == lane, row_sum, 0.0), axis=0, keepdims=True)
    for term in split_terms(sum_row, 3):
        extra_ref[at : at + 1, :] = term
        at += 1
    extra = extra_ref[...].astype(jnp.bfloat16)
    for i in range(local_rows // rows):
        out_ref[i * rows : (i + 1) * rows, embed:] = extra


def images_body(
    full_width, place_ref, own_ref, *refs
):
    parts = (own_ref,) + refs[:-3]
    texts_ref, out_ref, weight_sum_ref = refs[-3:]
    rows = own_ref.shape[0]
    embed = own_ref.shape[1] - LANES
    chunks = embed // LANES
    width = full_width // len(parts)
    row = lax.broadcasted_iota(jnp.int32, (rows, LANES), 0)
    lane = lax.broadcasted_iota(jnp.int32, (rows, LANES), 1)
    mine = lane == row + place_ref[1] * rows
    project = jnp.zeros((rows, embed), jnp.float32)
    weight_sum = jnp.zeros((1, embed), jnp.float32)
    sums = []
    column_sums = []
    for part in parts:
        project = project + part[:, :embed].astype(jnp.float32)
        extra = part[:, embed:].astype(jnp.float32)
        column_sum = jnp.concatenate(
            [extra[i : i + 1] + extra[chunks + i : chunks + i + 1] for i in range(chunks)], axis=1
        )
        at = 2 * chunks
        sum_row = extra[at : at + 1] + extra[at + 1 : at + 2] + extra[at + 2 : at + 3]
        sums.append(jnp.sum(jnp.where(mine, sum_row, 0.0), axis=1, keepdims=True))
        column_sums.append(column_sum)
        weight_sum = weight_sum + column_sum
    mean = sum(sums) / full_width
    for part_sum, column_sum in zip(sums, column_sums):
        project = project + (part_sum / width - mean) * column_sum
    weight_sum_ref[...] = weight_sum
    inv_norm = lax.rsqrt(jnp.sum(project * project, axis=1, keepdims=True) + epsilon)
    unit_img = project * inv_norm
    unit_txt_b = texts_ref[...]
    logits = (
        logit_scale
        * lax.dot_general(
            unit_img.astype(jnp.bfloat16),
            unit_txt_b,
            (((1,), (1,)), ((), ())),
            preferred_element_type=jnp.float32,
        )
        + logit_bias
    )
    text = lax.broadcasted_iota(jnp.int32, logits.shape, 1)
    image = lax.broadcasted_iota(jnp.int32, logits.shape, 0) + place_ref[0] * rows
    labels = jnp.where(text == image, 1.0, -1.0)
    slopes = (-labels / (1.0 + jnp.exp(labels * logits))).astype(jnp.bfloat16)
    grad_unit = logit_scale * jnp.dot(slopes, unit_txt_b, preferred_element_type=jnp.float32)
    grad_proj = inv_norm * (
        grad_unit - unit_img * jnp.sum(unit_img * grad_unit, axis=1, keepdims=True)
    )
    out_ref[:, :embed] = grad_proj.astype(jnp.bfloat16)
    mean_terms = split_terms(mean, 3)
    extra = jnp.zeros((rows, LANES), jnp.float32)
    for i, term in enumerate(mean_terms):
        extra = jnp.where(lane == i, term, extra)
    out_ref[:, embed:] = extra.astype(jnp.bfloat16)


def weight_body(
    full_width, rows, group, order, place_ref, features_ref, weight_ref, weight_sum_ref, *refs
):
    (*gathered, grad_features_ref, grad_weight_ref, normed_ref, own_ref) = refs
    embed = weight_ref.shape[1]
    here = place_ref[0]
    per = gathered[0].shape[0] // rows
    total = None
    for g, part in enumerate(gathered):
        extra = part[:, embed:].astype(jnp.float32)
        mean = extra[:, 0:1] + extra[:, 1:2] + extra[:, 2:3]
        for i in range(per):
            device = here ^ order[g * per + i]
            block = features_ref[pl.ds(pl.multiple_of(device * rows, rows), rows), :]
            normed_ref[i * rows : (i + 1) * rows, :] = (
                block.astype(jnp.float32) - mean[i * rows : (i + 1) * rows]
            ).astype(jnp.bfloat16)
            if order[g * per + i] < group:
                slot = (here & (group - 1)) ^ order[g * per + i]
                own_ref[pl.ds(pl.multiple_of(slot * rows, rows), rows), :] = part[
                    i * rows : (i + 1) * rows, :embed
                ]
        product = lax.dot_general(
            normed_ref[...],
            part[:, :embed],
            (((0,), (0,)), ((), ())),
            preferred_element_type=jnp.float32,
        )
        total = product if total is None else total + product
    grad_weight_ref[...] = total
    own = own_ref[...]
    grad_normed = lax.dot_general(
        own, weight_ref[...], (((1,), (1,)), ((), ())), preferred_element_type=jnp.float32
    )
    grad_total = jnp.sum(
        own.astype(jnp.float32) * weight_sum_ref[...], axis=1, keepdims=True
    )
    grad_features_ref[...] = (grad_normed - grad_total / full_width).astype(jnp.bfloat16)


def shards_gathered(features, proj_weight, texts):
    axes = ("dp", "mp")
    dp_count, mp_count = lax.axis_size("dp"), lax.axis_size("mp")
    count = dp_count * mp_count
    local_rows, width = features.shape
    embed = proj_weight.shape[1]
    rows = texts.shape[0]
    full_width = width * mp_count
    mp_index = lax.axis_index("mp")
    device = lax.axis_index("dp") * mp_count + mp_index
    place = jnp.stack([device, mp_index]).astype(jnp.int32)

    def swap(value, flip):
        return lax.ppermute(value, axes, [(i, i ^ flip) for i in range(count)])

    smem = pl.BlockSpec(memory_space=pltpu.SMEM)
    vmem = pl.BlockSpec(memory_space=pltpu.VMEM)

    unit_txt_b = kernel_call(
        texts_body, jax.ShapeDtypeStruct(texts.shape, jnp.bfloat16), name="unit_texts"
    )(texts)
    all_texts = lax.all_gather(unit_txt_b, axes, axis=0, tiled=True)
    all_features = lax.all_gather(features, "dp", axis=0, tiled=True)

    partial = kernel_call(
        functools.partial(project_body, rows),
        jax.ShapeDtypeStruct((local_rows, embed + LANES), jnp.bfloat16),
        scratch=[pltpu.VMEM((rows, LANES), jnp.float32)],
        name="project",
    )(features, proj_weight)

    def quarter(index):
        return lax.dynamic_slice_in_dim(partial, index * rows, rows, axis=0)

    received = [swap(quarter(mp_index ^ flip), flip) for flip in range(1, mp_count)]
    grad_rows, weight_sum = kernel_call(
        functools.partial(images_body, full_width),
        (
            jax.ShapeDtypeStruct((rows, embed + LANES), jnp.bfloat16),
            jax.ShapeDtypeStruct((1, embed), jnp.float32),
        ),
        in_specs=[smem] + [vmem] * (mp_count + 1),
        name="images",
    )(place, quarter(mp_index), *received, all_texts)

    flips = [1 << i for i in reversed(range(count.bit_length() - 1))]
    order = [0]
    held = grad_rows
    for flip in flips[:-1]:
        held = jnp.concatenate([held, swap(held, flip)], axis=0)
        order = order + [o ^ flip for o in order]
    gathered = [held, swap(held, flips[-1])]
    order = order + [o ^ flips[-1] for o in order]

    return tuple(
        kernel_call(
            functools.partial(weight_body, full_width, rows, mp_count, tuple(order)),
            (
                jax.ShapeDtypeStruct(features.shape, jnp.bfloat16),
                jax.ShapeDtypeStruct(proj_weight.shape, jnp.float32),
            ),
            scratch=[
                pltpu.VMEM((count * rows // len(gathered), width), jnp.bfloat16),
                pltpu.VMEM((local_rows, embed), jnp.bfloat16),
            ],
            in_specs=[smem] + [vmem] * (3 + len(gathered)),
            name="weight",
        )(place, all_features, proj_weight, weight_sum, *gathered)
    )


def shards(features, proj_weight, texts):
    dp_count, mp_count = lax.axis_size("dp"), lax.axis_size("mp")
    count = dp_count * mp_count
    rows = texts.shape[0]
    embed = texts.shape[1]
    fits = (
        count * rows * (embed + LANES) * 2 <= GATHER_BYTES
        and count & (count - 1) == 0
        and mp_count & (mp_count - 1) == 0
        and features.shape[0] == LANES == mp_count * rows
        and embed % LANES == 0
        and 2 * (embed // LANES) + 3 <= rows
        and rows % 16 == 0
    )
    plan = shards_gathered if fits else shards_summed
    return plan(features, proj_weight, texts)


def solution(mesh):
    return jax.shard_map(
        shards,
        mesh=mesh,
        in_specs=(P("dp", "mp"), P("mp", None), P(("dp", "mp"), None)),
        out_specs=(P("dp", "mp"), P("mp", None)),
        check_vma=False,
    )
```

```python
import functools

import jax
import jax.numpy as jnp
from jax import lax
from jax.experimental import pallas as pl
from jax.experimental.pallas import tpu as pltpu
from jax.sharding import PartitionSpec as P

logit_scale = 100.0
logit_bias = -10.0
epsilon = 1e-06
LANES = 128
GATHER_BYTES = 8 << 20
VMEM_BYTES = 40 << 20


def unit_rows(values):
    return values * lax.rsqrt(jnp.sum(values * values, axis=1, keepdims=True) + epsilon)


def add_texts(unit_img_b, image_ids, piece, piece_ids):
    unit_txt_b = unit_rows(piece.astype(jnp.float32)).astype(jnp.bfloat16)
    logits = (
        logit_scale * jnp.dot(unit_img_b, unit_txt_b.T, preferred_element_type=jnp.float32)
        + logit_bias
    )
    labels = jnp.where(image_ids[:, None] == piece_ids[None, :], 1.0, -1.0).astype(jnp.float32)
    slopes = (-labels * jax.nn.sigmoid(-labels * logits)).astype(jnp.bfloat16)
    return logit_scale * jnp.dot(slopes, unit_txt_b, preferred_element_type=jnp.float32)


def shards_summed(features, proj_weight, texts):
    local_rows = features.shape[0]
    width_local = features.shape[1]
    mp_count = lax.axis_size("mp")
    full_width = width_local * mp_count
    mp_index = lax.axis_index("mp")
    dp_index = lax.axis_index("dp")
    text_rows = texts.shape[0]
    inputs = features.astype(jnp.float32)
    mean_in = lax.psum(jnp.sum(inputs, axis=1, keepdims=True), "mp") / full_width
    centred = inputs - mean_in
    normed_b = centred.astype(jnp.bfloat16)
    partial_proj = jnp.dot(normed_b, proj_weight, preferred_element_type=jnp.float32)
    project = lax.psum(partial_proj, "mp")
    inv_norm = lax.rsqrt(jnp.sum(project * project, axis=1, keepdims=True) + epsilon)
    unit_img = project * inv_norm
    unit_img_b = unit_img.astype(jnp.bfloat16)
    image_ids = dp_index * local_rows + jnp.arange(local_rows, dtype=jnp.int32)
    piece = lax.all_gather(texts, "dp", axis=0, tiled=True)
    positions = jnp.arange(piece.shape[0], dtype=jnp.int32)
    shard_of = positions // text_rows
    piece_ids = (shard_of * mp_count + mp_index) * text_rows + positions % text_rows
    grad_unit = add_texts(unit_img_b, image_ids, piece, piece_ids)
    grad_unit = lax.psum(grad_unit, "mp")
    grad_proj = inv_norm * (
        grad_unit - unit_img * jnp.sum(unit_img * grad_unit, axis=1, keepdims=True)
    )
    grad_proj_b = grad_proj.astype(jnp.bfloat16)
    weight_part = jnp.dot(normed_b.T, grad_proj_b, preferred_element_type=jnp.float32)
    grad_weight = lax.psum(weight_part, "dp")
    grad_normed = jnp.dot(grad_proj_b, proj_weight.T, preferred_element_type=jnp.float32)
    grad_total = lax.psum(jnp.sum(grad_normed, axis=1, keepdims=True), "mp")
    grad_in = grad_normed - grad_total / full_width
    return (grad_in.astype(jnp.bfloat16), grad_weight)


def split_terms(value, count):
    terms = []
    for _ in range(count):
        term = value.astype(jnp.bfloat16).astype(jnp.float32)
        terms.append(term)
        value = value - term
    return terms


def kernel_call(body, outs, scratch=(), **names):
    return pl.pallas_call(
        body,
        out_shape=outs,
        scratch_shapes=scratch,
        compiler_params=pltpu.CompilerParams(vmem_limit_bytes=VMEM_BYTES),
        **names,
    )


def split_columns(embed):
    return embed // LANES // 3 * LANES


def texts_body(texts_ref, out_ref):
    out_ref[...] = unit_rows(texts_ref[...].astype(jnp.float32)).astype(jnp.bfloat16)


def project_body(rows, place_ref, features_ref, weight_ref, *refs):
    (*outs, extra_ref) = refs
    embed = weight_ref.shape[1]
    local_rows, width = features_ref.shape
    values = features_ref[...].astype(jnp.float32)
    row_sum = jnp.sum(values, axis=1, keepdims=True)
    column_sum = jnp.sum(weight_ref[...].astype(jnp.float32), axis=0, keepdims=True)
    extra_ref[...] = jnp.zeros_like(extra_ref)
    at = 0
    for term in split_terms(column_sum, 2):
        for i in range(embed // LANES):
            extra_ref[at : at + 1, :] = term[:, i * LANES : (i + 1) * LANES]
            at += 1
    row = lax.broadcasted_iota(jnp.int32, (local_rows, LANES), 0)
    lane = lax.broadcasted_iota(jnp.int32, (local_rows, LANES), 1)
    sum_row = jnp.sum(jnp.where(row == lane, row_sum, 0.0), axis=0, keepdims=True)
    for term in split_terms(sum_row, 3):
        extra_ref[at : at + 1, :] = term
        at += 1
    extra = extra_ref[...].astype(jnp.bfloat16)
    ordered = []
    for flip in range(len(outs)):
        start = pl.multiple_of((place_ref[0] ^ flip) * rows, rows)
        block = features_ref[pl.ds(start, rows), :].astype(jnp.float32)
        block_sum = jnp.sum(block, axis=1, keepdims=True)
        ordered.append(block - block_sum / width)
    centred = jnp.concatenate(ordered, axis=0).astype(jnp.bfloat16)
    product = jnp.dot(centred, weight_ref[...], preferred_element_type=jnp.float32)
    for flip, out_ref in enumerate(outs):
        out_ref[:, :embed] = product[flip * rows : (flip + 1) * rows].astype(jnp.bfloat16)
        out_ref[:, embed:] = extra


def unit_body(full_width, place_ref, *refs):
    (*parts, unit_b_ref, unit_ref, inv_norm_ref, mean_ref, weight_sum_ref) = refs
    rows = parts[0].shape[0]
    embed = parts[0].shape[1] - LANES
    chunks = embed // LANES
    width = full_width // len(parts)
    row = lax.broadcasted_iota(jnp.int32, (rows, LANES), 0)
    lane = lax.broadcasted_iota(jnp.int32, (rows, LANES), 1)
    mine = lane == row + place_ref[0] * rows
    project = jnp.zeros((rows, embed), jnp.float32)
    weight_sum = jnp.zeros((1, embed), jnp.float32)
    sums = []
    column_sums = []
    for part in parts:
        project = project + part[:, :embed].astype(jnp.float32)
        extra = part[:, embed:].astype(jnp.float32)
        column_sum = jnp.concatenate(
            [extra[i : i + 1] + extra[chunks + i : chunks + i + 1] for i in range(chunks)], axis=1
        )
        at = 2 * chunks
        sum_row = extra[at : at + 1] + extra[at + 1 : at + 2] + extra[at + 2 : at + 3]
        sums.append(jnp.sum(jnp.where(mine, sum_row, 0.0), axis=1, keepdims=True))
        column_sums.append(column_sum)
        weight_sum = weight_sum + column_sum
    mean = sum(sums) / full_width
    for part_sum, column_sum in zip(sums, column_sums):
        project = project + (part_sum / width - mean) * column_sum
    inv_norm = lax.rsqrt(jnp.sum(project * project, axis=1, keepdims=True) + epsilon)
    unit_img = project * inv_norm
    unit_ref[...] = unit_img
    unit_b_ref[...] = unit_img.astype(jnp.bfloat16)
    inv_norm_ref[...] = inv_norm
    mean_ref[...] = mean
    weight_sum_ref[...] = weight_sum


def slopes_body(mp_count, *refs):
    images, texts = refs[:mp_count], refs[mp_count : -mp_count]
    outs = refs[-mp_count:]
    rows = images[0].shape[0]
    unit_img_b = jnp.concatenate([ref[...] for ref in images], axis=0)
    unit_txt_b = jnp.concatenate([ref[...] for ref in texts], axis=0)
    logits = (
        logit_scale
        * lax.dot_general(
            unit_img_b,
            unit_txt_b,
            (((1,), (1,)), ((), ())),
            preferred_element_type=jnp.float32,
        )
        + logit_bias
    )
    text = lax.broadcasted_iota(jnp.int32, logits.shape, 1)
    image = lax.broadcasted_iota(jnp.int32, logits.shape, 0)
    labels = jnp.where((text == image) & (image < rows), 1.0, -1.0)
    slopes = (-labels / (1.0 + jnp.exp(labels * logits))).astype(jnp.bfloat16)
    grad_unit = logit_scale * jnp.dot(slopes, unit_txt_b, preferred_element_type=jnp.float32)
    for flip, out_ref in enumerate(outs):
        out_ref[...] = grad_unit[flip * rows : (flip + 1) * rows].astype(out_ref.dtype)


def grad_body(unit_ref, inv_norm_ref, mean_ref, *refs):
    (*parts, first_ref, second_ref) = refs
    rows, embed = unit_ref.shape
    cut = first_ref.shape[1]
    grad_unit = sum(part[...].astype(jnp.float32) for part in parts)
    unit_img = unit_ref[...]
    grad_proj = inv_norm_ref[...] * (
        grad_unit - unit_img * jnp.sum(unit_img * grad_unit, axis=1, keepdims=True)
    )
    grad_proj_b = grad_proj.astype(jnp.bfloat16)
    first_ref[...] = grad_proj_b[:, :cut]
    second_ref[:, : embed - cut] = grad_proj_b[:, cut:]
    lane = lax.broadcasted_iota(jnp.int32, (rows, LANES), 1)
    extra = jnp.zeros((rows, LANES), jnp.float32)
    for i, term in enumerate(split_terms(mean_ref[...], 3)):
        extra = jnp.where(lane == i, term, extra)
    second_ref[:, embed - cut :] = extra.astype(jnp.bfloat16)


def weight_body(
    full_width, rows, mp_count, dp_count, first_order, second_order, place_ref, weight_ref,
    weight_sum_ref, *refs
):
    (*arrays, grad_features_ref, grad_weight_ref, all_ref, normed_ref, own_ref) = refs
    features = arrays[:dp_count]
    first = arrays[dp_count : dp_count + len(first_order)]
    second = arrays[dp_count + len(first_order) :]
    embed = weight_ref.shape[1]
    cut = first[0].shape[1]
    for part, order in zip(first, first_order):
        for i, flip in enumerate(order):
            all_ref[flip * rows : (flip + 1) * rows, :cut] = part[i * rows : (i + 1) * rows, :]
    for part, order in zip(second, second_order):
        for i, flip in enumerate(order):
            here = slice(i * rows, (i + 1) * rows)
            there = slice(flip * rows, (flip + 1) * rows)
            all_ref[there, cut:] = part[here, : embed - cut]
            extra = part[here, embed - cut :].astype(jnp.float32)
            mean = extra[:, 0:1] + extra[:, 1:2] + extra[:, 2:3]
            start = pl.multiple_of((place_ref[0] ^ (flip % mp_count)) * rows, rows)
            block = features[flip // mp_count][pl.ds(start, rows), :].astype(jnp.float32)
            normed_ref[there, :] = (block - mean).astype(jnp.bfloat16)
    for flip in range(mp_count):
        start = pl.multiple_of((place_ref[0] ^ flip) * rows, rows)
        own_ref[pl.ds(start, rows), :] = all_ref[flip * rows : (flip + 1) * rows, :]
    grad_weight_ref[...] = lax.dot_general(
        normed_ref[...],
        all_ref[...],
        (((0,), (0,)), ((), ())),
        preferred_element_type=jnp.float32,
    )
    own = own_ref[...]
    grad_normed = lax.dot_general(
        own, weight_ref[...], (((1,), (1,)), ((), ())), preferred_element_type=jnp.float32
    )
    grad_total = jnp.sum(own.astype(jnp.float32) * weight_sum_ref[...], axis=1, keepdims=True)
    grad_features_ref[...] = (grad_normed - grad_total / full_width).astype(jnp.bfloat16)


def shards_gathered(features, proj_weight, texts):
    axes = ("dp", "mp")
    dp_count, mp_count = lax.axis_size("dp"), lax.axis_size("mp")
    count = dp_count * mp_count
    local_rows, width = features.shape
    embed = proj_weight.shape[1]
    rows = texts.shape[0]
    full_width = width * mp_count
    cut = split_columns(embed)
    place = lax.axis_index("mp").astype(jnp.int32).reshape(1)

    def swap(value, flip):
        return lax.ppermute(value, axes, [(i, i ^ flip) for i in range(count)])

    def struct(dims, kind=jnp.bfloat16):
        return jax.ShapeDtypeStruct(dims, kind)

    smem = pl.BlockSpec(memory_space=pltpu.SMEM)
    vmem = pl.BlockSpec(memory_space=pltpu.VMEM)
    mp_flips = range(1, mp_count)
    dp_flips = range(mp_count, count, mp_count)

    partial = kernel_call(
        functools.partial(project_body, rows),
        [struct((rows, embed + LANES))] * mp_count,
        scratch=[pltpu.VMEM((rows, LANES), jnp.float32)],
        in_specs=[smem, vmem, vmem],
        name="project",
    )(place, features, proj_weight)
    parts = [partial[0]] + [swap(partial[flip], flip) for flip in mp_flips]

    unit_txt_b = kernel_call(texts_body, struct(texts.shape), name="unit_texts")(texts)
    all_texts = [unit_txt_b] + [swap(unit_txt_b, flip) for flip in dp_flips]
    all_features = [features] + [swap(features, flip) for flip in dp_flips]

    unit_img_b, unit_img, inv_norm, mean, weight_sum = kernel_call(
        functools.partial(unit_body, full_width),
        [
            struct((rows, embed)),
            struct((rows, embed), jnp.float32),
            struct((rows, 1), jnp.float32),
            struct((rows, 1), jnp.float32),
            struct((1, embed), jnp.float32),
        ],
        in_specs=[smem] + [vmem] * mp_count,
        name="unit_images",
    )(place, *parts)
    images = [unit_img_b] + [swap(unit_img_b, flip) for flip in mp_flips]

    grad_parts = kernel_call(
        functools.partial(slopes_body, mp_count),
        [struct((rows, embed), jnp.float32)] + [struct((rows, embed))] * (mp_count - 1),
        name="slopes",
    )(*images, *all_texts)
    grad_parts = [grad_parts[0]] + [swap(grad_parts[flip], flip) for flip in mp_flips]

    first, second = kernel_call(
        grad_body,
        [struct((rows, cut)), struct((rows, embed - cut + LANES))],
        name="grad_project",
    )(unit_img, inv_norm, mean, *grad_parts)

    line = [f for f in dp_flips if f % (2 * mp_count) == 0]
    plane = [f for f in range(2, 2 * mp_count, 2)]

    def gather(value, stages):
        held, orders = [value], [[0]]
        for flips in stages:
            value = jnp.concatenate(held, axis=0) if len(held) > 1 else held[0]
            order = sum(orders, [])
            held = [value] + [swap(value, flip) for flip in flips]
            orders = [order] + [[o ^ flip for o in order] for flip in flips]
        others = [swap(value, 1) for value in held]
        return held + others, orders + [[o ^ 1 for o in order] for order in orders]

    first, first_order = gather(first, [plane, line])
    second, second_order = gather(second, [line, plane])

    return tuple(
        kernel_call(
            functools.partial(
                weight_body, full_width, rows, mp_count, dp_count, first_order, second_order
            ),
            [struct(features.shape), struct(proj_weight.shape, jnp.float32)],
            scratch=[
                pltpu.VMEM((count * rows, embed), jnp.bfloat16),
                pltpu.VMEM((count * rows, width), jnp.bfloat16),
                pltpu.VMEM((local_rows, embed), jnp.bfloat16),
            ],
            in_specs=[smem] + [vmem] * (2 + dp_count + len(first) + len(second)),
            name="weight",
        )(place, proj_weight, weight_sum, *all_features, *first, *second)
    )


def shards(features, proj_weight, texts):
    dp_count, mp_count = lax.axis_size("dp"), lax.axis_size("mp")
    count = dp_count * mp_count
    rows = texts.shape[0]
    embed = texts.shape[1]
    fits = (
        count * rows * (embed + LANES) * 2 <= GATHER_BYTES
        and count & (count - 1) == 0
        and mp_count & (mp_count - 1) == 0
        and features.shape[0] == LANES == mp_count * rows
        and embed % LANES == 0
        and 2 * (embed // LANES) + 3 <= rows
        and rows % 16 == 0
    )
    plan = shards_gathered if fits else shards_summed
    return plan(features, proj_weight, texts)


def solution(mesh):
    return jax.shard_map(
        shards,
        mesh=mesh,
        in_specs=(P("dp", "mp"), P("mp", None), P(("dp", "mp"), None)),
        out_specs=(P("dp", "mp"), P("mp", None)),
        check_vma=False,
    )
```

```python
import functools

import jax
import jax.numpy as jnp
from jax import lax
from jax.experimental import pallas as pl
from jax.experimental.pallas import tpu as pltpu
from jax.sharding import PartitionSpec as P

logit_scale = 100.0
logit_bias = -10.0
epsilon = 1e-06
LANES = 128
GATHER_BYTES = 8 << 20
VMEM_BYTES = 40 << 20


def unit_rows(values):
    return values * lax.rsqrt(jnp.sum(values * values, axis=1, keepdims=True) + epsilon)


def add_texts(unit_img_b, image_ids, piece, piece_ids):
    unit_txt_b = unit_rows(piece.astype(jnp.float32)).astype(jnp.bfloat16)
    logits = (
        logit_scale * jnp.dot(unit_img_b, unit_txt_b.T, preferred_element_type=jnp.float32)
        + logit_bias
    )
    labels = jnp.where(image_ids[:, None] == piece_ids[None, :], 1.0, -1.0).astype(jnp.float32)
    slopes = (-labels * jax.nn.sigmoid(-labels * logits)).astype(jnp.bfloat16)
    return logit_scale * jnp.dot(slopes, unit_txt_b, preferred_element_type=jnp.float32)


def shards_summed(features, proj_weight, texts):
    local_rows = features.shape[0]
    width_local = features.shape[1]
    mp_count = lax.axis_size("mp")
    full_width = width_local * mp_count
    mp_index = lax.axis_index("mp")
    dp_index = lax.axis_index("dp")
    text_rows = texts.shape[0]
    inputs = features.astype(jnp.float32)
    mean_in = lax.psum(jnp.sum(inputs, axis=1, keepdims=True), "mp") / full_width
    centred = inputs - mean_in
    normed_b = centred.astype(jnp.bfloat16)
    partial_proj = jnp.dot(normed_b, proj_weight, preferred_element_type=jnp.float32)
    project = lax.psum(partial_proj, "mp")
    inv_norm = lax.rsqrt(jnp.sum(project * project, axis=1, keepdims=True) + epsilon)
    unit_img = project * inv_norm
    unit_img_b = unit_img.astype(jnp.bfloat16)
    image_ids = dp_index * local_rows + jnp.arange(local_rows, dtype=jnp.int32)
    piece = lax.all_gather(texts, "dp", axis=0, tiled=True)
    positions = jnp.arange(piece.shape[0], dtype=jnp.int32)
    shard_of = positions // text_rows
    piece_ids = (shard_of * mp_count + mp_index) * text_rows + positions % text_rows
    grad_unit = add_texts(unit_img_b, image_ids, piece, piece_ids)
    grad_unit = lax.psum(grad_unit, "mp")
    grad_proj = inv_norm * (
        grad_unit - unit_img * jnp.sum(unit_img * grad_unit, axis=1, keepdims=True)
    )
    grad_proj_b = grad_proj.astype(jnp.bfloat16)
    weight_part = jnp.dot(normed_b.T, grad_proj_b, preferred_element_type=jnp.float32)
    grad_weight = lax.psum(weight_part, "dp")
    grad_normed = jnp.dot(grad_proj_b, proj_weight.T, preferred_element_type=jnp.float32)
    grad_total = lax.psum(jnp.sum(grad_normed, axis=1, keepdims=True), "mp")
    grad_in = grad_normed - grad_total / full_width
    return (grad_in.astype(jnp.bfloat16), grad_weight)


def split_terms(value, count):
    terms = []
    for _ in range(count):
        term = value.astype(jnp.bfloat16).astype(jnp.float32)
        terms.append(term)
        value = value - term
    return terms


def kernel_call(body, outs, scratch=(), **names):
    return pl.pallas_call(
        body,
        out_shape=outs,
        scratch_shapes=scratch,
        compiler_params=pltpu.CompilerParams(vmem_limit_bytes=VMEM_BYTES),
        **names,
    )


def texts_body(texts_ref, out_ref):
    out_ref[...] = unit_rows(texts_ref[...].astype(jnp.float32)).astype(jnp.bfloat16)


def project_body(rows, features_ref, weight_ref, out_ref, extra_ref):
    embed = weight_ref.shape[1]
    local_rows, width = features_ref.shape
    values = features_ref[...].astype(jnp.float32)
    row_sum = jnp.sum(values, axis=1, keepdims=True)
    column_sum = jnp.sum(weight_ref[...].astype(jnp.float32), axis=0, keepdims=True)
    extra_ref[...] = jnp.zeros_like(extra_ref)
    at = 0
    for term in split_terms(column_sum, 2):
        for i in range(embed // LANES):
            extra_ref[at : at + 1, :] = term[:, i * LANES : (i + 1) * LANES]
            at += 1
    row = lax.broadcasted_iota(jnp.int32, (local_rows, LANES), 0)
    lane = lax.broadcasted_iota(jnp.int32, (local_rows, LANES), 1)
    sum_row = jnp.sum(jnp.where(row == lane, row_sum, 0.0), axis=0, keepdims=True)
    for term in split_terms(sum_row, 3):
        extra_ref[at : at + 1, :] = term
        at += 1
    centred = (values - row_sum / width).astype(jnp.bfloat16)
    product = jnp.dot(centred, weight_ref[...], preferred_element_type=jnp.float32)
    out_ref[:, :embed] = product.astype(jnp.bfloat16)
    extra = extra_ref[...].astype(jnp.bfloat16)
    for i in range(local_rows // rows):
        out_ref[i * rows : (i + 1) * rows, embed:] = extra


def unit_body(full_width, mp_count, place_ref, parts_ref, *refs):
    (unit_b_ref, unit_ref, inv_norm_ref, mean_ref, weight_sum_ref) = refs
    rows = parts_ref.shape[0] // mp_count
    embed = parts_ref.shape[1] - LANES
    chunks = embed // LANES
    width = full_width // mp_count
    row = lax.broadcasted_iota(jnp.int32, (rows, LANES), 0)
    lane = lax.broadcasted_iota(jnp.int32, (rows, LANES), 1)
    mine = lane == row + (place_ref[0] & (mp_count - 1)) * rows
    project = jnp.zeros((rows, embed), jnp.float32)
    weight_sum = jnp.zeros((1, embed), jnp.float32)
    sums = []
    column_sums = []
    for k in range(mp_count):
        part = parts_ref[k * rows : (k + 1) * rows, :].astype(jnp.float32)
        project = project + part[:, :embed]
        extra = part[:, embed:]
        column_sum = jnp.concatenate(
            [extra[i : i + 1] + extra[chunks + i : chunks + i + 1] for i in range(chunks)], axis=1
        )
        at = 2 * chunks
        sum_row = extra[at : at + 1] + extra[at + 1 : at + 2] + extra[at + 2 : at + 3]
        sums.append(jnp.sum(jnp.where(mine, sum_row, 0.0), axis=1, keepdims=True))
        column_sums.append(column_sum)
        weight_sum = weight_sum + column_sum
    mean = sum(sums) / full_width
    for part_sum, column_sum in zip(sums, column_sums):
        project = project + (part_sum / width - mean) * column_sum
    inv_norm = lax.rsqrt(jnp.sum(project * project, axis=1, keepdims=True) + epsilon)
    unit_img = project * inv_norm
    unit_ref[...] = unit_img
    unit_img_b = unit_img.astype(jnp.bfloat16)
    for k in range(mp_count):
        unit_b_ref[k * rows : (k + 1) * rows, :] = unit_img_b
    inv_norm_ref[...] = inv_norm
    mean_ref[...] = mean
    weight_sum_ref[...] = weight_sum


def slopes_body(mp_count, place_ref, images_ref, *refs):
    (*texts, out_ref) = refs
    rows = images_ref.shape[0] // mp_count
    unit_txt_b = jnp.concatenate([ref[...] for ref in texts], axis=0)
    logits = (
        logit_scale
        * lax.dot_general(
            images_ref[...],
            unit_txt_b,
            (((1,), (1,)), ((), ())),
            preferred_element_type=jnp.float32,
        )
        + logit_bias
    )
    text = lax.broadcasted_iota(jnp.int32, logits.shape, 1)
    image = lax.broadcasted_iota(jnp.int32, logits.shape, 0)
    own = (place_ref[0] & (mp_count - 1)) * rows
    labels = jnp.where((text + own == image) & (text < rows), 1.0, -1.0)
    slopes = (-labels / (1.0 + jnp.exp(labels * logits))).astype(jnp.bfloat16)
    grad_unit = logit_scale * jnp.dot(slopes, unit_txt_b, preferred_element_type=jnp.float32)
    out_ref[...] = grad_unit.astype(out_ref.dtype)


def grad_body(copies, mp_count, unit_ref, inv_norm_ref, mean_ref, parts_ref, out_ref):
    rows, embed = unit_ref.shape
    grad_unit = jnp.zeros((rows, embed), jnp.float32)
    for k in range(mp_count):
        grad_unit = grad_unit + parts_ref[k * rows : (k + 1) * rows, :].astype(jnp.float32)
    unit_img = unit_ref[...]
    grad_proj = inv_norm_ref[...] * (
        grad_unit - unit_img * jnp.sum(unit_img * grad_unit, axis=1, keepdims=True)
    )
    grad_proj_b = grad_proj.astype(jnp.bfloat16)
    lane = lax.broadcasted_iota(jnp.int32, (rows, LANES), 1)
    extra = jnp.zeros((rows, LANES), jnp.float32)
    for i, term in enumerate(split_terms(mean_ref[...], 3)):
        extra = jnp.where(lane == i, term, extra)
    extra = extra.astype(jnp.bfloat16)
    for k in range(copies):
        out_ref[k * rows : (k + 1) * rows, :embed] = grad_proj_b
        out_ref[k * rows : (k + 1) * rows, embed:] = extra


def weight_body(full_width, rows, mp_count, line_count, place_ref, weight_ref, weight_sum_ref,
                features_a_ref, features_b_ref, own_ref, other_ref, *refs):
    (grad_features_ref, grad_weight_ref, all_ref, normed_ref, group_ref) = refs
    embed = weight_ref.shape[1]
    here = place_ref[0]
    plane = 2 * mp_count
    for flip in range(plane * line_count):
        device = here ^ flip
        at = ((device & (plane - 1)) >> 1) * line_count + device // plane
        part_ref = other_ref if flip & 1 else own_ref
        part = part_ref[pl.ds(pl.multiple_of(at * rows, rows), rows), :]
        there = slice(flip * rows, (flip + 1) * rows)
        all_ref[there, :] = part[:, :embed]
        extra = part[:, embed:].astype(jnp.float32)
        mean = extra[:, 0:1] + extra[:, 1:2] + extra[:, 2:3]
        features_ref = features_b_ref if flip & mp_count else features_a_ref
        start = (flip // plane) * mp_count * rows + (device & (mp_count - 1)) * rows
        block = features_ref[pl.ds(pl.multiple_of(start, rows), rows), :].astype(jnp.float32)
        normed_ref[there, :] = (block - mean).astype(jnp.bfloat16)
        if flip < mp_count:
            start = pl.multiple_of((device & (mp_count - 1)) * rows, rows)
            group_ref[pl.ds(start, rows), :] = part[:, :embed]
    grad_weight_ref[...] = lax.dot_general(
        normed_ref[...],
        all_ref[...],
        (((0,), (0,)), ((), ())),
        preferred_element_type=jnp.float32,
    )
    group = group_ref[...]
    grad_normed = lax.dot_general(
        group, weight_ref[...], (((1,), (1,)), ((), ())), preferred_element_type=jnp.float32
    )
    grad_total = jnp.sum(group.astype(jnp.float32) * weight_sum_ref[...], axis=1, keepdims=True)
    grad_features_ref[...] = (grad_normed - grad_total / full_width).astype(jnp.bfloat16)


def shards_gathered(features, proj_weight, texts):
    axes = ("dp", "mp")
    dp_count, mp_count = lax.axis_size("dp"), lax.axis_size("mp")
    count = dp_count * mp_count
    plane_count = 2 * mp_count
    line_count = count // plane_count
    local_rows, width = features.shape
    embed = proj_weight.shape[1]
    rows = texts.shape[0]
    full_width = width * mp_count
    place = (lax.axis_index("dp") * mp_count + lax.axis_index("mp")).astype(jnp.int32).reshape(1)

    def swap(value, flip):
        return lax.ppermute(value, axes, [(i, i ^ flip) for i in range(count)])

    def exchange(value, flips=None):
        if flips is None:
            return lax.all_to_all(value, "mp", 0, 0, tiled=True)
        mask = functools.reduce(lambda x, y: x | y, flips)
        groups = [sorted(i ^ f for f in flips) for i in range(count) if i & mask == 0]
        return lax.all_to_all(value, axes, 0, 0, tiled=True, axis_index_groups=groups)

    def struct(dims, kind=jnp.bfloat16):
        return jax.ShapeDtypeStruct(dims, kind)

    smem = pl.BlockSpec(memory_space=pltpu.SMEM)
    vmem = pl.BlockSpec(memory_space=pltpu.VMEM)
    line = list(range(0, count, plane_count))
    plane = list(range(0, plane_count, 2))

    unit_txt_b = kernel_call(texts_body, struct(texts.shape), name="unit_texts")(texts)
    line_texts = [unit_txt_b] + [swap(unit_txt_b, flip) for flip in line[1:]]
    line_texts = jnp.concatenate(line_texts, axis=0)
    all_texts = [line_texts, swap(line_texts, mp_count)]

    line_features = [features] + [swap(features, flip) for flip in line[1:]]
    line_features = jnp.concatenate(line_features, axis=0)

    partial = kernel_call(
        functools.partial(project_body, rows),
        struct((local_rows, embed + LANES)),
        scratch=[pltpu.VMEM((rows, LANES), jnp.float32)],
        name="project",
    )(features, proj_weight)
    parts = exchange(partial)

    unit_img_b, unit_img, inv_norm, mean, weight_sum = kernel_call(
        functools.partial(unit_body, full_width, mp_count),
        [
            struct((local_rows, embed)),
            struct((rows, embed), jnp.float32),
            struct((rows, 1), jnp.float32),
            struct((rows, 1), jnp.float32),
            struct((1, embed), jnp.float32),
        ],
        in_specs=[smem, vmem],
        name="unit_images",
    )(place, parts)
    images = exchange(unit_img_b)
    images, line_features = lax.optimization_barrier((images, line_features))

    other_features = swap(line_features, mp_count)
    grad_parts = kernel_call(
        functools.partial(slopes_body, mp_count),
        struct((local_rows, embed)),
        in_specs=[smem] + [vmem] * 3,
        name="slopes",
    )(place, images, *all_texts)
    grad_parts = exchange(grad_parts)
    grad_parts, other_features = lax.optimization_barrier((grad_parts, other_features))

    grad_rows = kernel_call(
        functools.partial(grad_body, line_count, mp_count),
        struct((line_count * rows, embed + LANES)),
        name="grad_project",
    )(unit_img, inv_norm, mean, grad_parts)

    grad_rows = exchange(grad_rows, line)
    grad_rows = exchange(jnp.concatenate([grad_rows] * len(plane), axis=0), plane)
    grad_others = swap(grad_rows, 1)

    return tuple(
        kernel_call(
            functools.partial(weight_body, full_width, rows, mp_count, line_count),
            [struct(features.shape), struct(proj_weight.shape, jnp.float32)],
            scratch=[
                pltpu.VMEM((count * rows, embed), jnp.bfloat16),
                pltpu.VMEM((count * rows, width), jnp.bfloat16),
                pltpu.VMEM((local_rows, embed), jnp.bfloat16),
            ],
            in_specs=[smem] + [vmem] * 6,
            name="weight",
        )(place, proj_weight, weight_sum, line_features, other_features, grad_rows, grad_others)
    )


def shards(features, proj_weight, texts):
    dp_count, mp_count = lax.axis_size("dp"), lax.axis_size("mp")
    count = dp_count * mp_count
    rows = texts.shape[0]
    embed = texts.shape[1]
    fits = (
        count * rows * (embed + LANES) * 2 <= GATHER_BYTES
        and count & (count - 1) == 0
        and mp_count & (mp_count - 1) == 0
        and features.shape[0] == LANES == mp_count * rows
        and embed % LANES == 0
        and 2 * (embed // LANES) + 3 <= rows
        and rows % 16 == 0
    )
    plan = shards_gathered if fits else shards_summed
    return plan(features, proj_weight, texts)


def solution(mesh):
    return jax.shard_map(
        shards,
        mesh=mesh,
        in_specs=(P("dp", "mp"), P("mp", None), P(("dp", "mp"), None)),
        out_specs=(P("dp", "mp"), P("mp", None)),
        check_vma=False,
    )
```

```python
import functools

import jax
import jax.numpy as jnp
from jax import lax
from jax.experimental import pallas as pl
from jax.experimental.pallas import tpu as pltpu
from jax.sharding import PartitionSpec as P

logit_scale = 100.0
logit_bias = -10.0
epsilon = 1e-06
LANES = 128
GATHER_BYTES = 8 << 20
VMEM_BYTES = 40 << 20


def unit_rows(values):
    return values * lax.rsqrt(jnp.sum(values * values, axis=1, keepdims=True) + epsilon)


def add_texts(unit_img_b, image_ids, piece, piece_ids):
    unit_txt_b = unit_rows(piece.astype(jnp.float32)).astype(jnp.bfloat16)
    logits = (
        logit_scale * jnp.dot(unit_img_b, unit_txt_b.T, preferred_element_type=jnp.float32)
        + logit_bias
    )
    labels = jnp.where(image_ids[:, None] == piece_ids[None, :], 1.0, -1.0).astype(jnp.float32)
    slopes = (-labels * jax.nn.sigmoid(-labels * logits)).astype(jnp.bfloat16)
    return logit_scale * jnp.dot(slopes, unit_txt_b, preferred_element_type=jnp.float32)


def shards_summed(features, proj_weight, texts):
    local_rows = features.shape[0]
    width_local = features.shape[1]
    mp_count = lax.axis_size("mp")
    full_width = width_local * mp_count
    mp_index = lax.axis_index("mp")
    dp_index = lax.axis_index("dp")
    text_rows = texts.shape[0]
    inputs = features.astype(jnp.float32)
    mean_in = lax.psum(jnp.sum(inputs, axis=1, keepdims=True), "mp") / full_width
    centred = inputs - mean_in
    normed_b = centred.astype(jnp.bfloat16)
    partial_proj = jnp.dot(normed_b, proj_weight, preferred_element_type=jnp.float32)
    project = lax.psum(partial_proj, "mp")
    inv_norm = lax.rsqrt(jnp.sum(project * project, axis=1, keepdims=True) + epsilon)
    unit_img = project * inv_norm
    unit_img_b = unit_img.astype(jnp.bfloat16)
    image_ids = dp_index * local_rows + jnp.arange(local_rows, dtype=jnp.int32)
    piece = lax.all_gather(texts, "dp", axis=0, tiled=True)
    positions = jnp.arange(piece.shape[0], dtype=jnp.int32)
    shard_of = positions // text_rows
    piece_ids = (shard_of * mp_count + mp_index) * text_rows + positions % text_rows
    grad_unit = add_texts(unit_img_b, image_ids, piece, piece_ids)
    grad_unit = lax.psum(grad_unit, "mp")
    grad_proj = inv_norm * (
        grad_unit - unit_img * jnp.sum(unit_img * grad_unit, axis=1, keepdims=True)
    )
    grad_proj_b = grad_proj.astype(jnp.bfloat16)
    weight_part = jnp.dot(normed_b.T, grad_proj_b, preferred_element_type=jnp.float32)
    grad_weight = lax.psum(weight_part, "dp")
    grad_normed = jnp.dot(grad_proj_b, proj_weight.T, preferred_element_type=jnp.float32)
    grad_total = lax.psum(jnp.sum(grad_normed, axis=1, keepdims=True), "mp")
    grad_in = grad_normed - grad_total / full_width
    return (grad_in.astype(jnp.bfloat16), grad_weight)


def split_terms(value, count):
    terms = []
    for _ in range(count):
        term = value.astype(jnp.bfloat16).astype(jnp.float32)
        terms.append(term)
        value = value - term
    return terms


def kernel_call(body, outs, scratch=(), **names):
    return pl.pallas_call(
        body,
        out_shape=outs,
        scratch_shapes=scratch,
        compiler_params=pltpu.CompilerParams(vmem_limit_bytes=VMEM_BYTES),
        **names,
    )


def texts_body(texts_ref, out_ref):
    out_ref[...] = unit_rows(texts_ref[...].astype(jnp.float32)).astype(jnp.bfloat16)


def store_sums(extra_ref, column_sum, sum_row):
    extra_ref[...] = jnp.zeros_like(extra_ref)
    at = 0
    for term in split_terms(column_sum, 2):
        for i in range(column_sum.shape[1] // LANES):
            extra_ref[at : at + 1, :] = term[:, i * LANES : (i + 1) * LANES]
            at += 1
    for term in split_terms(sum_row, 3):
        extra_ref[at : at + 1, :] = term
        at += 1
    return extra_ref[...].astype(jnp.bfloat16)


def load_sums(extra, embed):
    chunks = embed // LANES
    extra = extra.astype(jnp.float32)
    column_sum = jnp.concatenate(
        [extra[i : i + 1] + extra[chunks + i : chunks + i + 1] for i in range(chunks)], axis=1
    )
    at = 2 * chunks
    return column_sum, extra[at : at + 1] + extra[at + 1 : at + 2] + extra[at + 2 : at + 3]


def pick_rows(sum_row, rows, group):
    row = lax.broadcasted_iota(jnp.int32, (rows, LANES), 0)
    lane = lax.broadcasted_iota(jnp.int32, (rows, LANES), 1)
    return jnp.sum(jnp.where(lane == row + group * rows, sum_row, 0.0), axis=1, keepdims=True)


def project_body(
    rows, mp_count, place_ref, features_ref, weight_ref,
    keep_ref, send_ref, column_sum_ref, sum_row_ref, extra_ref,
):
    embed = weight_ref.shape[1]
    local_rows, width = features_ref.shape
    values = features_ref[...].astype(jnp.float32)
    row_sum = jnp.sum(values, axis=1, keepdims=True)
    column_sum = jnp.sum(weight_ref[...].astype(jnp.float32), axis=0, keepdims=True)
    row = lax.broadcasted_iota(jnp.int32, (local_rows, LANES), 0)
    lane = lax.broadcasted_iota(jnp.int32, (local_rows, LANES), 1)
    sum_row = jnp.sum(jnp.where(row == lane, row_sum, 0.0), axis=0, keepdims=True)
    ordered = []
    for flip in list(range(0, mp_count, 2)) + list(range(1, mp_count, 2)):
        start = pl.multiple_of(((place_ref[0] ^ flip) & (mp_count - 1)) * rows, rows)
        block = features_ref[pl.ds(start, rows), :].astype(jnp.float32)
        ordered.append(block - jnp.sum(block, axis=1, keepdims=True) / width)
    centred = jnp.concatenate(ordered, axis=0).astype(jnp.bfloat16)
    product = jnp.dot(centred, weight_ref[...], preferred_element_type=jnp.float32)
    half = local_rows // 2
    keep_ref[...] = product[:half]
    send_ref[:, :embed] = product[half:].astype(jnp.bfloat16)
    extra = store_sums(extra_ref, column_sum, sum_row)
    for i in range(half // rows):
        send_ref[i * rows : (i + 1) * rows, embed:] = extra
    column_sum_ref[...] = column_sum
    sum_row_ref[...] = sum_row


def chip_body(
    width, mp_count, place_ref, keep_ref, received_ref, column_sum_ref, sum_row_ref,
    own_ref, send_ref, chip_column_ref, chip_row_ref, extra_ref,
):
    rows = own_ref.shape[0]
    embed = own_ref.shape[1]
    columns = [column_sum_ref[...], None]
    sum_rows = [sum_row_ref[...], None]
    columns[1], sum_rows[1] = load_sums(received_ref[:rows, embed:], embed)
    chip_column = columns[0] + columns[1]
    chip_row = sum_rows[0] + sum_rows[1]
    for i in range(2):
        group = (place_ref[0] ^ (2 * i)) & (mp_count - 1)
        mean = pick_rows(chip_row, rows, group) / (2 * width)
        here = slice(i * rows, (i + 1) * rows)
        total = keep_ref[here, :] + received_ref[here, :embed].astype(jnp.float32)
        for column, sum_row in zip(columns, sum_rows):
            total = total + (pick_rows(sum_row, rows, group) / width - mean) * column
        if i == 0:
            own_ref[...] = total
        else:
            send_ref[:, :embed] = total.astype(jnp.bfloat16)
    send_ref[:, embed:] = store_sums(extra_ref, chip_column, chip_row)
    chip_column_ref[...] = chip_column
    chip_row_ref[...] = chip_row


def unit_body(
    full_width, mp_count, place_ref, own_ref, received_ref, column_sum_ref, sum_row_ref,
    unit_b_ref, unit_ref, inv_norm_ref, mean_ref, weight_sum_ref,
):
    rows, embed = own_ref.shape
    columns = [column_sum_ref[...], None]
    sum_rows = [sum_row_ref[...], None]
    columns[1], sum_rows[1] = load_sums(received_ref[:, embed:], embed)
    group = place_ref[0] & (mp_count - 1)
    mean = pick_rows(sum_rows[0] + sum_rows[1], rows, group) / full_width
    project = own_ref[...] + received_ref[:, :embed].astype(jnp.float32)
    for column, sum_row in zip(columns, sum_rows):
        part_mean = pick_rows(sum_row, rows, group) / (full_width // 2)
        project = project + (part_mean - mean) * column
    inv_norm = lax.rsqrt(jnp.sum(project * project, axis=1, keepdims=True) + epsilon)
    unit_img = project * inv_norm
    unit_ref[...] = unit_img
    unit_b_ref[...] = unit_img.astype(jnp.bfloat16)
    inv_norm_ref[...] = inv_norm
    mean_ref[...] = mean
    weight_sum_ref[...] = columns[0] + columns[1]


def slopes_body(images_a_ref, images_b_ref, texts_a_ref, texts_b_ref, keep_ref, send_ref):
    half, embed = images_a_ref.shape
    rows = half // 2
    unit_img_b = jnp.concatenate([images_a_ref[...], images_b_ref[...]], axis=0)
    unit_txt_b = jnp.concatenate([texts_a_ref[...], texts_b_ref[...]], axis=0)
    logits = (
        logit_scale
        * lax.dot_general(
            unit_img_b,
            unit_txt_b,
            (((1,), (1,)), ((), ())),
            preferred_element_type=jnp.float32,
        )
        + logit_bias
    )
    text = lax.broadcasted_iota(jnp.int32, logits.shape, 1)
    image = lax.broadcasted_iota(jnp.int32, logits.shape, 0)
    labels = jnp.where((text == image) & (image < rows), 1.0, -1.0)
    slopes = (-labels / (1.0 + jnp.exp(labels * logits))).astype(jnp.bfloat16)
    grad_unit = logit_scale * jnp.dot(slopes, unit_txt_b, preferred_element_type=jnp.float32)
    keep_ref[...] = grad_unit[:half]
    send_ref[...] = grad_unit[half:].astype(jnp.bfloat16)


def chip_grad_body(keep_ref, received_ref, own_ref, send_ref):
    rows = own_ref.shape[0]
    own_ref[...] = keep_ref[:rows, :] + received_ref[:rows, :].astype(jnp.float32)
    total = keep_ref[rows:, :] + received_ref[rows:, :].astype(jnp.float32)
    send_ref[...] = total.astype(jnp.bfloat16)


def grad_body(unit_ref, inv_norm_ref, mean_ref, own_ref, received_ref, out_ref):
    rows, embed = unit_ref.shape
    grad_unit = own_ref[...] + received_ref[...].astype(jnp.float32)
    unit_img = unit_ref[...]
    grad_proj = inv_norm_ref[...] * (
        grad_unit - unit_img * jnp.sum(unit_img * grad_unit, axis=1, keepdims=True)
    )
    out_ref[:, :embed] = grad_proj.astype(jnp.bfloat16)
    lane = lax.broadcasted_iota(jnp.int32, (rows, LANES), 1)
    extra = jnp.zeros((rows, LANES), jnp.float32)
    for i, term in enumerate(split_terms(mean_ref[...], 3)):
        extra = jnp.where(lane == i, term, extra)
    out_ref[:, embed:] = extra.astype(jnp.bfloat16)


def weight_body(rows, mp_count, flip, place_ref, features_ref, own_ref, other_ref, *refs):
    (*previous, out_ref, normed_ref) = refs
    embed = own_ref.shape[1] - LANES
    half = own_ref.shape[0]
    for i, part_ref in enumerate((own_ref, other_ref)):
        group = (place_ref[0] ^ flip ^ i) & (mp_count - 1)
        for k in range(half // rows):
            here = slice(k * rows, (k + 1) * rows)
            extra = part_ref[here, embed:].astype(jnp.float32)
            mean = extra[:, 0:1] + extra[:, 1:2] + extra[:, 2:3]
            start = pl.multiple_of((k * mp_count + group) * rows, rows)
            block = features_ref[pl.ds(start, rows), :].astype(jnp.float32)
            there = slice(i * half + k * rows, i * half + (k + 1) * rows)
            normed_ref[there, :] = (block - mean).astype(jnp.bfloat16)
    both = jnp.concatenate([own_ref[:, :embed], other_ref[:, :embed]], axis=0)
    total = lax.dot_general(
        normed_ref[...], both, (((0,), (0,)), ((), ())), preferred_element_type=jnp.float32
    )
    for ref in previous:
        total = total + ref[...]
    out_ref[...] = total


def features_body(full_width, rows, mp_count, place_ref, weight_ref, weight_sum_ref, *refs):
    (*parts, out_ref, group_ref) = refs
    embed = weight_ref.shape[1]
    for flip, part in enumerate(parts):
        start = pl.multiple_of(((place_ref[0] ^ flip) & (mp_count - 1)) * rows, rows)
        group_ref[pl.ds(start, rows), :] = part[:rows, :embed]
    group = group_ref[...]
    grad_normed = lax.dot_general(
        group, weight_ref[...], (((1,), (1,)), ((), ())), preferred_element_type=jnp.float32
    )
    grad_total = jnp.sum(group.astype(jnp.float32) * weight_sum_ref[...], axis=1, keepdims=True)
    out_ref[...] = (grad_normed - grad_total / full_width).astype(jnp.bfloat16)


def shards_gathered(features, proj_weight, texts):
    axes = ("dp", "mp")
    dp_count, mp_count = lax.axis_size("dp"), lax.axis_size("mp")
    count = dp_count * mp_count
    plane_count = 2 * mp_count
    local_rows, width = features.shape
    embed = proj_weight.shape[1]
    rows = texts.shape[0]
    half = local_rows // 2
    full_width = width * mp_count
    place = (lax.axis_index("dp") * mp_count + lax.axis_index("mp")).astype(jnp.int32).reshape(1)
    core, across, column = 1, 2, mp_count
    line = list(range(plane_count, count, plane_count))

    def swap(value, flip):
        return lax.ppermute(value, axes, [(i, i ^ flip) for i in range(count)])

    def struct(dims, kind=jnp.bfloat16):
        return jax.ShapeDtypeStruct(dims, kind)

    def along_line(value):
        return jnp.concatenate([value] + [swap(value, flip) for flip in line], axis=0)

    smem = pl.BlockSpec(memory_space=pltpu.SMEM)
    vmem = pl.BlockSpec(memory_space=pltpu.VMEM)
    sums = [struct((1, embed), jnp.float32), struct((1, LANES), jnp.float32)]
    extra = pltpu.VMEM((rows, LANES), jnp.float32)

    unit_txt_b = kernel_call(texts_body, struct(texts.shape), name="unit_texts")(texts)
    texts_a = along_line(unit_txt_b)
    texts_b = swap(texts_a, column)
    features_a = along_line(features)

    keep, send, column_sum, sum_row = kernel_call(
        functools.partial(project_body, rows, mp_count),
        [struct((half, embed), jnp.float32), struct((half, embed + LANES))] + sums,
        scratch=[extra],
        in_specs=[smem, vmem, vmem],
        name="project",
    )(place, features, proj_weight)
    own, send, column_sum, sum_row = kernel_call(
        functools.partial(chip_body, width, mp_count),
        [struct((rows, embed), jnp.float32), struct((rows, embed + LANES))] + sums,
        scratch=[extra],
        in_specs=[smem] + [vmem] * 4,
        name="chip_project",
    )(place, keep, swap(send, core), column_sum, sum_row)
    unit_img_b, unit_img, inv_norm, mean, weight_sum = kernel_call(
        functools.partial(unit_body, full_width, mp_count),
        [
            struct((rows, embed)),
            struct((rows, embed), jnp.float32),
            struct((rows, 1), jnp.float32),
            struct((rows, 1), jnp.float32),
            struct((1, embed), jnp.float32),
        ],
        in_specs=[smem] + [vmem] * 4,
        name="unit_images",
    )(place, own, swap(send, across), column_sum, sum_row)

    images_a = jnp.concatenate([unit_img_b, swap(unit_img_b, across)], axis=0)
    images_b = swap(images_a, core)
    images_b, features_a = lax.optimization_barrier((images_b, features_a))
    features_b = swap(features_a, column)

    keep, send = kernel_call(
        slopes_body,
        [struct((half, embed), jnp.float32), struct((half, embed))],
        name="slopes",
    )(images_a, images_b, texts_a, texts_b)
    own, send = kernel_call(
        chip_grad_body,
        [struct((rows, embed), jnp.float32), struct((rows, embed))],
        name="chip_grad",
    )(keep, swap(send, core))
    grad_rows = kernel_call(
        grad_body, struct((rows, embed + LANES)), name="grad_project"
    )(unit_img, inv_norm, mean, own, swap(send, across))

    grad_line = along_line(grad_rows)
    grad_line, features_b = lax.optimization_barrier((grad_line, features_b))
    plane = [0, column, across, column | across]
    grads = [grad_line] + [swap(grad_line, flip) for flip in plane[1:]]
    others = [swap(value, core) for value in grads]

    grad_weight = []
    for flip, value, other in zip(plane, grads, others):
        grad_weight = [
            kernel_call(
                functools.partial(weight_body, rows, mp_count, flip),
                struct(proj_weight.shape, jnp.float32),
                scratch=[pltpu.VMEM((2 * local_rows, width), jnp.bfloat16)],
                in_specs=[smem] + [vmem] * (3 + len(grad_weight)),
                name="weight",
            )(place, features_b if flip & column else features_a, value, other, *grad_weight)
        ]
    group = [grads[0], others[0], grads[plane.index(across)], others[plane.index(across)]]
    grad_features = kernel_call(
        functools.partial(features_body, full_width, rows, mp_count),
        struct(features.shape),
        scratch=[pltpu.VMEM((local_rows, embed), jnp.bfloat16)],
        in_specs=[smem] + [vmem] * (2 + mp_count),
        name="grad_features",
    )(place, proj_weight, weight_sum, *group)
    return grad_features, grad_weight[0]


def shards(features, proj_weight, texts):
    dp_count, mp_count = lax.axis_size("dp"), lax.axis_size("mp")
    count = dp_count * mp_count
    rows = texts.shape[0]
    embed = texts.shape[1]
    fits = (
        count * rows * (embed + LANES) * 2 <= GATHER_BYTES
        and count & (count - 1) == 0
        and mp_count == 4
        and count >= 4 * mp_count
        and features.shape[0] == LANES == mp_count * rows
        and embed % LANES == 0
        and 2 * (embed // LANES) + 3 <= rows
        and rows % 16 == 0
    )
    plan = shards_gathered if fits else shards_summed
    return plan(features, proj_weight, texts)


def solution(mesh):
    return jax.shard_map(
        shards,
        mesh=mesh,
        in_specs=(P("dp", "mp"), P("mp", None), P(("dp", "mp"), None)),
        out_specs=(P("dp", "mp"), P("mp", None)),
        check_vma=False,
    )
```

```python
import functools

import jax
import jax.numpy as jnp
from jax import lax
from jax.experimental import pallas as pl
from jax.experimental.pallas import tpu as pltpu
from jax.sharding import PartitionSpec as P

logit_scale = 100.0
logit_bias = -10.0
epsilon = 1e-06
LANES = 128
GATHER_BYTES = 8 << 20
VMEM_BYTES = 40 << 20


def unit_rows(values):
    return values * lax.rsqrt(jnp.sum(values * values, axis=1, keepdims=True) + epsilon)


def add_texts(unit_img_b, image_ids, piece, piece_ids):
    unit_txt_b = unit_rows(piece.astype(jnp.float32)).astype(jnp.bfloat16)
    logits = (
        logit_scale * jnp.dot(unit_img_b, unit_txt_b.T, preferred_element_type=jnp.float32)
        + logit_bias
    )
    labels = jnp.where(image_ids[:, None] == piece_ids[None, :], 1.0, -1.0).astype(jnp.float32)
    slopes = (-labels * jax.nn.sigmoid(-labels * logits)).astype(jnp.bfloat16)
    return logit_scale * jnp.dot(slopes, unit_txt_b, preferred_element_type=jnp.float32)


def shards_summed(features, proj_weight, texts):
    local_rows = features.shape[0]
    width_local = features.shape[1]
    mp_count = lax.axis_size("mp")
    full_width = width_local * mp_count
    mp_index = lax.axis_index("mp")
    dp_index = lax.axis_index("dp")
    text_rows = texts.shape[0]
    inputs = features.astype(jnp.float32)
    mean_in = lax.psum(jnp.sum(inputs, axis=1, keepdims=True), "mp") / full_width
    centred = inputs - mean_in
    normed_b = centred.astype(jnp.bfloat16)
    partial_proj = jnp.dot(normed_b, proj_weight, preferred_element_type=jnp.float32)
    project = lax.psum(partial_proj, "mp")
    inv_norm = lax.rsqrt(jnp.sum(project * project, axis=1, keepdims=True) + epsilon)
    unit_img = project * inv_norm
    unit_img_b = unit_img.astype(jnp.bfloat16)
    image_ids = dp_index * local_rows + jnp.arange(local_rows, dtype=jnp.int32)
    piece = lax.all_gather(texts, "dp", axis=0, tiled=True)
    positions = jnp.arange(piece.shape[0], dtype=jnp.int32)
    shard_of = positions // text_rows
    piece_ids = (shard_of * mp_count + mp_index) * text_rows + positions % text_rows
    grad_unit = add_texts(unit_img_b, image_ids, piece, piece_ids)
    grad_unit = lax.psum(grad_unit, "mp")
    grad_proj = inv_norm * (
        grad_unit - unit_img * jnp.sum(unit_img * grad_unit, axis=1, keepdims=True)
    )
    grad_proj_b = grad_proj.astype(jnp.bfloat16)
    weight_part = jnp.dot(normed_b.T, grad_proj_b, preferred_element_type=jnp.float32)
    grad_weight = lax.psum(weight_part, "dp")
    grad_normed = jnp.dot(grad_proj_b, proj_weight.T, preferred_element_type=jnp.float32)
    grad_total = lax.psum(jnp.sum(grad_normed, axis=1, keepdims=True), "mp")
    grad_in = grad_normed - grad_total / full_width
    return (grad_in.astype(jnp.bfloat16), grad_weight)


def split_terms(value, count):
    terms = []
    for _ in range(count):
        term = value.astype(jnp.bfloat16).astype(jnp.float32)
        terms.append(term)
        value = value - term
    return terms


def kernel_call(body, outs, scratch=(), flops=0, **names):
    return pl.pallas_call(
        body,
        out_shape=outs,
        scratch_shapes=scratch,
        compiler_params=pltpu.CompilerParams(vmem_limit_bytes=VMEM_BYTES),
        cost_estimate=pl.CostEstimate(flops=flops, bytes_accessed=1 << 20, transcendentals=0),
        **names,
    )


def split_columns(embed):
    return embed // LANES // 3 * LANES


def texts_body(texts_ref, out_ref):
    out_ref[...] = unit_rows(texts_ref[...].astype(jnp.float32)).astype(jnp.bfloat16)


def store_sums(extra_ref, column_sum, sum_row):
    extra_ref[...] = jnp.zeros_like(extra_ref)
    at = 0
    for term in split_terms(column_sum, 2):
        for i in range(column_sum.shape[1] // LANES):
            extra_ref[at : at + 1, :] = term[:, i * LANES : (i + 1) * LANES]
            at += 1
    for term in split_terms(sum_row, 3):
        extra_ref[at : at + 1, :] = term
        at += 1
    return extra_ref[...].astype(jnp.bfloat16)


def load_sums(extra, embed):
    chunks = embed // LANES
    extra = extra.astype(jnp.float32)
    column_sum = jnp.concatenate(
        [extra[i : i + 1] + extra[chunks + i : chunks + i + 1] for i in range(chunks)], axis=1
    )
    at = 2 * chunks
    return column_sum, extra[at : at + 1] + extra[at + 1 : at + 2] + extra[at + 2 : at + 3]


def pick_rows(sum_row, rows, group):
    row = lax.broadcasted_iota(jnp.int32, (rows, LANES), 0)
    lane = lax.broadcasted_iota(jnp.int32, (rows, LANES), 1)
    return jnp.sum(jnp.where(lane == row + group * rows, sum_row, 0.0), axis=1, keepdims=True)


def project_body(
    rows, mp_count, place_ref, features_ref, weight_ref,
    keep_ref, send_ref, column_sum_ref, sum_row_ref, extra_ref,
):
    embed = weight_ref.shape[1]
    local_rows, width = features_ref.shape
    values = features_ref[...].astype(jnp.float32)
    row_sum = jnp.sum(values, axis=1, keepdims=True)
    column_sum = jnp.sum(weight_ref[...].astype(jnp.float32), axis=0, keepdims=True)
    row = lax.broadcasted_iota(jnp.int32, (local_rows, LANES), 0)
    lane = lax.broadcasted_iota(jnp.int32, (local_rows, LANES), 1)
    sum_row = jnp.sum(jnp.where(row == lane, row_sum, 0.0), axis=0, keepdims=True)
    ordered = []
    for flip in list(range(0, mp_count, 2)) + list(range(1, mp_count, 2)):
        start = pl.multiple_of(((place_ref[0] ^ flip) & (mp_count - 1)) * rows, rows)
        block = features_ref[pl.ds(start, rows), :].astype(jnp.float32)
        ordered.append(block - jnp.sum(block, axis=1, keepdims=True) / width)
    centred = jnp.concatenate(ordered, axis=0).astype(jnp.bfloat16)
    product = jnp.dot(centred, weight_ref[...], preferred_element_type=jnp.float32)
    half = local_rows // 2
    keep_ref[...] = product[:half]
    send_ref[:, :embed] = product[half:].astype(jnp.bfloat16)
    extra = store_sums(extra_ref, column_sum, sum_row)
    for i in range(half // rows):
        send_ref[i * rows : (i + 1) * rows, embed:] = extra
    column_sum_ref[...] = column_sum
    sum_row_ref[...] = sum_row


def chip_body(
    width, mp_count, place_ref, keep_ref, received_ref, column_sum_ref, sum_row_ref,
    own_ref, send_ref, chip_column_ref, chip_row_ref, extra_ref,
):
    rows = own_ref.shape[0]
    embed = own_ref.shape[1]
    columns = [column_sum_ref[...], None]
    sum_rows = [sum_row_ref[...], None]
    columns[1], sum_rows[1] = load_sums(received_ref[:rows, embed:], embed)
    chip_column = columns[0] + columns[1]
    chip_row = sum_rows[0] + sum_rows[1]
    for i in range(2):
        group = (place_ref[0] ^ (2 * i)) & (mp_count - 1)
        mean = pick_rows(chip_row, rows, group) / (2 * width)
        here = slice(i * rows, (i + 1) * rows)
        total = keep_ref[here, :] + received_ref[here, :embed].astype(jnp.float32)
        for column, sum_row in zip(columns, sum_rows):
            total = total + (pick_rows(sum_row, rows, group) / width - mean) * column
        if i == 0:
            own_ref[...] = total
        else:
            send_ref[:, :embed] = total.astype(jnp.bfloat16)
    send_ref[:, embed:] = store_sums(extra_ref, chip_column, chip_row)
    chip_column_ref[...] = chip_column
    chip_row_ref[...] = chip_row


def unit_body(
    full_width, mp_count, place_ref, features_ref, own_ref, received_ref, column_sum_ref,
    sum_row_ref, unit_b_ref, unit_ref, inv_norm_ref, normed_ref, weight_sum_ref,
):
    rows, embed = own_ref.shape
    columns = [column_sum_ref[...], None]
    sum_rows = [sum_row_ref[...], None]
    columns[1], sum_rows[1] = load_sums(received_ref[:, embed:], embed)
    group = place_ref[0] & (mp_count - 1)
    full_row = sum_rows[0] + sum_rows[1]
    mean = pick_rows(full_row, rows, group) / full_width
    project = own_ref[...] + received_ref[:, :embed].astype(jnp.float32)
    for column, sum_row in zip(columns, sum_rows):
        part_mean = pick_rows(sum_row, rows, group) / (full_width // 2)
        project = project + (part_mean - mean) * column
    inv_norm = lax.rsqrt(jnp.sum(project * project, axis=1, keepdims=True) + epsilon)
    unit_img = project * inv_norm
    unit_ref[...] = unit_img
    unit_b_ref[...] = unit_img.astype(jnp.bfloat16)
    inv_norm_ref[...] = inv_norm
    mean = pick_rows(full_row, features_ref.shape[0], 0) / full_width
    normed_ref[...] = (features_ref[...].astype(jnp.float32) - mean).astype(jnp.bfloat16)
    weight_sum_ref[...] = columns[0] + columns[1]


def slopes_body(images_a_ref, images_b_ref, texts_a_ref, texts_b_ref, keep_ref, send_ref):
    half, embed = images_a_ref.shape
    rows = half // 2
    unit_img_b = jnp.concatenate([images_a_ref[...], images_b_ref[...]], axis=0)
    unit_txt_b = jnp.concatenate([texts_a_ref[...], texts_b_ref[...]], axis=0)
    logits = (
        logit_scale
        * lax.dot_general(
            unit_img_b,
            unit_txt_b,
            (((1,), (1,)), ((), ())),
            preferred_element_type=jnp.float32,
        )
        + logit_bias
    )
    text = lax.broadcasted_iota(jnp.int32, logits.shape, 1)
    image = lax.broadcasted_iota(jnp.int32, logits.shape, 0)
    labels = jnp.where((text == image) & (image < rows), 1.0, -1.0)
    slopes = (-labels / (1.0 + jnp.exp(labels * logits))).astype(jnp.bfloat16)
    grad_unit = logit_scale * jnp.dot(slopes, unit_txt_b, preferred_element_type=jnp.float32)
    keep_ref[...] = grad_unit[:half]
    send_ref[...] = grad_unit[half:].astype(jnp.bfloat16)


def chip_grad_body(keep_ref, received_ref, own_ref, send_ref):
    rows = own_ref.shape[0]
    own_ref[...] = keep_ref[:rows, :] + received_ref[:rows, :].astype(jnp.float32)
    total = keep_ref[rows:, :] + received_ref[rows:, :].astype(jnp.float32)
    send_ref[...] = total.astype(jnp.bfloat16)


def grad_body(unit_ref, inv_norm_ref, own_ref, received_ref, first_ref, second_ref):
    cut = first_ref.shape[1]
    grad_unit = own_ref[...] + received_ref[...].astype(jnp.float32)
    unit_img = unit_ref[...]
    grad_proj = inv_norm_ref[...] * (
        grad_unit - unit_img * jnp.sum(unit_img * grad_unit, axis=1, keepdims=True)
    )
    grad_proj_b = grad_proj.astype(jnp.bfloat16)
    first_ref[...] = grad_proj_b[:, :cut]
    second_ref[...] = grad_proj_b[:, cut:]


def weight_body(rows, mp_count, normed_order, orders, place_ref, normed_a_ref, normed_b_ref, *refs):
    refs = list(refs)
    products = []
    for order in orders:
        arrays = [refs.pop(0) for _ in order]
        if not order:
            products.append(None)
            continue
        blocks = []
        for flip in sum(order, []):
            normed_ref = normed_b_ref if flip & mp_count else normed_a_ref
            group = (place_ref[0] ^ flip) & (mp_count - 1)
            line_flip = flip - flip % (2 * mp_count)
            start = (normed_order.index(line_flip) * mp_count + group) * rows
            blocks.append(normed_ref[pl.ds(pl.multiple_of(start, rows), rows), :])
        products.append(
            lax.dot_general(
                jnp.concatenate(blocks, axis=0),
                jnp.concatenate([array[...] for array in arrays], axis=0),
                (((0,), (0,)), ((), ())),
                preferred_element_type=jnp.float32,
            )
        )
    outs = refs[len(refs) // 2 :] if len(refs) == 4 else refs[-1:] if len(refs) == 3 else refs
    previous = refs[: -len(outs)]
    at = 0
    for i, product in enumerate(products):
        if previous:
            product = previous[i][...] if product is None else product + previous[i][...]
        if len(outs) > 1:
            outs[i][...] = product
        else:
            outs[0][:, at : at + product.shape[1]] = product
            at += product.shape[1]


def features_body(full_width, rows, mp_count, places, place_ref, weight_ref, weight_sum_ref, *refs):
    (*arrays, out_ref, group_ref) = refs
    embed = weight_ref.shape[1]
    cut = split_columns(embed)
    for flip, (first, second) in enumerate(places):
        start = pl.multiple_of(((place_ref[0] ^ flip) & (mp_count - 1)) * rows, rows)
        index, at = first
        group_ref[pl.ds(start, rows), :cut] = arrays[index][at * rows : (at + 1) * rows, :]
        index, at = second
        group_ref[pl.ds(start, rows), cut:] = arrays[index][at * rows : (at + 1) * rows, :]
    group = group_ref[...]
    grad_normed = lax.dot_general(
        group, weight_ref[...], (((1,), (1,)), ((), ())), preferred_element_type=jnp.float32
    )
    grad_total = jnp.sum(group.astype(jnp.float32) * weight_sum_ref[...], axis=1, keepdims=True)
    out_ref[...] = (grad_normed - grad_total / full_width).astype(jnp.bfloat16)


def shards_gathered(features, proj_weight, texts):
    axes = ("dp", "mp")
    dp_count, mp_count = lax.axis_size("dp"), lax.axis_size("mp")
    count = dp_count * mp_count
    plane_count = 2 * mp_count
    local_rows, width = features.shape
    embed = proj_weight.shape[1]
    rows = texts.shape[0]
    half = local_rows // 2
    full_width = width * mp_count
    cut = split_columns(embed)
    place = (lax.axis_index("dp") * mp_count + lax.axis_index("mp")).astype(jnp.int32).reshape(1)
    core, across, column = 1, 2, mp_count
    line = list(range(plane_count, count, plane_count))

    def swap(value, flip):
        return lax.ppermute(value, axes, [(i, i ^ flip) for i in range(count)])

    def struct(dims, kind=jnp.bfloat16):
        return jax.ShapeDtypeStruct(dims, kind)

    def along_line(value):
        return jnp.concatenate([value] + [swap(value, flip) for flip in line], axis=0)

    smem = pl.BlockSpec(memory_space=pltpu.SMEM)
    vmem = pl.BlockSpec(memory_space=pltpu.VMEM)
    sums = [struct((1, embed), jnp.float32), struct((1, LANES), jnp.float32)]
    extra = pltpu.VMEM((rows, LANES), jnp.float32)

    unit_txt_b = kernel_call(texts_body, struct(texts.shape), name="unit_texts")(texts)
    unit_txt_b, features = lax.optimization_barrier((unit_txt_b, features))
    texts_a = along_line(unit_txt_b)
    texts_b = swap(texts_a, column)

    keep, send, column_sum, sum_row = kernel_call(
        functools.partial(project_body, rows, mp_count),
        [struct((half, embed), jnp.float32), struct((half, embed + LANES))] + sums,
        scratch=[extra],
        in_specs=[smem, vmem, vmem],
        flops=2 * local_rows * width * embed,
        name="project",
    )(place, features, proj_weight)
    own, send, column_sum, sum_row = kernel_call(
        functools.partial(chip_body, width, mp_count),
        [struct((rows, embed), jnp.float32), struct((rows, embed + LANES))] + sums,
        scratch=[extra],
        in_specs=[smem] + [vmem] * 4,
        name="chip_project",
    )(place, keep, swap(send, core), column_sum, sum_row)
    unit_img_b, unit_img, inv_norm, normed_b, weight_sum = kernel_call(
        functools.partial(unit_body, full_width, mp_count),
        [
            struct((rows, embed)),
            struct((rows, embed), jnp.float32),
            struct((rows, 1), jnp.float32),
            struct((local_rows, width)),
            struct((1, embed), jnp.float32),
        ],
        in_specs=[smem] + [vmem] * 5,
        name="unit_images",
    )(place, features, own, swap(send, across), column_sum, sum_row)

    images_a = jnp.concatenate([unit_img_b, swap(unit_img_b, across)], axis=0)
    images_a, normed_b = lax.optimization_barrier((images_a, normed_b))
    normed_line, normed_order = normed_b, [0]
    for flip in reversed([f for f in line if f & (f - 1) == 0]):
        normed_line = jnp.concatenate([normed_line, swap(normed_line, flip)], axis=0)
        normed_order = normed_order + [o ^ flip for o in normed_order]

    images_b = swap(images_a, core)

    keep, send = kernel_call(
        slopes_body,
        [struct((half, embed), jnp.float32), struct((half, embed))],
        flops=4 * local_rows * local_rows * 2 * embed,
        name="slopes",
    )(images_a, images_b, texts_a, texts_b)
    send, normed_line = lax.optimization_barrier((send, normed_line))
    normed_other = swap(normed_line, column)
    own, send = kernel_call(
        chip_grad_body,
        [struct((rows, embed), jnp.float32), struct((rows, embed))],
        name="chip_grad",
    )(keep, swap(send, core))
    first, second = kernel_call(
        grad_body, [struct((rows, cut)), struct((rows, embed - cut))], name="grad_project"
    )(unit_img, inv_norm, own, swap(send, across))

    line_order = [0] + line
    plane_order = [0, column, across, column | across]
    first = jnp.concatenate([first, swap(first, column)], axis=0)
    first = jnp.concatenate([first, swap(first, across)], axis=0)
    second = along_line(second)
    first, second, normed_other = lax.optimization_barrier((first, second, normed_other))
    first_lines = [swap(first, flip) for flip in line]
    second_x, second_y = swap(second, column), swap(second, across)
    second_x, second_y, *first_lines[:-1] = lax.optimization_barrier(
        (second_x, second_y, *first_lines[:-1])
    )

    def moved(order, flip):
        return [o ^ flip for o in order]

    def product(first_parts, second_parts, previous, final):
        orders = [[order for _, order in first_parts], [order for _, order in second_parts]]
        arrays = [value for value, _ in first_parts + second_parts]
        outs = [struct((width, cut), jnp.float32), struct((width, embed - cut), jnp.float32)]
        result = kernel_call(
            functools.partial(weight_body, rows, mp_count, normed_order, orders),
            struct((width, embed), jnp.float32) if final else outs,
            in_specs=[smem] + [vmem] * (2 + len(arrays) + len(previous)),
            flops=2 * width * embed * local_rows * 2,
            name="weight",
        )(place, normed_line, normed_other, *arrays, *previous)
        return result

    def both_cores(value, order):
        return [(value, order), (swap(value, core), moved(order, core))]

    first_parts = both_cores(first, plane_order)
    second_parts = both_cores(second, line_order)
    partial = product(first_parts, second_parts, [], False)
    middle = local_rows // 2
    second_d = jnp.concatenate(
        [swap(second_x[:middle], across), swap(second_y[middle:], column)], axis=0
    )
    x_parts = both_cores(second_x, moved(line_order, column))
    y_parts = both_cores(second_y, moved(line_order, across))
    partial = product([], x_parts + y_parts, partial, False)

    arrays = [value for value, _ in first_parts + second_parts + y_parts]
    y_at = plane_order.index(across)
    places = [((0, 0), (2, 0)), ((1, 0), (3, 0)), ((0, y_at), (4, 0)), ((1, y_at), (5, 0))]
    grad_features = kernel_call(
        functools.partial(features_body, full_width, rows, mp_count, places),
        struct(features.shape),
        scratch=[pltpu.VMEM((local_rows, embed), jnp.bfloat16)],
        in_specs=[smem] + [vmem] * (2 + len(arrays)),
        flops=2 * local_rows * width * embed,
        name="grad_features",
    )(place, proj_weight, weight_sum, *arrays)

    second_d, grad_features, *partial = lax.optimization_barrier(
        (second_d, grad_features, *partial)
    )
    last_first = sum(
        [both_cores(v, moved(plane_order, f)) for v, f in zip(first_lines, line)], []
    )
    last_second = both_cores(second_d, moved(line_order, column | across))
    grad_weight = product(last_first, last_second, partial, True)
    return grad_features, grad_weight


def shards(features, proj_weight, texts):
    dp_count, mp_count = lax.axis_size("dp"), lax.axis_size("mp")
    count = dp_count * mp_count
    rows = texts.shape[0]
    embed = texts.shape[1]
    fits = (
        count * rows * (embed + LANES) * 2 <= GATHER_BYTES
        and count & (count - 1) == 0
        and mp_count == 4
        and count >= 4 * mp_count
        and features.shape[0] == LANES == mp_count * rows
        and embed % LANES == 0
        and 2 * (embed // LANES) + 3 <= rows
        and rows % 16 == 0
    )
    plan = shards_gathered if fits else shards_summed
    return plan(features, proj_weight, texts)


def solution(mesh):
    return jax.shard_map(
        shards,
        mesh=mesh,
        in_specs=(P("dp", "mp"), P("mp", None), P(("dp", "mp"), None)),
        out_specs=(P("dp", "mp"), P("mp", None)),
        check_vma=False,
    )
```

```python
import functools

import jax
import jax.numpy as jnp
from jax import lax
from jax.experimental import pallas as pl
from jax.experimental.pallas import tpu as pltpu
from jax.sharding import PartitionSpec as P

logit_scale = 100.0
logit_bias = -10.0
epsilon = 1e-06
LANES = 128
GATHER_BYTES = 8 << 20
VMEM_BYTES = 40 << 20
VMEM_ALL_BYTES = 62 << 20


def unit_rows(values):
    return values * lax.rsqrt(jnp.sum(values * values, axis=1, keepdims=True) + epsilon)


def add_texts(unit_img_b, image_ids, piece, piece_ids):
    unit_txt_b = unit_rows(piece.astype(jnp.float32)).astype(jnp.bfloat16)
    logits = (
        logit_scale * jnp.dot(unit_img_b, unit_txt_b.T, preferred_element_type=jnp.float32)
        + logit_bias
    )
    labels = jnp.where(image_ids[:, None] == piece_ids[None, :], 1.0, -1.0).astype(jnp.float32)
    slopes = (-labels * jax.nn.sigmoid(-labels * logits)).astype(jnp.bfloat16)
    return logit_scale * jnp.dot(slopes, unit_txt_b, preferred_element_type=jnp.float32)


def shards_summed(features, proj_weight, texts):
    local_rows = features.shape[0]
    width_local = features.shape[1]
    mp_count = lax.axis_size("mp")
    full_width = width_local * mp_count
    mp_index = lax.axis_index("mp")
    dp_index = lax.axis_index("dp")
    text_rows = texts.shape[0]
    inputs = features.astype(jnp.float32)
    mean_in = lax.psum(jnp.sum(inputs, axis=1, keepdims=True), "mp") / full_width
    centred = inputs - mean_in
    normed_b = centred.astype(jnp.bfloat16)
    partial_proj = jnp.dot(normed_b, proj_weight, preferred_element_type=jnp.float32)
    project = lax.psum(partial_proj, "mp")
    inv_norm = lax.rsqrt(jnp.sum(project * project, axis=1, keepdims=True) + epsilon)
    unit_img = project * inv_norm
    unit_img_b = unit_img.astype(jnp.bfloat16)
    image_ids = dp_index * local_rows + jnp.arange(local_rows, dtype=jnp.int32)
    piece = lax.all_gather(texts, "dp", axis=0, tiled=True)
    positions = jnp.arange(piece.shape[0], dtype=jnp.int32)
    shard_of = positions // text_rows
    piece_ids = (shard_of * mp_count + mp_index) * text_rows + positions % text_rows
    grad_unit = add_texts(unit_img_b, image_ids, piece, piece_ids)
    grad_unit = lax.psum(grad_unit, "mp")
    grad_proj = inv_norm * (
        grad_unit - unit_img * jnp.sum(unit_img * grad_unit, axis=1, keepdims=True)
    )
    grad_proj_b = grad_proj.astype(jnp.bfloat16)
    weight_part = jnp.dot(normed_b.T, grad_proj_b, preferred_element_type=jnp.float32)
    grad_weight = lax.psum(weight_part, "dp")
    grad_normed = jnp.dot(grad_proj_b, proj_weight.T, preferred_element_type=jnp.float32)
    grad_total = lax.psum(jnp.sum(grad_normed, axis=1, keepdims=True), "mp")
    grad_in = grad_normed - grad_total / full_width
    return (grad_in.astype(jnp.bfloat16), grad_weight)


def split_terms(value, count):
    terms = []
    for _ in range(count):
        term = value.astype(jnp.bfloat16).astype(jnp.float32)
        terms.append(term)
        value = value - term
    return terms


def kernel_call(body, outs, scratch=(), flops=0, vmem=VMEM_BYTES, **names):
    return pl.pallas_call(
        body,
        out_shape=outs,
        scratch_shapes=scratch,
        compiler_params=pltpu.CompilerParams(vmem_limit_bytes=vmem),
        cost_estimate=pl.CostEstimate(flops=flops, bytes_accessed=1 << 20, transcendentals=0),
        **names,
    )


def store_sums(extra_ref, column_sum, sum_row):
    extra_ref[...] = jnp.zeros_like(extra_ref)
    at = 0
    for term in split_terms(column_sum, 2):
        for i in range(column_sum.shape[1] // LANES):
            extra_ref[at : at + 1, :] = term[:, i * LANES : (i + 1) * LANES]
            at += 1
    for term in split_terms(sum_row, 3):
        extra_ref[at : at + 1, :] = term
        at += 1
    return extra_ref[...].astype(jnp.bfloat16)


def load_sums(extra, embed):
    chunks = embed // LANES
    extra = extra.astype(jnp.float32)
    column_sum = jnp.concatenate(
        [extra[i : i + 1] + extra[chunks + i : chunks + i + 1] for i in range(chunks)], axis=1
    )
    at = 2 * chunks
    return column_sum, extra[at : at + 1] + extra[at + 1 : at + 2] + extra[at + 2 : at + 3]


def pick_rows(sum_row, rows, group):
    row = lax.broadcasted_iota(jnp.int32, (rows, LANES), 0)
    lane = lax.broadcasted_iota(jnp.int32, (rows, LANES), 1)
    return jnp.sum(jnp.where(lane == row + group * rows, sum_row, 0.0), axis=1, keepdims=True)


def project_body(
    rows, mp_count, place_ref, features_hbm, weight_hbm, texts_hbm,
    keep_ref, send_ref, column_sum_ref, sum_row_ref, unit_txt_ref,
    extra_ref, features_ref, weight_ref, texts_ref, arrived,
):
    copies = [
        pltpu.make_async_copy(texts_hbm, texts_ref, arrived.at[0]),
        pltpu.make_async_copy(features_hbm, features_ref, arrived.at[1]),
        pltpu.make_async_copy(weight_hbm, weight_ref, arrived.at[2]),
    ]
    for copy in copies:
        copy.start()
    copies[0].wait()
    unit_txt_ref[...] = unit_rows(texts_ref[...].astype(jnp.float32)).astype(jnp.bfloat16)
    copies[1].wait()
    embed = weight_ref.shape[1]
    local_rows, width = features_ref.shape
    values = features_ref[...].astype(jnp.float32)
    row_sum = jnp.sum(values, axis=1, keepdims=True)
    row = lax.broadcasted_iota(jnp.int32, (local_rows, LANES), 0)
    lane = lax.broadcasted_iota(jnp.int32, (local_rows, LANES), 1)
    sum_row = jnp.sum(jnp.where(row == lane, row_sum, 0.0), axis=0, keepdims=True)
    ordered = []
    for flip in list(range(0, mp_count, 2)) + list(range(1, mp_count, 2)):
        start = pl.multiple_of(((place_ref[0] ^ flip) & (mp_count - 1)) * rows, rows)
        block = features_ref[pl.ds(start, rows), :].astype(jnp.float32)
        ordered.append(block - jnp.sum(block, axis=1, keepdims=True) / width)
    centred = jnp.concatenate(ordered, axis=0).astype(jnp.bfloat16)
    copies[2].wait()
    column_sum = jnp.sum(weight_ref[...].astype(jnp.float32), axis=0, keepdims=True)
    product = jnp.dot(centred, weight_ref[...], preferred_element_type=jnp.float32)
    half = local_rows // 2
    keep_ref[...] = product[:half]
    send_ref[:, :embed] = product[half:].astype(jnp.bfloat16)
    extra = store_sums(extra_ref, column_sum, sum_row)
    for i in range(half // rows):
        send_ref[i * rows : (i + 1) * rows, embed:] = extra
    column_sum_ref[...] = column_sum
    sum_row_ref[...] = sum_row


def chip_body(
    width, mp_count, place_ref, keep_ref, received_ref, column_sum_ref, sum_row_ref,
    own_ref, send_ref, chip_column_ref, chip_row_ref, extra_ref,
):
    rows = own_ref.shape[0]
    embed = own_ref.shape[1]
    columns = [column_sum_ref[...], None]
    sum_rows = [sum_row_ref[...], None]
    columns[1], sum_rows[1] = load_sums(received_ref[:rows, embed:], embed)
    chip_column = columns[0] + columns[1]
    chip_row = sum_rows[0] + sum_rows[1]
    for i in range(2):
        group = (place_ref[0] ^ (2 * i)) & (mp_count - 1)
        mean = pick_rows(chip_row, rows, group) / (2 * width)
        here = slice(i * rows, (i + 1) * rows)
        total = keep_ref[here, :] + received_ref[here, :embed].astype(jnp.float32)
        for column, sum_row in zip(columns, sum_rows):
            total = total + (pick_rows(sum_row, rows, group) / width - mean) * column
        if i == 0:
            own_ref[...] = total
        else:
            send_ref[:, :embed] = total.astype(jnp.bfloat16)
    send_ref[:, embed:] = store_sums(extra_ref, chip_column, chip_row)
    chip_column_ref[...] = chip_column
    chip_row_ref[...] = chip_row


def unit_body(
    full_width, mp_count, place_ref, features_ref, own_ref, received_ref, column_sum_ref,
    sum_row_ref, unit_b_ref, unit_ref, inv_norm_ref, normed_ref, weight_sum_ref,
):
    rows, embed = own_ref.shape
    columns = [column_sum_ref[...], None]
    sum_rows = [sum_row_ref[...], None]
    columns[1], sum_rows[1] = load_sums(received_ref[:, embed:], embed)
    group = place_ref[0] & (mp_count - 1)
    full_row = sum_rows[0] + sum_rows[1]
    mean = pick_rows(full_row, rows, group) / full_width
    project = own_ref[...] + received_ref[:, :embed].astype(jnp.float32)
    for column, sum_row in zip(columns, sum_rows):
        part_mean = pick_rows(sum_row, rows, group) / (full_width // 2)
        project = project + (part_mean - mean) * column
    inv_norm = lax.rsqrt(jnp.sum(project * project, axis=1, keepdims=True) + epsilon)
    unit_img = project * inv_norm
    unit_ref[...] = unit_img
    unit_b_ref[...] = unit_img.astype(jnp.bfloat16)
    inv_norm_ref[...] = inv_norm
    mean = pick_rows(full_row, features_ref.shape[0], 0) / full_width
    normed_ref[...] = (features_ref[...].astype(jnp.float32) - mean).astype(jnp.bfloat16)
    weight_sum_ref[...] = columns[0] + columns[1]


def slopes_body(images_a_ref, images_b_ref, texts_a_ref, texts_b_ref, keep_ref, send_ref):
    half, embed = images_a_ref.shape
    rows = half // 2
    unit_img_b = jnp.concatenate([images_a_ref[...], images_b_ref[...]], axis=0)
    unit_txt_b = jnp.concatenate([texts_a_ref[...], texts_b_ref[...]], axis=0)
    logits = (
        logit_scale
        * lax.dot_general(
            unit_img_b,
            unit_txt_b,
            (((1,), (1,)), ((), ())),
            preferred_element_type=jnp.float32,
        )
        + logit_bias
    )
    text = lax.broadcasted_iota(jnp.int32, logits.shape, 1)
    image = lax.broadcasted_iota(jnp.int32, logits.shape, 0)
    labels = jnp.where((text == image) & (image < rows), 1.0, -1.0)
    slopes = (-labels / (1.0 + jnp.exp(labels * logits))).astype(jnp.bfloat16)
    grad_unit = logit_scale * jnp.dot(slopes, unit_txt_b, preferred_element_type=jnp.float32)
    keep_ref[...] = grad_unit[:half]
    send_ref[...] = grad_unit[half:].astype(jnp.bfloat16)


def chip_grad_body(keep_ref, received_ref, own_ref, send_ref):
    rows = own_ref.shape[0]
    own_ref[...] = keep_ref[:rows, :] + received_ref[:rows, :].astype(jnp.float32)
    total = keep_ref[rows:, :] + received_ref[rows:, :].astype(jnp.float32)
    send_ref[...] = total.astype(jnp.bfloat16)


def grad_body(unit_ref, inv_norm_ref, own_ref, received_ref, out_ref):
    grad_unit = own_ref[...] + received_ref[...].astype(jnp.float32)
    unit_img = unit_ref[...]
    grad_proj = inv_norm_ref[...] * (
        grad_unit - unit_img * jnp.sum(unit_img * grad_unit, axis=1, keepdims=True)
    )
    out_ref[...] = grad_proj.astype(jnp.bfloat16)


def weight_body(rows, mp_count, line, normed_order, flip, place_ref, normed_ref, own_ref, other_ref,
                *refs):
    (*previous, out_ref) = refs
    blocks = []
    for i in range(2):
        group = (place_ref[0] ^ flip ^ i) & (mp_count - 1)
        for line_flip in line:
            start = (normed_order.index(line_flip) * mp_count + group) * rows
            blocks.append(normed_ref[pl.ds(pl.multiple_of(start, rows), rows), :])
    total = lax.dot_general(
        jnp.concatenate(blocks, axis=0),
        jnp.concatenate([own_ref[...], other_ref[...]], axis=0),
        (((0,), (0,)), ((), ())),
        preferred_element_type=jnp.float32,
    )
    for ref in previous:
        total = total + ref[...]
    out_ref[...] = total


def features_body(full_width, rows, mp_count, place_ref, weight_ref, weight_sum_ref, *refs):
    (*parts, out_ref, group_ref) = refs
    for flip, part in enumerate(parts):
        start = pl.multiple_of(((place_ref[0] ^ flip) & (mp_count - 1)) * rows, rows)
        group_ref[pl.ds(start, rows), :] = part[:rows, :]
    group = group_ref[...]
    grad_normed = lax.dot_general(
        group, weight_ref[...], (((1,), (1,)), ((), ())), preferred_element_type=jnp.float32
    )
    grad_total = jnp.sum(group.astype(jnp.float32) * weight_sum_ref[...], axis=1, keepdims=True)
    out_ref[...] = (grad_normed - grad_total / full_width).astype(jnp.bfloat16)


def shards_gathered(features, proj_weight, texts):
    axes = ("dp", "mp")
    dp_count, mp_count = lax.axis_size("dp"), lax.axis_size("mp")
    count = dp_count * mp_count
    plane_count = 2 * mp_count
    local_rows, width = features.shape
    embed = proj_weight.shape[1]
    rows = texts.shape[0]
    half = local_rows // 2
    full_width = width * mp_count
    place = (lax.axis_index("dp") * mp_count + lax.axis_index("mp")).astype(jnp.int32).reshape(1)
    core, across, column = 1, 2, mp_count
    line = list(range(count - plane_count, 0, -plane_count))

    def swap(value, flip):
        return lax.ppermute(value, axes, [(i, i ^ flip) for i in range(count)])

    def struct(dims, kind=jnp.bfloat16):
        return jax.ShapeDtypeStruct(dims, kind)

    def along_line(value):
        return jnp.concatenate([value] + [swap(value, flip) for flip in line], axis=0)

    smem = pl.BlockSpec(memory_space=pltpu.SMEM)
    vmem = pl.BlockSpec(memory_space=pltpu.VMEM)
    sums = [struct((1, embed), jnp.float32), struct((1, LANES), jnp.float32)]
    extra = pltpu.VMEM((rows, LANES), jnp.float32)

    hbm = pl.BlockSpec(memory_space=pltpu.HBM)
    keep, send, column_sum, sum_row, unit_txt_b = kernel_call(
        functools.partial(project_body, rows, mp_count),
        [struct((half, embed), jnp.float32), struct((half, embed + LANES))]
        + sums
        + [struct(texts.shape)],
        scratch=[
            extra,
            pltpu.VMEM(features.shape, features.dtype),
            pltpu.VMEM(proj_weight.shape, proj_weight.dtype),
            pltpu.VMEM(texts.shape, texts.dtype),
            pltpu.SemaphoreType.DMA((3,)),
        ],
        in_specs=[smem, hbm, hbm, hbm],
        flops=2 * local_rows * width * embed,
        vmem=VMEM_ALL_BYTES,
        name="project",
    )(place, features, proj_weight, texts)

    texts_a = along_line(unit_txt_b)
    texts_b = swap(texts_a, column)

    own, send, column_sum, sum_row = kernel_call(
        functools.partial(chip_body, width, mp_count),
        [struct((rows, embed), jnp.float32), struct((rows, embed + LANES))] + sums,
        scratch=[extra],
        in_specs=[smem] + [vmem] * 4,
        name="chip_project",
    )(place, keep, swap(send, core), column_sum, sum_row)
    unit_img_b, unit_img, inv_norm, normed_b, weight_sum = kernel_call(
        functools.partial(unit_body, full_width, mp_count),
        [
            struct((rows, embed)),
            struct((rows, embed), jnp.float32),
            struct((rows, 1), jnp.float32),
            struct((local_rows, width)),
            struct((1, embed), jnp.float32),
        ],
        in_specs=[smem] + [vmem] * 5,
        name="unit_images",
    )(place, features, own, swap(send, across), column_sum, sum_row)

    images_a = jnp.concatenate([unit_img_b, swap(unit_img_b, across)], axis=0)
    images_a, texts_a, normed_b = lax.optimization_barrier((images_a, texts_a, normed_b))
    images_b = swap(images_a, core)
    normed_line, normed_order = normed_b, [0]
    far, near = line[len(line) // 2], line[-1]
    normed_line = jnp.concatenate([normed_line, swap(normed_line, far)], axis=0)

    keep, send = kernel_call(
        slopes_body,
        [struct((half, embed), jnp.float32), struct((half, embed))],
        flops=4 * local_rows * local_rows * 2 * embed,
        name="slopes",
    )(images_a, images_b, texts_a, texts_b)
    send, normed_line = lax.optimization_barrier((send, normed_line))
    normed_line = jnp.concatenate([normed_line, swap(normed_line, near)], axis=0)
    normed_order = [0, far, near, far ^ near]
    own, send = kernel_call(
        chip_grad_body,
        [struct((rows, embed), jnp.float32), struct((rows, embed))],
        name="chip_grad",
    )(keep, swap(send, core))
    received = swap(send, across)
    received, normed_line = lax.optimization_barrier((received, normed_line))
    normed_other = swap(normed_line, column)
    grad_rows = kernel_call(grad_body, struct((rows, embed)), name="grad_project")(
        unit_img, inv_norm, own, received
    )

    grad_line = along_line(grad_rows)
    grad_line, normed_other = lax.optimization_barrier((grad_line, normed_other))
    plane = [0, across, column, column | across]
    grads = [grad_line] + [swap(grad_line, flip) for flip in plane[1:]]
    others = [swap(value, core) for value in grads[:2]]
    group = [grads[0], others[0], grads[1], others[1]]
    grad_features = kernel_call(
        functools.partial(features_body, full_width, rows, mp_count),
        struct(features.shape),
        scratch=[pltpu.VMEM((local_rows, embed), jnp.bfloat16)],
        in_specs=[smem] + [vmem] * (2 + mp_count),
        flops=2 * local_rows * width * embed,
        name="grad_features",
    )(place, proj_weight, weight_sum, *group)

    def add_product(index, previous):
        return kernel_call(
            functools.partial(
                weight_body, rows, mp_count, [0] + line, normed_order, plane[index]
            ),
            struct(proj_weight.shape, jnp.float32),
            in_specs=[smem] + [vmem] * (3 + len(previous)),
            flops=4 * width * embed * local_rows,
            name="weight",
        )(
            place,
            normed_other if plane[index] & column else normed_line,
            grads[index],
            others[index],
            *previous,
        )

    grad_weight = add_product(0, [])
    grads[2], grad_weight = lax.optimization_barrier((grads[2], grad_weight))
    others.append(swap(grads[2], core))
    grad_weight = add_product(1, [grad_weight])
    grads[3], grad_weight, grad_features = lax.optimization_barrier(
        (grads[3], grad_weight, grad_features)
    )
    others.append(swap(grads[3], core))
    grad_weight = add_product(2, [grad_weight])
    grad_weight = add_product(3, [grad_weight])
    return grad_features, grad_weight


def shards(features, proj_weight, texts):
    dp_count, mp_count = lax.axis_size("dp"), lax.axis_size("mp")
    count = dp_count * mp_count
    rows = texts.shape[0]
    embed = texts.shape[1]
    fits = (
        count * rows * (embed + LANES) * 2 <= GATHER_BYTES
        and count & (count - 1) == 0
        and mp_count == 4
        and count == 8 * mp_count
        and features.shape[0] == LANES == mp_count * rows
        and embed % LANES == 0
        and 2 * (embed // LANES) + 3 <= rows
        and rows % 16 == 0
    )
    plan = shards_gathered if fits else shards_summed
    return plan(features, proj_weight, texts)


def solution(mesh):
    return jax.shard_map(
        shards,
        mesh=mesh,
        in_specs=(P("dp", "mp"), P("mp", None), P(("dp", "mp"), None)),
        out_specs=(P("dp", "mp"), P("mp", None)),
        check_vma=False,
    )
```

```python
import functools

import jax
import jax.numpy as jnp
from jax import lax
from jax.experimental import pallas as pl
from jax.experimental.pallas import tpu as pltpu
from jax.sharding import PartitionSpec as P

logit_scale = 100.0
logit_bias = -10.0
epsilon = 1e-06
LANES = 128
GATHER_BYTES = 8 << 20
VMEM_BYTES = 40 << 20


def unit_rows(values):
    return values * lax.rsqrt(jnp.sum(values * values, axis=1, keepdims=True) + epsilon)


def add_texts(unit_img_b, image_ids, piece, piece_ids):
    unit_txt_b = unit_rows(piece.astype(jnp.float32)).astype(jnp.bfloat16)
    logits = (
        logit_scale * jnp.dot(unit_img_b, unit_txt_b.T, preferred_element_type=jnp.float32)
        + logit_bias
    )
    labels = jnp.where(image_ids[:, None] == piece_ids[None, :], 1.0, -1.0).astype(jnp.float32)
    slopes = (-labels * jax.nn.sigmoid(-labels * logits)).astype(jnp.bfloat16)
    return logit_scale * jnp.dot(slopes, unit_txt_b, preferred_element_type=jnp.float32)


def shards_summed(features, proj_weight, texts):
    local_rows = features.shape[0]
    width_local = features.shape[1]
    mp_count = lax.axis_size("mp")
    full_width = width_local * mp_count
    mp_index = lax.axis_index("mp")
    dp_index = lax.axis_index("dp")
    text_rows = texts.shape[0]
    inputs = features.astype(jnp.float32)
    mean_in = lax.psum(jnp.sum(inputs, axis=1, keepdims=True), "mp") / full_width
    centred = inputs - mean_in
    normed_b = centred.astype(jnp.bfloat16)
    partial_proj = jnp.dot(normed_b, proj_weight, preferred_element_type=jnp.float32)
    project = lax.psum(partial_proj, "mp")
    inv_norm = lax.rsqrt(jnp.sum(project * project, axis=1, keepdims=True) + epsilon)
    unit_img = project * inv_norm
    unit_img_b = unit_img.astype(jnp.bfloat16)
    image_ids = dp_index * local_rows + jnp.arange(local_rows, dtype=jnp.int32)
    piece = lax.all_gather(texts, "dp", axis=0, tiled=True)
    positions = jnp.arange(piece.shape[0], dtype=jnp.int32)
    shard_of = positions // text_rows
    piece_ids = (shard_of * mp_count + mp_index) * text_rows + positions % text_rows
    grad_unit = add_texts(unit_img_b, image_ids, piece, piece_ids)
    grad_unit = lax.psum(grad_unit, "mp")
    grad_proj = inv_norm * (
        grad_unit - unit_img * jnp.sum(unit_img * grad_unit, axis=1, keepdims=True)
    )
    grad_proj_b = grad_proj.astype(jnp.bfloat16)
    weight_part = jnp.dot(normed_b.T, grad_proj_b, preferred_element_type=jnp.float32)
    grad_weight = lax.psum(weight_part, "dp")
    grad_normed = jnp.dot(grad_proj_b, proj_weight.T, preferred_element_type=jnp.float32)
    grad_total = lax.psum(jnp.sum(grad_normed, axis=1, keepdims=True), "mp")
    grad_in = grad_normed - grad_total / full_width
    return (grad_in.astype(jnp.bfloat16), grad_weight)


def split_terms(value, count):
    terms = []
    for _ in range(count):
        term = value.astype(jnp.bfloat16).astype(jnp.float32)
        terms.append(term)
        value = value - term
    return terms


def kernel_call(body, outs, scratch=(), flops=0, **names):
    return pl.pallas_call(
        body,
        out_shape=outs,
        scratch_shapes=scratch,
        compiler_params=pltpu.CompilerParams(vmem_limit_bytes=VMEM_BYTES),
        cost_estimate=pl.CostEstimate(flops=flops, bytes_accessed=1 << 20, transcendentals=0),
        **names,
    )


def texts_body(texts_ref, out_ref):
    out_ref[...] = unit_rows(texts_ref[...].astype(jnp.float32)).astype(jnp.bfloat16)


def store_sums(extra_ref, column_sum, sum_row):
    extra_ref[...] = jnp.zeros_like(extra_ref)
    at = 0
    for term in split_terms(column_sum, 2):
        for i in range(column_sum.shape[1] // LANES):
            extra_ref[at : at + 1, :] = term[:, i * LANES : (i + 1) * LANES]
            at += 1
    for term in split_terms(sum_row, 3):
        extra_ref[at : at + 1, :] = term
        at += 1
    return extra_ref[...].astype(jnp.bfloat16)


def load_sums(extra, embed):
    chunks = embed // LANES
    extra = extra.astype(jnp.float32)
    column_sum = jnp.concatenate(
        [extra[i : i + 1] + extra[chunks + i : chunks + i + 1] for i in range(chunks)], axis=1
    )
    at = 2 * chunks
    return column_sum, extra[at : at + 1] + extra[at + 1 : at + 2] + extra[at + 2 : at + 3]


def pick_rows(sum_row, rows, group):
    row = lax.broadcasted_iota(jnp.int32, (rows, LANES), 0)
    lane = lax.broadcasted_iota(jnp.int32, (rows, LANES), 1)
    return jnp.sum(jnp.where(lane == row + group * rows, sum_row, 0.0), axis=1, keepdims=True)


def project_body(
    rows, mp_count, place_ref, features_ref, weight_ref,
    keep_ref, send_ref, column_sum_ref, sum_row_ref, extra_ref,
):
    embed = weight_ref.shape[1]
    local_rows, width = features_ref.shape
    values = features_ref[...].astype(jnp.float32)
    row_sum = jnp.sum(values, axis=1, keepdims=True)
    column_sum = jnp.sum(weight_ref[...].astype(jnp.float32), axis=0, keepdims=True)
    row = lax.broadcasted_iota(jnp.int32, (local_rows, LANES), 0)
    lane = lax.broadcasted_iota(jnp.int32, (local_rows, LANES), 1)
    sum_row = jnp.sum(jnp.where(row == lane, row_sum, 0.0), axis=0, keepdims=True)
    ordered = []
    for flip in list(range(0, mp_count, 2)) + list(range(1, mp_count, 2)):
        start = pl.multiple_of(((place_ref[0] ^ flip) & (mp_count - 1)) * rows, rows)
        block = features_ref[pl.ds(start, rows), :].astype(jnp.float32)
        ordered.append(block - jnp.sum(block, axis=1, keepdims=True) / width)
    centred = jnp.concatenate(ordered, axis=0).astype(jnp.bfloat16)
    product = jnp.dot(centred, weight_ref[...], preferred_element_type=jnp.float32)
    half = local_rows // 2
    keep_ref[...] = product[:half]
    send_ref[:, :embed] = product[half:].astype(jnp.bfloat16)
    extra = store_sums(extra_ref, column_sum, sum_row)
    for i in range(half // rows):
        send_ref[i * rows : (i + 1) * rows, embed:] = extra
    column_sum_ref[...] = column_sum
    sum_row_ref[...] = sum_row


def chip_body(
    width, mp_count, place_ref, keep_ref, received_ref, column_sum_ref, sum_row_ref,
    own_ref, send_ref, chip_column_ref, chip_row_ref, extra_ref,
):
    rows = own_ref.shape[0]
    embed = own_ref.shape[1]
    columns = [column_sum_ref[...], None]
    sum_rows = [sum_row_ref[...], None]
    columns[1], sum_rows[1] = load_sums(received_ref[:rows, embed:], embed)
    chip_column = columns[0] + columns[1]
    chip_row = sum_rows[0] + sum_rows[1]
    for i in range(2):
        group = (place_ref[0] ^ (2 * i)) & (mp_count - 1)
        mean = pick_rows(chip_row, rows, group) / (2 * width)
        here = slice(i * rows, (i + 1) * rows)
        total = keep_ref[here, :] + received_ref[here, :embed].astype(jnp.float32)
        for column, sum_row in zip(columns, sum_rows):
            total = total + (pick_rows(sum_row, rows, group) / width - mean) * column
        if i == 0:
            own_ref[...] = total
        else:
            send_ref[:, :embed] = total.astype(jnp.bfloat16)
    send_ref[:, embed:] = store_sums(extra_ref, chip_column, chip_row)
    chip_column_ref[...] = chip_column
    chip_row_ref[...] = chip_row


def unit_body(
    full_width, mp_count, place_ref, features_ref, own_ref, received_ref, column_sum_ref,
    sum_row_ref, unit_b_ref, unit_ref, inv_norm_ref, normed_ref, weight_sum_ref,
):
    rows, embed = own_ref.shape
    columns = [column_sum_ref[...], None]
    sum_rows = [sum_row_ref[...], None]
    columns[1], sum_rows[1] = load_sums(received_ref[:, embed:], embed)
    group = place_ref[0] & (mp_count - 1)
    full_row = sum_rows[0] + sum_rows[1]
    mean = pick_rows(full_row, rows, group) / full_width
    project = own_ref[...] + received_ref[:, :embed].astype(jnp.float32)
    for column, sum_row in zip(columns, sum_rows):
        part_mean = pick_rows(sum_row, rows, group) / (full_width // 2)
        project = project + (part_mean - mean) * column
    inv_norm = lax.rsqrt(jnp.sum(project * project, axis=1, keepdims=True) + epsilon)
    unit_img = project * inv_norm
    unit_ref[...] = unit_img
    unit_b_ref[...] = unit_img.astype(jnp.bfloat16)
    inv_norm_ref[...] = inv_norm
    mean = pick_rows(full_row, features_ref.shape[0], 0) / full_width
    normed_ref[...] = (features_ref[...].astype(jnp.float32) - mean).astype(jnp.bfloat16)
    weight_sum_ref[...] = columns[0] + columns[1]


def slopes_body(images_a_ref, images_b_ref, texts_a_ref, texts_b_ref, keep_ref, send_ref):
    half, embed = images_a_ref.shape
    rows = half // 2
    unit_img_b = jnp.concatenate([images_a_ref[...], images_b_ref[...]], axis=0)
    unit_txt_b = jnp.concatenate([texts_a_ref[...], texts_b_ref[...]], axis=0)
    logits = (
        logit_scale
        * lax.dot_general(
            unit_img_b,
            unit_txt_b,
            (((1,), (1,)), ((), ())),
            preferred_element_type=jnp.float32,
        )
        + logit_bias
    )
    text = lax.broadcasted_iota(jnp.int32, logits.shape, 1)
    image = lax.broadcasted_iota(jnp.int32, logits.shape, 0)
    labels = jnp.where((text == image) & (image < rows), 1.0, -1.0)
    slopes = (-labels / (1.0 + jnp.exp(labels * logits))).astype(jnp.bfloat16)
    grad_unit = logit_scale * jnp.dot(slopes, unit_txt_b, preferred_element_type=jnp.float32)
    keep_ref[...] = grad_unit[:half]
    send_ref[...] = grad_unit[half:].astype(jnp.bfloat16)


def chip_grad_body(keep_ref, received_ref, own_ref, send_ref):
    rows = own_ref.shape[0]
    own_ref[...] = keep_ref[:rows, :] + received_ref[:rows, :].astype(jnp.float32)
    total = keep_ref[rows:, :] + received_ref[rows:, :].astype(jnp.float32)
    send_ref[...] = total.astype(jnp.bfloat16)


def grad_body(unit_ref, inv_norm_ref, own_ref, received_ref, out_ref):
    grad_unit = own_ref[...] + received_ref[...].astype(jnp.float32)
    unit_img = unit_ref[...]
    grad_proj = inv_norm_ref[...] * (
        grad_unit - unit_img * jnp.sum(unit_img * grad_unit, axis=1, keepdims=True)
    )
    out_ref[...] = grad_proj.astype(jnp.bfloat16)


def weight_body(rows, mp_count, line, normed_order, flip, place_ref, normed_ref, own_ref, other_ref,
                *refs):
    (*previous, out_ref) = refs
    blocks = []
    for i in range(2):
        group = (place_ref[0] ^ flip ^ i) & (mp_count - 1)
        for line_flip in line:
            start = (normed_order.index(line_flip) * mp_count + group) * rows
            blocks.append(normed_ref[pl.ds(pl.multiple_of(start, rows), rows), :])
    total = lax.dot_general(
        jnp.concatenate(blocks, axis=0),
        jnp.concatenate([own_ref[...], other_ref[...]], axis=0),
        (((0,), (0,)), ((), ())),
        preferred_element_type=jnp.float32,
    )
    for ref in previous:
        total = total + ref[...]
    out_ref[...] = total


def features_body(full_width, rows, mp_count, place_ref, weight_ref, weight_sum_ref, *refs):
    (*parts, out_ref, group_ref) = refs
    for flip, part in enumerate(parts):
        start = pl.multiple_of(((place_ref[0] ^ flip) & (mp_count - 1)) * rows, rows)
        group_ref[pl.ds(start, rows), :] = part[:rows, :]
    group = group_ref[...]
    grad_normed = lax.dot_general(
        group, weight_ref[...], (((1,), (1,)), ((), ())), preferred_element_type=jnp.float32
    )
    grad_total = jnp.sum(group.astype(jnp.float32) * weight_sum_ref[...], axis=1, keepdims=True)
    out_ref[...] = (grad_normed - grad_total / full_width).astype(jnp.bfloat16)


def shards_gathered(features, proj_weight, texts):
    axes = ("dp", "mp")
    dp_count, mp_count = lax.axis_size("dp"), lax.axis_size("mp")
    count = dp_count * mp_count
    plane_count = 2 * mp_count
    local_rows, width = features.shape
    embed = proj_weight.shape[1]
    rows = texts.shape[0]
    half = local_rows // 2
    full_width = width * mp_count
    place = (lax.axis_index("dp") * mp_count + lax.axis_index("mp")).astype(jnp.int32).reshape(1)
    core, across, column = 1, 2, mp_count
    line = list(range(plane_count, count, plane_count))

    def swap(value, flip):
        return lax.ppermute(value, axes, [(i, i ^ flip) for i in range(count)])

    def struct(dims, kind=jnp.bfloat16):
        return jax.ShapeDtypeStruct(dims, kind)

    def along_line(value):
        return jnp.concatenate([value] + [swap(value, flip) for flip in line], axis=0)

    smem = pl.BlockSpec(memory_space=pltpu.SMEM)
    vmem = pl.BlockSpec(memory_space=pltpu.VMEM)
    sums = [struct((1, embed), jnp.float32), struct((1, LANES), jnp.float32)]
    extra = pltpu.VMEM((rows, LANES), jnp.float32)

    keep, send, column_sum, sum_row = kernel_call(
        functools.partial(project_body, rows, mp_count),
        [struct((half, embed), jnp.float32), struct((half, embed + LANES))] + sums,
        scratch=[extra],
        in_specs=[smem, vmem, vmem],
        flops=2 * local_rows * width * embed,
        name="project",
    )(place, features, proj_weight)
    own, send, column_sum, sum_row = kernel_call(
        functools.partial(chip_body, width, mp_count),
        [struct((rows, embed), jnp.float32), struct((rows, embed + LANES))] + sums,
        scratch=[extra],
        in_specs=[smem] + [vmem] * 4,
        name="chip_project",
    )(place, keep, swap(send, core), column_sum, sum_row)
    unit_txt_b = kernel_call(texts_body, struct(texts.shape), name="unit_texts")(texts)
    texts_a = along_line(unit_txt_b)
    texts_b = swap(texts_a, column)

    unit_img_b, unit_img, inv_norm, normed_b, weight_sum = kernel_call(
        functools.partial(unit_body, full_width, mp_count),
        [
            struct((rows, embed)),
            struct((rows, embed), jnp.float32),
            struct((rows, 1), jnp.float32),
            struct((local_rows, width)),
            struct((1, embed), jnp.float32),
        ],
        in_specs=[smem] + [vmem] * 5,
        name="unit_images",
    )(place, features, own, swap(send, across), column_sum, sum_row)

    images_a = jnp.concatenate([unit_img_b, swap(unit_img_b, across)], axis=0)
    images_a, texts_a, normed_b = lax.optimization_barrier((images_a, texts_a, normed_b))
    images_b = swap(images_a, core)
    normed_line, normed_order = normed_b, [0]
    far, near = line[len(line) // 2], line[0]
    normed_line = jnp.concatenate([normed_line, swap(normed_line, far)], axis=0)

    keep, send = kernel_call(
        slopes_body,
        [struct((half, embed), jnp.float32), struct((half, embed))],
        flops=4 * local_rows * local_rows * 2 * embed,
        name="slopes",
    )(images_a, images_b, texts_a, texts_b)
    send, normed_line = lax.optimization_barrier((send, normed_line))
    normed_line = jnp.concatenate([normed_line, swap(normed_line, near)], axis=0)
    normed_order = [0, far, near, far ^ near]
    own, send = kernel_call(
        chip_grad_body,
        [struct((rows, embed), jnp.float32), struct((rows, embed))],
        name="chip_grad",
    )(keep, swap(send, core))
    received = swap(send, across)
    received, normed_line = lax.optimization_barrier((received, normed_line))
    normed_other = swap(normed_line, column)
    grad_rows = kernel_call(grad_body, struct((rows, embed)), name="grad_project")(
        unit_img, inv_norm, own, received
    )

    grad_line = along_line(grad_rows)
    grad_line, normed_other = lax.optimization_barrier((grad_line, normed_other))
    plane = [0, across, column, column | across]
    grads = [grad_line] + [swap(grad_line, flip) for flip in plane[1:]]
    others = [swap(value, core) for value in grads[:2]]
    group = [grads[0], others[0], grads[1], others[1]]
    grad_features = kernel_call(
        functools.partial(features_body, full_width, rows, mp_count),
        struct(features.shape),
        scratch=[pltpu.VMEM((local_rows, embed), jnp.bfloat16)],
        in_specs=[smem] + [vmem] * (2 + mp_count),
        flops=2 * local_rows * width * embed,
        name="grad_features",
    )(place, proj_weight, weight_sum, *group)

    def add_product(index, previous):
        return kernel_call(
            functools.partial(
                weight_body, rows, mp_count, [0] + line, normed_order, plane[index]
            ),
            struct(proj_weight.shape, jnp.float32),
            in_specs=[smem] + [vmem] * (3 + len(previous)),
            flops=4 * width * embed * local_rows,
            name="weight",
        )(
            place,
            normed_other if plane[index] & column else normed_line,
            grads[index],
            others[index],
            *previous,
        )

    grad_weight = add_product(0, [])
    others.append(swap(grads[2], core))
    grad_weight = add_product(1, [grad_weight])
    others.append(swap(grads[3], core))
    grad_weight = add_product(2, [grad_weight])
    grad_weight = add_product(3, [grad_weight])
    return grad_features, grad_weight


def shards(features, proj_weight, texts):
    dp_count, mp_count = lax.axis_size("dp"), lax.axis_size("mp")
    count = dp_count * mp_count
    rows = texts.shape[0]
    embed = texts.shape[1]
    fits = (
        count * rows * (embed + LANES) * 2 <= GATHER_BYTES
        and count & (count - 1) == 0
        and mp_count == 4
        and count == 8 * mp_count
        and features.shape[0] == LANES == mp_count * rows
        and embed % LANES == 0
        and 2 * (embed // LANES) + 3 <= rows
        and rows % 16 == 0
    )
    plan = shards_gathered if fits else shards_summed
    return plan(features, proj_weight, texts)


def solution(mesh):
    return jax.shard_map(
        shards,
        mesh=mesh,
        in_specs=(P("dp", "mp"), P("mp", None), P(("dp", "mp"), None)),
        out_specs=(P("dp", "mp"), P("mp", None)),
        check_vma=False,
    )
```

```python
import functools

import jax
import jax.numpy as jnp
from jax import lax
from jax.experimental import pallas as pl
from jax.experimental.pallas import tpu as pltpu
from jax.sharding import PartitionSpec as P

logit_scale = 100.0
logit_bias = -10.0
epsilon = 1e-06
LANES = 128
GATHER_BYTES = 8 << 20
VMEM_BYTES = 40 << 20


def unit_rows(values):
    return values * lax.rsqrt(jnp.sum(values * values, axis=1, keepdims=True) + epsilon)


def add_texts(unit_img_b, image_ids, piece, piece_ids):
    unit_txt_b = unit_rows(piece.astype(jnp.float32)).astype(jnp.bfloat16)
    logits = (
        logit_scale * jnp.dot(unit_img_b, unit_txt_b.T, preferred_element_type=jnp.float32)
        + logit_bias
    )
    labels = jnp.where(image_ids[:, None] == piece_ids[None, :], 1.0, -1.0).astype(jnp.float32)
    slopes = (-labels * jax.nn.sigmoid(-labels * logits)).astype(jnp.bfloat16)
    return logit_scale * jnp.dot(slopes, unit_txt_b, preferred_element_type=jnp.float32)


def shards_summed(features, proj_weight, texts):
    local_rows = features.shape[0]
    width_local = features.shape[1]
    mp_count = lax.axis_size("mp")
    full_width = width_local * mp_count
    mp_index = lax.axis_index("mp")
    dp_index = lax.axis_index("dp")
    text_rows = texts.shape[0]
    inputs = features.astype(jnp.float32)
    mean_in = lax.psum(jnp.sum(inputs, axis=1, keepdims=True), "mp") / full_width
    centred = inputs - mean_in
    normed_b = centred.astype(jnp.bfloat16)
    partial_proj = jnp.dot(normed_b, proj_weight, preferred_element_type=jnp.float32)
    project = lax.psum(partial_proj, "mp")
    inv_norm = lax.rsqrt(jnp.sum(project * project, axis=1, keepdims=True) + epsilon)
    unit_img = project * inv_norm
    unit_img_b = unit_img.astype(jnp.bfloat16)
    image_ids = dp_index * local_rows + jnp.arange(local_rows, dtype=jnp.int32)
    piece = lax.all_gather(texts, "dp", axis=0, tiled=True)
    positions = jnp.arange(piece.shape[0], dtype=jnp.int32)
    shard_of = positions // text_rows
    piece_ids = (shard_of * mp_count + mp_index) * text_rows + positions % text_rows
    grad_unit = add_texts(unit_img_b, image_ids, piece, piece_ids)
    grad_unit = lax.psum(grad_unit, "mp")
    grad_proj = inv_norm * (
        grad_unit - unit_img * jnp.sum(unit_img * grad_unit, axis=1, keepdims=True)
    )
    grad_proj_b = grad_proj.astype(jnp.bfloat16)
    weight_part = jnp.dot(normed_b.T, grad_proj_b, preferred_element_type=jnp.float32)
    grad_weight = lax.psum(weight_part, "dp")
    grad_normed = jnp.dot(grad_proj_b, proj_weight.T, preferred_element_type=jnp.float32)
    grad_total = lax.psum(jnp.sum(grad_normed, axis=1, keepdims=True), "mp")
    grad_in = grad_normed - grad_total / full_width
    return (grad_in.astype(jnp.bfloat16), grad_weight)


def split_terms(value, count):
    terms = []
    for _ in range(count):
        term = value.astype(jnp.bfloat16).astype(jnp.float32)
        terms.append(term)
        value = value - term
    return terms


def kernel_call(body, outs, scratch=(), flops=0, **names):
    return pl.pallas_call(
        body,
        out_shape=outs,
        scratch_shapes=scratch,
        compiler_params=pltpu.CompilerParams(vmem_limit_bytes=VMEM_BYTES),
        cost_estimate=pl.CostEstimate(flops=flops, bytes_accessed=0, transcendentals=0),
        **names,
    )


def texts_body(texts_ref, out_ref):
    out_ref[...] = unit_rows(texts_ref[...].astype(jnp.float32)).astype(jnp.bfloat16)


def store_sums(extra_ref, column_sum, sum_row):
    extra_ref[...] = jnp.zeros_like(extra_ref)
    at = 0
    for term in split_terms(column_sum, 2):
        for i in range(column_sum.shape[1] // LANES):
            extra_ref[at : at + 1, :] = term[:, i * LANES : (i + 1) * LANES]
            at += 1
    for term in split_terms(sum_row, 3):
        extra_ref[at : at + 1, :] = term
        at += 1
    return extra_ref[...].astype(jnp.bfloat16)


def load_sums(extra, embed):
    chunks = embed // LANES
    extra = extra.astype(jnp.float32)
    column_sum = jnp.concatenate(
        [extra[i : i + 1] + extra[chunks + i : chunks + i + 1] for i in range(chunks)], axis=1
    )
    at = 2 * chunks
    return column_sum, extra[at : at + 1] + extra[at + 1 : at + 2] + extra[at + 2 : at + 3]


def pick_rows(sum_row, rows, group):
    row = lax.broadcasted_iota(jnp.int32, (rows, LANES), 0)
    lane = lax.broadcasted_iota(jnp.int32, (rows, LANES), 1)
    return jnp.sum(jnp.where(lane == row + group * rows, sum_row, 0.0), axis=1, keepdims=True)


def project_body(
    rows, mp_count, place_ref, features_ref, weight_ref,
    keep_ref, send_ref, column_sum_ref, sum_row_ref, extra_ref,
):
    embed = weight_ref.shape[1]
    local_rows, width = features_ref.shape
    values = features_ref[...].astype(jnp.float32)
    row_sum = jnp.sum(values, axis=1, keepdims=True)
    column_sum = jnp.sum(weight_ref[...].astype(jnp.float32), axis=0, keepdims=True)
    row = lax.broadcasted_iota(jnp.int32, (local_rows, LANES), 0)
    lane = lax.broadcasted_iota(jnp.int32, (local_rows, LANES), 1)
    sum_row = jnp.sum(jnp.where(row == lane, row_sum, 0.0), axis=0, keepdims=True)
    ordered = []
    for flip in list(range(0, mp_count, 2)) + list(range(1, mp_count, 2)):
        start = pl.multiple_of(((place_ref[0] ^ flip) & (mp_count - 1)) * rows, rows)
        block = features_ref[pl.ds(start, rows), :].astype(jnp.float32)
        ordered.append(block - jnp.sum(block, axis=1, keepdims=True) / width)
    centred = jnp.concatenate(ordered, axis=0).astype(jnp.bfloat16)
    product = jnp.dot(centred, weight_ref[...], preferred_element_type=jnp.float32)
    half = local_rows // 2
    keep_ref[...] = product[:half]
    send_ref[:, :embed] = product[half:].astype(jnp.bfloat16)
    extra = store_sums(extra_ref, column_sum, sum_row)
    for i in range(half // rows):
        send_ref[i * rows : (i + 1) * rows, embed:] = extra
    column_sum_ref[...] = column_sum
    sum_row_ref[...] = sum_row


def chip_body(
    width, mp_count, place_ref, keep_ref, received_ref, column_sum_ref, sum_row_ref,
    own_ref, send_ref, chip_column_ref, chip_row_ref, extra_ref,
):
    rows = own_ref.shape[0]
    embed = own_ref.shape[1]
    columns = [column_sum_ref[...], None]
    sum_rows = [sum_row_ref[...], None]
    columns[1], sum_rows[1] = load_sums(received_ref[:rows, embed:], embed)
    chip_column = columns[0] + columns[1]
    chip_row = sum_rows[0] + sum_rows[1]
    for i in range(2):
        group = (place_ref[0] ^ (2 * i)) & (mp_count - 1)
        mean = pick_rows(chip_row, rows, group) / (2 * width)
        here = slice(i * rows, (i + 1) * rows)
        total = keep_ref[here, :] + received_ref[here, :embed].astype(jnp.float32)
        for column, sum_row in zip(columns, sum_rows):
            total = total + (pick_rows(sum_row, rows, group) / width - mean) * column
        if i == 0:
            own_ref[...] = total
        else:
            send_ref[:, :embed] = total.astype(jnp.bfloat16)
    send_ref[:, embed:] = store_sums(extra_ref, chip_column, chip_row)
    chip_column_ref[...] = chip_column
    chip_row_ref[...] = chip_row


def unit_body(
    full_width, mp_count, place_ref, own_ref, received_ref, column_sum_ref, sum_row_ref,
    unit_b_ref, unit_ref, inv_norm_ref, mean_ref, weight_sum_ref,
):
    rows, embed = own_ref.shape
    columns = [column_sum_ref[...], None]
    sum_rows = [sum_row_ref[...], None]
    columns[1], sum_rows[1] = load_sums(received_ref[:, embed:], embed)
    group = place_ref[0] & (mp_count - 1)
    full_row = sum_rows[0] + sum_rows[1]
    mean = pick_rows(full_row, rows, group) / full_width
    project = own_ref[...] + received_ref[:, :embed].astype(jnp.float32)
    for column, sum_row in zip(columns, sum_rows):
        part_mean = pick_rows(sum_row, rows, group) / (full_width // 2)
        project = project + (part_mean - mean) * column
    inv_norm = lax.rsqrt(jnp.sum(project * project, axis=1, keepdims=True) + epsilon)
    unit_img = project * inv_norm
    unit_ref[...] = unit_img
    unit_b_ref[...] = unit_img.astype(jnp.bfloat16)
    inv_norm_ref[...] = inv_norm
    mean_ref[...] = pick_rows(full_row, mean_ref.shape[0], 0) / full_width
    weight_sum_ref[...] = columns[0] + columns[1]


def centre_body(features_ref, mean_ref, out_ref):
    centred = features_ref[...].astype(jnp.float32) - mean_ref[...]
    out_ref[...] = centred.astype(jnp.bfloat16)


def slopes_body(images_a_ref, images_b_ref, texts_a_ref, texts_b_ref, keep_ref, send_ref):
    half, embed = images_a_ref.shape
    rows = half // 2
    unit_img_b = jnp.concatenate([images_a_ref[...], images_b_ref[...]], axis=0)
    unit_txt_b = jnp.concatenate([texts_a_ref[...], texts_b_ref[...]], axis=0)
    logits = (
        logit_scale
        * lax.dot_general(
            unit_img_b,
            unit_txt_b,
            (((1,), (1,)), ((), ())),
            preferred_element_type=jnp.float32,
        )
        + logit_bias
    )
    text = lax.broadcasted_iota(jnp.int32, logits.shape, 1)
    image = lax.broadcasted_iota(jnp.int32, logits.shape, 0)
    labels = jnp.where((text == image) & (image < rows), 1.0, -1.0)
    slopes = (-labels / (1.0 + jnp.exp(labels * logits))).astype(jnp.bfloat16)
    grad_unit = logit_scale * jnp.dot(slopes, unit_txt_b, preferred_element_type=jnp.float32)
    keep_ref[...] = grad_unit[:half]
    send_ref[...] = grad_unit[half:].astype(jnp.bfloat16)


def chip_grad_body(keep_ref, received_ref, own_ref, send_ref):
    rows = own_ref.shape[0]
    own_ref[...] = keep_ref[:rows, :] + received_ref[:rows, :].astype(jnp.float32)
    total = keep_ref[rows:, :] + received_ref[rows:, :].astype(jnp.float32)
    send_ref[...] = total.astype(jnp.bfloat16)


def grad_body(unit_ref, inv_norm_ref, own_ref, received_ref, out_ref):
    grad_unit = own_ref[...] + received_ref[...].astype(jnp.float32)
    unit_img = unit_ref[...]
    grad_proj = inv_norm_ref[...] * (
        grad_unit - unit_img * jnp.sum(unit_img * grad_unit, axis=1, keepdims=True)
    )
    out_ref[...] = grad_proj.astype(jnp.bfloat16)


def weight_body(rows, mp_count, normed_order, order, flip, place_ref, normed_ref, own_ref, other_ref, *refs):
    (*previous, out_ref) = refs
    blocks = []
    for i in range(2):
        group = (place_ref[0] ^ flip ^ i) & (mp_count - 1)
        for line_flip in order:
            start = (normed_order.index(line_flip) * mp_count + group) * rows
            blocks.append(normed_ref[pl.ds(pl.multiple_of(start, rows), rows), :])
    total = lax.dot_general(
        jnp.concatenate(blocks, axis=0),
        jnp.concatenate([own_ref[...], other_ref[...]], axis=0),
        (((0,), (0,)), ((), ())),
        preferred_element_type=jnp.float32,
    )
    for ref in previous:
        total = total + ref[...]
    out_ref[...] = total


def features_body(full_width, rows, mp_count, place_ref, weight_ref, weight_sum_ref, *refs):
    (*parts, out_ref, group_ref) = refs
    for flip, part in enumerate(parts):
        start = pl.multiple_of(((place_ref[0] ^ flip) & (mp_count - 1)) * rows, rows)
        group_ref[pl.ds(start, rows), :] = part[:rows, :]
    group = group_ref[...]
    grad_normed = lax.dot_general(
        group, weight_ref[...], (((1,), (1,)), ((), ())), preferred_element_type=jnp.float32
    )
    grad_total = jnp.sum(group.astype(jnp.float32) * weight_sum_ref[...], axis=1, keepdims=True)
    out_ref[...] = (grad_normed - grad_total / full_width).astype(jnp.bfloat16)


def shards_gathered(features, proj_weight, texts):
    axes = ("dp", "mp")
    dp_count, mp_count = lax.axis_size("dp"), lax.axis_size("mp")
    count = dp_count * mp_count
    plane_count = 2 * mp_count
    local_rows, width = features.shape
    embed = proj_weight.shape[1]
    rows = texts.shape[0]
    half = local_rows // 2
    full_width = width * mp_count
    place = (lax.axis_index("dp") * mp_count + lax.axis_index("mp")).astype(jnp.int32).reshape(1)
    core, across, column = 1, 2, mp_count
    line = list(range(plane_count, count, plane_count))

    def swap(value, flip):
        return lax.ppermute(value, axes, [(i, i ^ flip) for i in range(count)])

    def struct(dims, kind=jnp.bfloat16):
        return jax.ShapeDtypeStruct(dims, kind)

    def along_line(value, order):
        return jnp.concatenate([value] + [swap(value, flip) for flip in order], axis=0)

    smem = pl.BlockSpec(memory_space=pltpu.SMEM)
    vmem = pl.BlockSpec(memory_space=pltpu.VMEM)
    sums = [struct((1, embed), jnp.float32), struct((1, LANES), jnp.float32)]
    extra = pltpu.VMEM((rows, LANES), jnp.float32)

    keep, send, column_sum, sum_row = kernel_call(
        functools.partial(project_body, rows, mp_count),
        [struct((half, embed), jnp.float32), struct((half, embed + LANES))] + sums,
        scratch=[extra],
        in_specs=[smem, vmem, vmem],
        flops=2 * local_rows * width * embed,
        name="project",
    )(place, features, proj_weight)
    own, send, column_sum, sum_row = kernel_call(
        functools.partial(chip_body, width, mp_count),
        [struct((rows, embed), jnp.float32), struct((rows, embed + LANES))] + sums,
        scratch=[extra],
        in_specs=[smem] + [vmem] * 4,
        name="chip_project",
    )(place, keep, swap(send, core), column_sum, sum_row)
    unit_txt_b = kernel_call(texts_body, struct(texts.shape), name="unit_texts")(texts)
    texts_a = along_line(unit_txt_b, line[::-1])
    texts_b = swap(texts_a, column)

    unit_img_b, unit_img, inv_norm, mean, weight_sum = kernel_call(
        functools.partial(unit_body, full_width, mp_count),
        [
            struct((rows, embed)),
            struct((rows, embed), jnp.float32),
            struct((rows, 1), jnp.float32),
            struct((local_rows, 1), jnp.float32),
            struct((1, embed), jnp.float32),
        ],
        in_specs=[smem] + [vmem] * 4,
        name="unit_images",
    )(place, own, swap(send, across), column_sum, sum_row)
    normed_b = kernel_call(centre_body, struct(features.shape), name="centre")(features, mean)

    images_a = jnp.concatenate([unit_img_b, swap(unit_img_b, across)], axis=0)
    images_a, normed_b = lax.optimization_barrier((images_a, normed_b))
    images_b = swap(images_a, core)
    normed_order = [0] + line[::-1]
    normed_parts = [normed_b] + [swap(normed_b, flip) for flip in normed_order[1:]]

    keep, send = kernel_call(
        slopes_body,
        [struct((half, embed), jnp.float32), struct((half, embed))],
        flops=4 * local_rows * local_rows * 2 * embed,
        name="slopes",
    )(images_a, images_b, texts_a, texts_b)
    at8, at16 = normed_order.index(line[0]), normed_order.index(line[1])
    send, normed_parts[at8], normed_parts[at16] = lax.optimization_barrier(
        (send, normed_parts[at8], normed_parts[at16])
    )
    own, send = kernel_call(
        chip_grad_body,
        [struct((rows, embed), jnp.float32), struct((rows, embed))],
        name="chip_grad",
    )(keep, swap(send, core))
    received = swap(send, across)
    received, *normed_parts = lax.optimization_barrier((received, *normed_parts))
    normed_line = jnp.concatenate(normed_parts, axis=0)
    normed_other = swap(normed_line, column)
    grad_rows = kernel_call(grad_body, struct((rows, embed)), name="grad_project")(
        unit_img, inv_norm, own, received
    )

    grad_order = [0] + line[::-1]
    grad_line = along_line(grad_rows, grad_order[1:])
    grad_line, normed_other = lax.optimization_barrier((grad_line, normed_other))
    plane = [0, across, column, column | across]
    grads = [grad_line] + [swap(grad_line, flip) for flip in plane[1:]]
    y_at = plane.index(across)
    others = [swap(grads[0], core)]
    def add_product(index, previous):
        return kernel_call(
            functools.partial(
                weight_body, rows, mp_count, normed_order, grad_order, plane[index]
            ),
            struct(proj_weight.shape, jnp.float32),
            in_specs=[smem] + [vmem] * (3 + len(previous)),
            flops=4 * width * embed * local_rows,
            name="weight",
        )(
            place,
            normed_other if plane[index] & column else normed_line,
            grads[index],
            others[index],
            *previous,
        )

    grad_weight = first_weight = add_product(0, [])
    others_y = None
    grad_y, _ = lax.optimization_barrier((grads[y_at], first_weight))
    others_y = swap(grad_y, core)
    grad_features = kernel_call(
        functools.partial(features_body, full_width, rows, mp_count),
        struct(features.shape),
        scratch=[pltpu.VMEM((local_rows, embed), jnp.bfloat16)],
        in_specs=[smem] + [vmem] * (2 + mp_count),
        name="grad_features",
    )(place, proj_weight, weight_sum, grads[0], others[0], grads[y_at], others_y)

    for i in range(1, 4):
        if plane[i] == across:
            others.append(others_y)
        else:
            grads[i], _ = lax.optimization_barrier((grads[i], first_weight))
            if i == 3:
                grads[i], grad_features = lax.optimization_barrier((grads[i], grad_features))
            others.append(swap(grads[i], core))
        grad_weight = add_product(i, [grad_weight])
    return grad_features, grad_weight


def shards(features, proj_weight, texts):
    dp_count, mp_count = lax.axis_size("dp"), lax.axis_size("mp")
    count = dp_count * mp_count
    rows = texts.shape[0]
    embed = texts.shape[1]
    fits = (
        count * rows * (embed + LANES) * 2 <= GATHER_BYTES
        and count & (count - 1) == 0
        and mp_count == 4
        and count == 8 * mp_count
        and features.shape[0] == LANES == mp_count * rows
        and embed % LANES == 0
        and 2 * (embed // LANES) + 3 <= rows
        and rows % 16 == 0
    )
    plan = shards_gathered if fits else shards_summed
    return plan(features, proj_weight, texts)


def solution(mesh):
    return jax.shard_map(
        shards,
        mesh=mesh,
        in_specs=(P("dp", "mp"), P("mp", None), P(("dp", "mp"), None)),
        out_specs=(P("dp", "mp"), P("mp", None)),
        check_vma=False,
    )
```

```python
import functools

import jax
import jax.numpy as jnp
from jax import lax
from jax.experimental import pallas as pl
from jax.experimental.pallas import tpu as pltpu
from jax.sharding import PartitionSpec as P

logit_scale = 100.0
logit_bias = -10.0
epsilon = 1e-06
LANES = 128
GATHER_BYTES = 8 << 20
VMEM_BYTES = 40 << 20


def unit_rows(values):
    return values * lax.rsqrt(jnp.sum(values * values, axis=1, keepdims=True) + epsilon)


def add_texts(unit_img_b, image_ids, piece, piece_ids):
    unit_txt_b = unit_rows(piece.astype(jnp.float32)).astype(jnp.bfloat16)
    logits = (
        logit_scale * jnp.dot(unit_img_b, unit_txt_b.T, preferred_element_type=jnp.float32)
        + logit_bias
    )
    labels = jnp.where(image_ids[:, None] == piece_ids[None, :], 1.0, -1.0).astype(jnp.float32)
    slopes = (-labels * jax.nn.sigmoid(-labels * logits)).astype(jnp.bfloat16)
    return logit_scale * jnp.dot(slopes, unit_txt_b, preferred_element_type=jnp.float32)


def shards_summed(features, proj_weight, texts):
    local_rows = features.shape[0]
    width_local = features.shape[1]
    mp_count = lax.axis_size("mp")
    full_width = width_local * mp_count
    mp_index = lax.axis_index("mp")
    dp_index = lax.axis_index("dp")
    text_rows = texts.shape[0]
    inputs = features.astype(jnp.float32)
    mean_in = lax.psum(jnp.sum(inputs, axis=1, keepdims=True), "mp") / full_width
    centred = inputs - mean_in
    normed_b = centred.astype(jnp.bfloat16)
    partial_proj = jnp.dot(normed_b, proj_weight, preferred_element_type=jnp.float32)
    project = lax.psum(partial_proj, "mp")
    inv_norm = lax.rsqrt(jnp.sum(project * project, axis=1, keepdims=True) + epsilon)
    unit_img = project * inv_norm
    unit_img_b = unit_img.astype(jnp.bfloat16)
    image_ids = dp_index * local_rows + jnp.arange(local_rows, dtype=jnp.int32)
    piece = lax.all_gather(texts, "dp", axis=0, tiled=True)
    positions = jnp.arange(piece.shape[0], dtype=jnp.int32)
    shard_of = positions // text_rows
    piece_ids = (shard_of * mp_count + mp_index) * text_rows + positions % text_rows
    grad_unit = add_texts(unit_img_b, image_ids, piece, piece_ids)
    grad_unit = lax.psum(grad_unit, "mp")
    grad_proj = inv_norm * (
        grad_unit - unit_img * jnp.sum(unit_img * grad_unit, axis=1, keepdims=True)
    )
    grad_proj_b = grad_proj.astype(jnp.bfloat16)
    weight_part = jnp.dot(normed_b.T, grad_proj_b, preferred_element_type=jnp.float32)
    grad_weight = lax.psum(weight_part, "dp")
    grad_normed = jnp.dot(grad_proj_b, proj_weight.T, preferred_element_type=jnp.float32)
    grad_total = lax.psum(jnp.sum(grad_normed, axis=1, keepdims=True), "mp")
    grad_in = grad_normed - grad_total / full_width
    return (grad_in.astype(jnp.bfloat16), grad_weight)


def split_terms(value, count):
    terms = []
    for _ in range(count):
        term = value.astype(jnp.bfloat16).astype(jnp.float32)
        terms.append(term)
        value = value - term
    return terms


def kernel_call(body, outs, scratch=(), flops=0, **names):
    return pl.pallas_call(
        body,
        out_shape=outs,
        scratch_shapes=scratch,
        compiler_params=pltpu.CompilerParams(vmem_limit_bytes=VMEM_BYTES),
        cost_estimate=pl.CostEstimate(flops=flops, bytes_accessed=0, transcendentals=0),
        **names,
    )


def texts_body(texts_ref, out_ref):
    out_ref[...] = unit_rows(texts_ref[...].astype(jnp.float32)).astype(jnp.bfloat16)


def store_sums(extra_ref, column_sum, sum_row):
    extra_ref[...] = jnp.zeros_like(extra_ref)
    at = 0
    for term in split_terms(column_sum, 2):
        for i in range(column_sum.shape[1] // LANES):
            extra_ref[at : at + 1, :] = term[:, i * LANES : (i + 1) * LANES]
            at += 1
    for term in split_terms(sum_row, 3):
        extra_ref[at : at + 1, :] = term
        at += 1
    return extra_ref[...].astype(jnp.bfloat16)


def load_sums(extra, embed):
    chunks = embed // LANES
    extra = extra.astype(jnp.float32)
    column_sum = jnp.concatenate(
        [extra[i : i + 1] + extra[chunks + i : chunks + i + 1] for i in range(chunks)], axis=1
    )
    at = 2 * chunks
    return column_sum, extra[at : at + 1] + extra[at + 1 : at + 2] + extra[at + 2 : at + 3]


def pick_rows(sum_row, rows, group):
    row = lax.broadcasted_iota(jnp.int32, (rows, LANES), 0)
    lane = lax.broadcasted_iota(jnp.int32, (rows, LANES), 1)
    return jnp.sum(jnp.where(lane == row + group * rows, sum_row, 0.0), axis=1, keepdims=True)


def project_body(
    rows, mp_count, place_ref, features_ref, weight_ref,
    keep_ref, send_ref, column_sum_ref, sum_row_ref, extra_ref,
):
    embed = weight_ref.shape[1]
    local_rows, width = features_ref.shape
    values = features_ref[...].astype(jnp.float32)
    row_sum = jnp.sum(values, axis=1, keepdims=True)
    column_sum = jnp.sum(weight_ref[...].astype(jnp.float32), axis=0, keepdims=True)
    row = lax.broadcasted_iota(jnp.int32, (local_rows, LANES), 0)
    lane = lax.broadcasted_iota(jnp.int32, (local_rows, LANES), 1)
    sum_row = jnp.sum(jnp.where(row == lane, row_sum, 0.0), axis=0, keepdims=True)
    ordered = []
    for flip in list(range(0, mp_count, 2)) + list(range(1, mp_count, 2)):
        start = pl.multiple_of(((place_ref[0] ^ flip) & (mp_count - 1)) * rows, rows)
        block = features_ref[pl.ds(start, rows), :].astype(jnp.float32)
        ordered.append(block - jnp.sum(block, axis=1, keepdims=True) / width)
    centred = jnp.concatenate(ordered, axis=0).astype(jnp.bfloat16)
    product = jnp.dot(centred, weight_ref[...], preferred_element_type=jnp.float32)
    half = local_rows // 2
    keep_ref[...] = product[:half]
    send_ref[:, :embed] = product[half:].astype(jnp.bfloat16)
    extra = store_sums(extra_ref, column_sum, sum_row)
    for i in range(half // rows):
        send_ref[i * rows : (i + 1) * rows, embed:] = extra
    column_sum_ref[...] = column_sum
    sum_row_ref[...] = sum_row


def chip_body(
    width, mp_count, place_ref, keep_ref, received_ref, column_sum_ref, sum_row_ref,
    own_ref, send_ref, chip_column_ref, chip_row_ref, extra_ref,
):
    rows = own_ref.shape[0]
    embed = own_ref.shape[1]
    columns = [column_sum_ref[...], None]
    sum_rows = [sum_row_ref[...], None]
    columns[1], sum_rows[1] = load_sums(received_ref[:rows, embed:], embed)
    chip_column = columns[0] + columns[1]
    chip_row = sum_rows[0] + sum_rows[1]
    for i in range(2):
        group = (place_ref[0] ^ (2 * i)) & (mp_count - 1)
        mean = pick_rows(chip_row, rows, group) / (2 * width)
        here = slice(i * rows, (i + 1) * rows)
        total = keep_ref[here, :] + received_ref[here, :embed].astype(jnp.float32)
        for column, sum_row in zip(columns, sum_rows):
            total = total + (pick_rows(sum_row, rows, group) / width - mean) * column
        if i == 0:
            own_ref[...] = total
        else:
            send_ref[:, :embed] = total.astype(jnp.bfloat16)
    send_ref[:, embed:] = store_sums(extra_ref, chip_column, chip_row)
    chip_column_ref[...] = chip_column
    chip_row_ref[...] = chip_row


def unit_body(
    full_width, mp_count, place_ref, own_ref, received_ref, column_sum_ref, sum_row_ref,
    unit_b_ref, unit_ref, inv_norm_ref, mean_ref, weight_sum_ref,
):
    rows, embed = own_ref.shape
    columns = [column_sum_ref[...], None]
    sum_rows = [sum_row_ref[...], None]
    columns[1], sum_rows[1] = load_sums(received_ref[:, embed:], embed)
    group = place_ref[0] & (mp_count - 1)
    full_row = sum_rows[0] + sum_rows[1]
    mean = pick_rows(full_row, rows, group) / full_width
    project = own_ref[...] + received_ref[:, :embed].astype(jnp.float32)
    for column, sum_row in zip(columns, sum_rows):
        part_mean = pick_rows(sum_row, rows, group) / (full_width // 2)
        project = project + (part_mean - mean) * column
    inv_norm = lax.rsqrt(jnp.sum(project * project, axis=1, keepdims=True) + epsilon)
    unit_img = project * inv_norm
    unit_ref[...] = unit_img
    unit_b_ref[...] = unit_img.astype(jnp.bfloat16)
    inv_norm_ref[...] = inv_norm
    mean_ref[...] = pick_rows(full_row, mean_ref.shape[0], 0) / full_width
    weight_sum_ref[...] = columns[0] + columns[1]


def centre_body(features_ref, mean_ref, out_ref):
    centred = features_ref[...].astype(jnp.float32) - mean_ref[...]
    out_ref[...] = centred.astype(jnp.bfloat16)


def slopes_body(images_a_ref, images_b_ref, *refs):
    (*texts, keep_ref, send_ref) = refs
    half, embed = images_a_ref.shape
    rows = half // 2
    unit_img_b = jnp.concatenate([images_a_ref[...], images_b_ref[...]], axis=0)
    unit_txt_b = jnp.concatenate([ref[...] for ref in texts], axis=0)
    logits = (
        logit_scale
        * lax.dot_general(
            unit_img_b,
            unit_txt_b,
            (((1,), (1,)), ((), ())),
            preferred_element_type=jnp.float32,
        )
        + logit_bias
    )
    text = lax.broadcasted_iota(jnp.int32, logits.shape, 1)
    image = lax.broadcasted_iota(jnp.int32, logits.shape, 0)
    labels = jnp.where((text == image) & (image < rows), 1.0, -1.0)
    slopes = (-labels / (1.0 + jnp.exp(labels * logits))).astype(jnp.bfloat16)
    grad_unit = logit_scale * jnp.dot(slopes, unit_txt_b, preferred_element_type=jnp.float32)
    keep_ref[...] = grad_unit[:half]
    send_ref[...] = grad_unit[half:].astype(jnp.bfloat16)


def chip_grad_body(keep_ref, received_ref, own_ref, send_ref):
    rows = own_ref.shape[0]
    own_ref[...] = keep_ref[:rows, :] + received_ref[:rows, :].astype(jnp.float32)
    total = keep_ref[rows:, :] + received_ref[rows:, :].astype(jnp.float32)
    send_ref[...] = total.astype(jnp.bfloat16)


def grad_body(unit_ref, inv_norm_ref, own_ref, received_ref, out_ref):
    grad_unit = own_ref[...] + received_ref[...].astype(jnp.float32)
    unit_img = unit_ref[...]
    grad_proj = inv_norm_ref[...] * (
        grad_unit - unit_img * jnp.sum(unit_img * grad_unit, axis=1, keepdims=True)
    )
    out_ref[...] = grad_proj.astype(jnp.bfloat16)


def weight_body(
    rows, mp_count, normed_order, orders, tiles, place_ref, normed_ref, normed_other_ref, *refs
):
    count = 2 * len(orders)
    arrays = refs[:count]
    previous = refs[count : count + 1] if len(refs) - count > (1 if tiles == 1 else 3) else ()
    outs = refs[count + len(previous) :]
    blocks = []
    for order in orders:
        for i in range(2):
            for flip in order:
                ref = normed_other_ref if flip & mp_count else normed_ref
                group = (place_ref[0] ^ flip ^ i) & (mp_count - 1)
                at = normed_order.index(flip - flip % (2 * mp_count)) * mp_count
                start = pl.multiple_of((at + group) * rows, rows)
                blocks.append(ref[pl.ds(start, rows), :])
    normed = jnp.concatenate(blocks, axis=0)
    gradient = jnp.concatenate([array[...] for array in arrays], axis=0)
    if tiles == 1:
        total = lax.dot_general(
            normed, gradient, (((0,), (0,)), ((), ())), preferred_element_type=jnp.float32
        )
        for ref in previous:
            total = total + ref[...]
        outs[0][...] = total
        return
    out_hbm, total_ref, sent = outs
    wide = gradient.shape[1] // tiles
    copies = []
    for k in range(tiles):
        here = slice(k * wide, (k + 1) * wide)
        total = lax.dot_general(
            normed, gradient[:, here], (((0,), (0,)), ((), ())), preferred_element_type=jnp.float32
        )
        for ref in previous:
            total = total + ref[:, here]
        total_ref[:, here] = total
        copies.append(
            pltpu.make_async_copy(total_ref.at[:, here], out_hbm.at[:, here], sent.at[k])
        )
        copies[-1].start()
    for copy in copies:
        copy.wait()


def features_body(
    full_width, rows, mp_count, place_ref, weight_ref, weight_sum_ref, own_ref, other_ref,
    out_ref, group_ref,
):
    for flip in range(mp_count):
        part_ref = other_ref if flip & 1 else own_ref
        start = pl.multiple_of(((place_ref[0] ^ flip) & (mp_count - 1)) * rows, rows)
        at = flip // 2 * rows
        group_ref[pl.ds(start, rows), :] = part_ref[at : at + rows, :]
    group = group_ref[...]
    grad_normed = lax.dot_general(
        group, weight_ref[...], (((1,), (1,)), ((), ())), preferred_element_type=jnp.float32
    )
    grad_total = jnp.sum(group.astype(jnp.float32) * weight_sum_ref[...], axis=1, keepdims=True)
    out_ref[...] = (grad_normed - grad_total / full_width).astype(jnp.bfloat16)


def shards_gathered(features, proj_weight, texts):
    axes = ("dp", "mp")
    dp_count, mp_count = lax.axis_size("dp"), lax.axis_size("mp")
    count = dp_count * mp_count
    plane_count = 2 * mp_count
    local_rows, width = features.shape
    embed = proj_weight.shape[1]
    rows = texts.shape[0]
    half = local_rows // 2
    full_width = width * mp_count
    place = (lax.axis_index("dp") * mp_count + lax.axis_index("mp")).astype(jnp.int32).reshape(1)
    core, across, column = 1, 2, mp_count
    line = list(range(plane_count, count, plane_count))

    def swap(value, flip):
        return lax.ppermute(value, axes, [(i, i ^ flip) for i in range(count)])

    def struct(dims, kind=jnp.bfloat16):
        return jax.ShapeDtypeStruct(dims, kind)

    def along_line(value, order):
        return jnp.concatenate([value] + [swap(value, flip) for flip in order], axis=0)

    smem = pl.BlockSpec(memory_space=pltpu.SMEM)
    vmem = pl.BlockSpec(memory_space=pltpu.VMEM)
    sums = [struct((1, embed), jnp.float32), struct((1, LANES), jnp.float32)]
    extra = pltpu.VMEM((rows, LANES), jnp.float32)

    keep, send, column_sum, sum_row = kernel_call(
        functools.partial(project_body, rows, mp_count),
        [struct((half, embed), jnp.float32), struct((half, embed + LANES))] + sums,
        scratch=[extra],
        in_specs=[smem, vmem, vmem],
        flops=2 * local_rows * width * embed,
        name="project",
    )(place, features, proj_weight)
    own, send, column_sum, sum_row = kernel_call(
        functools.partial(chip_body, width, mp_count),
        [struct((rows, embed), jnp.float32), struct((rows, embed + LANES))] + sums,
        scratch=[extra],
        in_specs=[smem] + [vmem] * 4,
        name="chip_project",
    )(place, keep, swap(send, core), column_sum, sum_row)
    texts, own = lax.optimization_barrier((texts, own))
    unit_txt_b = kernel_call(texts_body, struct(texts.shape), name="unit_texts")(texts)
    texts_a = along_line(unit_txt_b, line)
    texts = [texts_a, swap(texts_a, column)]
    unit_img_b, unit_img, inv_norm, mean, weight_sum = kernel_call(
        functools.partial(unit_body, full_width, mp_count),
        [
            struct((rows, embed)),
            struct((rows, embed), jnp.float32),
            struct((rows, 1), jnp.float32),
            struct((local_rows, 1), jnp.float32),
            struct((1, embed), jnp.float32),
        ],
        in_specs=[smem] + [vmem] * 4,
        name="unit_images",
    )(place, own, swap(send, across), column_sum, sum_row)
    normed_b = kernel_call(centre_body, struct(features.shape), name="centre")(features, mean)

    images_a = jnp.concatenate([unit_img_b, swap(unit_img_b, across)], axis=0)
    texts_a, unit_img_b, normed_b = lax.optimization_barrier((texts_a, unit_img_b, normed_b))
    normed_order = [0] + line
    normed_parts = [normed_b] + [swap(normed_b, flip) for flip in normed_order[1:]]
    at = [normed_order.index(flip) for flip in line]
    normed_near = swap(normed_b, column)
    images_a, normed_parts[at[0]] = lax.optimization_barrier((images_a, normed_parts[at[0]]))
    images_b = swap(images_a, core)
    keep, send = kernel_call(
        slopes_body,
        [struct((half, embed), jnp.float32), struct((half, embed))],
        flops=4 * local_rows * local_rows * 2 * embed,
        name="slopes",
    )(images_a, images_b, *texts)
    send, normed_near = lax.optimization_barrier((send, normed_near))
    send, normed_parts[at[1]], normed_parts[at[2]] = lax.optimization_barrier(
        (send, normed_parts[at[1]], normed_parts[at[2]])
    )
    own, send = kernel_call(
        chip_grad_body,
        [struct((rows, embed), jnp.float32), struct((rows, embed))],
        name="chip_grad",
    )(keep, swap(send, core))
    received = swap(send, across)
    normed_line = jnp.concatenate(normed_parts, axis=0)
    normed_far = swap(jnp.concatenate(normed_parts[1:], axis=0), column)
    normed_other = jnp.concatenate([normed_near, normed_far], axis=0)
    grad_rows = kernel_call(grad_body, struct((rows, embed)), name="grad_project")(
        unit_img, inv_norm, own, received
    )

    near_order = [0, across, column, across | column]
    far_order = line
    far = jnp.concatenate([swap(grad_rows, flip) for flip in far_order], axis=0)
    near = jnp.concatenate(
        [grad_rows] + [swap(grad_rows, flip) for flip in near_order[1:]], axis=0
    )
    far, near, normed_other = lax.optimization_barrier((far, near, normed_other))
    plane = [column, across, across | column]
    grads = [swap(far, flip) for flip in plane]
    near_other, far_other = swap(near, core), swap(far, core)

    def add_product(parts, previous, final=False):
        arrays = sum([[own, other] for own, other, _ in parts], [])
        orders = [order for _, _, order in parts]
        tiles = 3 if final else 1
        scratch = [
            pltpu.VMEM(proj_weight.shape, jnp.float32),
            pltpu.SemaphoreType.DMA((tiles,)),
        ]
        return kernel_call(
            functools.partial(weight_body, rows, mp_count, normed_order, orders, tiles),
            struct(proj_weight.shape, jnp.float32),
            scratch=scratch if final else (),
            in_specs=[smem] + [vmem] * (2 + len(arrays) + len(previous)),
            out_specs=pl.BlockSpec(memory_space=pl.ANY) if final else vmem,
            flops=2 * width * embed * sum(a.shape[0] for a in arrays),
            name="weight",
        )(place, normed_line, normed_other, *arrays, *previous)

    grad_weight = add_product(
        [(near, near_other, near_order), (far, far_other, far_order)], []
    )
    grad_features = kernel_call(
        functools.partial(features_body, full_width, rows, mp_count),
        struct(features.shape),
        scratch=[pltpu.VMEM((local_rows, embed), jnp.bfloat16)],
        in_specs=[smem] + [vmem] * 4,
        flops=2 * local_rows * width * embed,
        name="grad_features",
    )(place, proj_weight, weight_sum, near, near_other)
    parts = []
    for i, (value, flip) in enumerate(zip(grads, plane)):
        value, _, _ = lax.optimization_barrier((value, grad_weight, grad_features))
        parts.append((value, swap(value, core), [o ^ flip for o in far_order]))
    grad_weight = add_product(parts[:2], [grad_weight])
    grad_weight = add_product(parts[2:], [grad_weight], True)
    return grad_features, grad_weight


def shards(features, proj_weight, texts):
    dp_count, mp_count = lax.axis_size("dp"), lax.axis_size("mp")
    count = dp_count * mp_count
    rows = texts.shape[0]
    embed = texts.shape[1]
    fits = (
        count * rows * (embed + LANES) * 2 <= GATHER_BYTES
        and count & (count - 1) == 0
        and mp_count == 4
        and count == 8 * mp_count
        and features.shape[0] == LANES == mp_count * rows
        and embed % LANES == 0
        and 2 * (embed // LANES) + 3 <= rows
        and rows % 16 == 0
    )
    plan = shards_gathered if fits else shards_summed
    return plan(features, proj_weight, texts)


def solution(mesh):
    return jax.shard_map(
        shards,
        mesh=mesh,
        in_specs=(P("dp", "mp"), P("mp", None), P(("dp", "mp"), None)),
        out_specs=(P("dp", "mp"), P("mp", None)),
        check_vma=False,
    )
```

```python
import functools

import jax
import jax.numpy as jnp
from jax import lax
from jax.experimental import pallas as pl
from jax.experimental.pallas import tpu as pltpu
from jax.sharding import PartitionSpec as P

logit_scale = 100.0
logit_bias = -10.0
epsilon = 1e-06
LANES = 128
GATHER_BYTES = 8 << 20
VMEM_BYTES = 40 << 20


def unit_rows(values):
    return values * lax.rsqrt(jnp.sum(values * values, axis=1, keepdims=True) + epsilon)


def add_texts(unit_img_b, image_ids, piece, piece_ids):
    unit_txt_b = unit_rows(piece.astype(jnp.float32)).astype(jnp.bfloat16)
    logits = (
        logit_scale * jnp.dot(unit_img_b, unit_txt_b.T, preferred_element_type=jnp.float32)
        + logit_bias
    )
    labels = jnp.where(image_ids[:, None] == piece_ids[None, :], 1.0, -1.0).astype(jnp.float32)
    slopes = (-labels * jax.nn.sigmoid(-labels * logits)).astype(jnp.bfloat16)
    return logit_scale * jnp.dot(slopes, unit_txt_b, preferred_element_type=jnp.float32)


def shards_summed(features, proj_weight, texts):
    local_rows = features.shape[0]
    width_local = features.shape[1]
    mp_count = lax.axis_size("mp")
    full_width = width_local * mp_count
    mp_index = lax.axis_index("mp")
    dp_index = lax.axis_index("dp")
    text_rows = texts.shape[0]
    inputs = features.astype(jnp.float32)
    mean_in = lax.psum(jnp.sum(inputs, axis=1, keepdims=True), "mp") / full_width
    centred = inputs - mean_in
    normed_b = centred.astype(jnp.bfloat16)
    partial_proj = jnp.dot(normed_b, proj_weight, preferred_element_type=jnp.float32)
    project = lax.psum(partial_proj, "mp")
    inv_norm = lax.rsqrt(jnp.sum(project * project, axis=1, keepdims=True) + epsilon)
    unit_img = project * inv_norm
    unit_img_b = unit_img.astype(jnp.bfloat16)
    image_ids = dp_index * local_rows + jnp.arange(local_rows, dtype=jnp.int32)
    piece = lax.all_gather(texts, "dp", axis=0, tiled=True)
    positions = jnp.arange(piece.shape[0], dtype=jnp.int32)
    shard_of = positions // text_rows
    piece_ids = (shard_of * mp_count + mp_index) * text_rows + positions % text_rows
    grad_unit = add_texts(unit_img_b, image_ids, piece, piece_ids)
    grad_unit = lax.psum(grad_unit, "mp")
    grad_proj = inv_norm * (
        grad_unit - unit_img * jnp.sum(unit_img * grad_unit, axis=1, keepdims=True)
    )
    grad_proj_b = grad_proj.astype(jnp.bfloat16)
    weight_part = jnp.dot(normed_b.T, grad_proj_b, preferred_element_type=jnp.float32)
    grad_weight = lax.psum(weight_part, "dp")
    grad_normed = jnp.dot(grad_proj_b, proj_weight.T, preferred_element_type=jnp.float32)
    grad_total = lax.psum(jnp.sum(grad_normed, axis=1, keepdims=True), "mp")
    grad_in = grad_normed - grad_total / full_width
    return (grad_in.astype(jnp.bfloat16), grad_weight)


def split_terms(value, count):
    terms = []
    for _ in range(count):
        term = value.astype(jnp.bfloat16).astype(jnp.float32)
        terms.append(term)
        value = value - term
    return terms


def kernel_call(body, outs, scratch=(), flops=0, **names):
    return pl.pallas_call(
        body,
        out_shape=outs,
        scratch_shapes=scratch,
        compiler_params=pltpu.CompilerParams(vmem_limit_bytes=VMEM_BYTES),
        cost_estimate=pl.CostEstimate(flops=flops, bytes_accessed=0, transcendentals=0),
        **names,
    )


def texts_body(texts_ref, out_ref):
    out_ref[...] = unit_rows(texts_ref[...].astype(jnp.float32)).astype(jnp.bfloat16)


def store_sums(extra_ref, column_sum, sum_row):
    extra_ref[...] = jnp.zeros_like(extra_ref)
    at = 0
    for term in split_terms(column_sum, 2):
        for i in range(column_sum.shape[1] // LANES):
            extra_ref[at : at + 1, :] = term[:, i * LANES : (i + 1) * LANES]
            at += 1
    for term in split_terms(sum_row, 3):
        extra_ref[at : at + 1, :] = term
        at += 1
    return extra_ref[...].astype(jnp.bfloat16)


def load_sums(extra, embed):
    chunks = embed // LANES
    extra = extra.astype(jnp.float32)
    column_sum = jnp.concatenate(
        [extra[i : i + 1] + extra[chunks + i : chunks + i + 1] for i in range(chunks)], axis=1
    )
    at = 2 * chunks
    return column_sum, extra[at : at + 1] + extra[at + 1 : at + 2] + extra[at + 2 : at + 3]


def pick_rows(sum_row, rows, group):
    row = lax.broadcasted_iota(jnp.int32, (rows, LANES), 0)
    lane = lax.broadcasted_iota(jnp.int32, (rows, LANES), 1)
    return jnp.sum(jnp.where(lane == row + group * rows, sum_row, 0.0), axis=1, keepdims=True)


def project_body(
    rows, mp_count, place_ref, features_ref, weight_ref,
    keep_ref, send_ref, column_sum_ref, sum_row_ref, extra_ref,
):
    embed = weight_ref.shape[1]
    local_rows, width = features_ref.shape
    values = features_ref[...].astype(jnp.float32)
    row_sum = jnp.sum(values, axis=1, keepdims=True)
    column_sum = jnp.sum(weight_ref[...].astype(jnp.float32), axis=0, keepdims=True)
    row = lax.broadcasted_iota(jnp.int32, (local_rows, LANES), 0)
    lane = lax.broadcasted_iota(jnp.int32, (local_rows, LANES), 1)
    sum_row = jnp.sum(jnp.where(row == lane, row_sum, 0.0), axis=0, keepdims=True)
    ordered = []
    for flip in list(range(0, mp_count, 2)) + list(range(1, mp_count, 2)):
        start = pl.multiple_of(((place_ref[0] ^ flip) & (mp_count - 1)) * rows, rows)
        block = features_ref[pl.ds(start, rows), :].astype(jnp.float32)
        ordered.append(block - jnp.sum(block, axis=1, keepdims=True) / width)
    centred = jnp.concatenate(ordered, axis=0).astype(jnp.bfloat16)
    product = jnp.dot(centred, weight_ref[...], preferred_element_type=jnp.float32)
    half = local_rows // 2
    keep_ref[...] = product[:half]
    send_ref[:, :embed] = product[half:].astype(jnp.bfloat16)
    extra = store_sums(extra_ref, column_sum, sum_row)
    for i in range(half // rows):
        send_ref[i * rows : (i + 1) * rows, embed:] = extra
    column_sum_ref[...] = column_sum
    sum_row_ref[...] = sum_row


def chip_body(
    width, mp_count, place_ref, keep_ref, received_ref, column_sum_ref, sum_row_ref,
    own_ref, send_ref, chip_column_ref, chip_row_ref, extra_ref,
):
    rows = own_ref.shape[0]
    embed = own_ref.shape[1]
    columns = [column_sum_ref[...], None]
    sum_rows = [sum_row_ref[...], None]
    columns[1], sum_rows[1] = load_sums(received_ref[:rows, embed:], embed)
    chip_column = columns[0] + columns[1]
    chip_row = sum_rows[0] + sum_rows[1]
    for i in range(2):
        group = (place_ref[0] ^ (2 * i)) & (mp_count - 1)
        mean = pick_rows(chip_row, rows, group) / (2 * width)
        here = slice(i * rows, (i + 1) * rows)
        total = keep_ref[here, :] + received_ref[here, :embed].astype(jnp.float32)
        for column, sum_row in zip(columns, sum_rows):
            total = total + (pick_rows(sum_row, rows, group) / width - mean) * column
        if i == 0:
            own_ref[...] = total
        else:
            send_ref[:, :embed] = total.astype(jnp.bfloat16)
    send_ref[:, embed:] = store_sums(extra_ref, chip_column, chip_row)
    chip_column_ref[...] = chip_column
    chip_row_ref[...] = chip_row


def rows_body(
    full_width, mp_count, place_ref, own_ref, received_ref, column_sum_ref, sum_row_ref,
    project_ref, mean_ref, weight_sum_ref,
):
    rows, embed = own_ref.shape
    columns = [column_sum_ref[...], None]
    sum_rows = [sum_row_ref[...], None]
    columns[1], sum_rows[1] = load_sums(received_ref[:, embed:], embed)
    group = place_ref[0] & (mp_count - 1)
    full_row = sum_rows[0] + sum_rows[1]
    mean = pick_rows(full_row, rows, group) / full_width
    project = own_ref[...] + received_ref[:, :embed].astype(jnp.float32)
    for column, sum_row in zip(columns, sum_rows):
        part_mean = pick_rows(sum_row, rows, group) / (full_width // 2)
        project = project + (part_mean - mean) * column
    project_ref[...] = project.astype(jnp.bfloat16)
    mean_ref[...] = pick_rows(full_row, mean_ref.shape[0], 0) / full_width
    weight_sum_ref[...] = columns[0] + columns[1]


def centre_body(features_ref, mean_ref, out_ref):
    centred = features_ref[...].astype(jnp.float32) - mean_ref[...]
    out_ref[...] = centred.astype(jnp.bfloat16)


def grad_body(first, project_ref, *refs):
    (*texts, out_ref) = refs
    project = project_ref[...].astype(jnp.float32)
    inv_norm = lax.rsqrt(jnp.sum(project * project, axis=1, keepdims=True) + epsilon)
    unit_img = project * inv_norm
    unit_img_b = unit_img.astype(jnp.bfloat16)
    grad_unit = jnp.zeros_like(project)
    at = 0
    for ref in texts:
        unit_txt_b = ref[...]
        logits = (
            logit_scale
            * lax.dot_general(
                unit_img_b,
                unit_txt_b,
                (((1,), (1,)), ((), ())),
                preferred_element_type=jnp.float32,
            )
            + logit_bias
        )
        text = lax.broadcasted_iota(jnp.int32, logits.shape, 1) + at
        image = lax.broadcasted_iota(jnp.int32, logits.shape, 0) + first
        labels = jnp.where(text == image, 1.0, -1.0)
        slopes = (-labels / (1.0 + jnp.exp(labels * logits))).astype(jnp.bfloat16)
        grad_unit = grad_unit + jnp.dot(slopes, unit_txt_b, preferred_element_type=jnp.float32)
        at += unit_txt_b.shape[0]
    grad_unit = logit_scale * grad_unit
    grad_proj = inv_norm * (
        grad_unit - unit_img * jnp.sum(unit_img * grad_unit, axis=1, keepdims=True)
    )
    out_ref[...] = grad_proj.astype(jnp.bfloat16)


def weight_body(
    rows, mp_count, normed_order, orders, tiles, place_ref, normed_ref, *refs
):
    count = 2 * len(orders)
    arrays = refs[:count]
    previous = refs[count : count + 1] if len(refs) - count > (1 if tiles == 1 else 3) else ()
    outs = refs[count + len(previous) :]
    blocks = []
    for order in orders:
        for i in range(2):
            for flip in order:
                group = (place_ref[0] ^ flip ^ i) & (mp_count - 1)
                at = normed_order.index(flip - flip % mp_count) * mp_count
                start = pl.multiple_of((at + group) * rows, rows)
                blocks.append(normed_ref[pl.ds(start, rows), :])
    normed = jnp.concatenate(blocks, axis=0)
    gradient = jnp.concatenate([array[...] for array in arrays], axis=0)
    if tiles == 1:
        total = lax.dot_general(
            normed, gradient, (((0,), (0,)), ((), ())), preferred_element_type=jnp.float32
        )
        for ref in previous:
            total = total + ref[...]
        outs[0][...] = total
        return
    out_hbm, total_ref, sent = outs
    wide = gradient.shape[1] // tiles
    copies = []
    for k in range(tiles):
        here = slice(k * wide, (k + 1) * wide)
        total = lax.dot_general(
            normed, gradient[:, here], (((0,), (0,)), ((), ())), preferred_element_type=jnp.float32
        )
        for ref in previous:
            total = total + ref[:, here]
        total_ref[:, here] = total
        copies.append(
            pltpu.make_async_copy(total_ref.at[:, here], out_hbm.at[:, here], sent.at[k])
        )
        copies[-1].start()
    for copy in copies:
        copy.wait()


def features_body(full_width, rows, mp_count, place_ref, weight_ref, weight_sum_ref, *refs):
    (*parts, out_ref, group_ref) = refs
    for flip, part in enumerate(parts):
        start = pl.multiple_of(((place_ref[0] ^ flip) & (mp_count - 1)) * rows, rows)
        group_ref[pl.ds(start, rows), :] = part[:rows, :]
    group = group_ref[...]
    grad_normed = lax.dot_general(
        group, weight_ref[...], (((1,), (1,)), ((), ())), preferred_element_type=jnp.float32
    )
    grad_total = jnp.sum(group.astype(jnp.float32) * weight_sum_ref[...], axis=1, keepdims=True)
    out_ref[...] = (grad_normed - grad_total / full_width).astype(jnp.bfloat16)


def shards_gathered(features, proj_weight, texts):
    axes = ("dp", "mp")
    dp_count, mp_count = lax.axis_size("dp"), lax.axis_size("mp")
    count = dp_count * mp_count
    plane_count = 2 * mp_count
    local_rows, width = features.shape
    embed = proj_weight.shape[1]
    rows = texts.shape[0]
    half = local_rows // 2
    full_width = width * mp_count
    place = (lax.axis_index("dp") * mp_count + lax.axis_index("mp")).astype(jnp.int32).reshape(1)
    core, across, column = 1, 2, mp_count
    line = list(range(plane_count, count, plane_count))

    def swap(value, flip):
        return lax.ppermute(value, axes, [(i, i ^ flip) for i in range(count)])

    def struct(dims, kind=jnp.bfloat16):
        return jax.ShapeDtypeStruct(dims, kind)

    def along_line(value, order):
        return jnp.concatenate([value] + [swap(value, flip) for flip in order], axis=0)

    smem = pl.BlockSpec(memory_space=pltpu.SMEM)
    vmem = pl.BlockSpec(memory_space=pltpu.VMEM)
    sums = [struct((1, embed), jnp.float32), struct((1, LANES), jnp.float32)]
    extra = pltpu.VMEM((rows, LANES), jnp.float32)

    keep, send, column_sum, sum_row = kernel_call(
        functools.partial(project_body, rows, mp_count),
        [struct((half, embed), jnp.float32), struct((half, embed + LANES))] + sums,
        scratch=[extra],
        in_specs=[smem, vmem, vmem],
        flops=2 * local_rows * width * embed,
        name="project",
    )(place, features, proj_weight)
    own, send, column_sum, sum_row = kernel_call(
        functools.partial(chip_body, width, mp_count),
        [struct((rows, embed), jnp.float32), struct((rows, embed + LANES))] + sums,
        scratch=[extra],
        in_specs=[smem] + [vmem] * 4,
        name="chip_project",
    )(place, keep, swap(send, core), column_sum, sum_row)
    far, near = line[1], line[0]
    order = [0, far, near, far ^ near]
    plane = [0, column, across, column | across]
    unit_txt_b = kernel_call(texts_body, struct(texts.shape), name="unit_texts")(texts)
    txt_line = jnp.concatenate(
        [unit_txt_b] + [swap(unit_txt_b, flip) for flip in order[1:]], axis=0
    )
    send, txt_line = lax.optimization_barrier((send, txt_line))
    txt_plane = [txt_line] + [swap(txt_line, flip) for flip in plane[1:]]

    project, mean, weight_sum = kernel_call(
        functools.partial(rows_body, full_width, mp_count),
        [
            struct((rows, embed)),
            struct((local_rows, 1), jnp.float32),
            struct((1, embed), jnp.float32),
        ],
        in_specs=[smem] + [vmem] * 4,
        name="project_rows",
    )(place, own, swap(send, across), column_sum, sum_row)
    normed_b = kernel_call(centre_body, struct(features.shape), name="centre")(features, mean)

    line_rows = jnp.concatenate([project, swap(project, far)], axis=0)
    line_rows = jnp.concatenate([line_rows, swap(line_rows, near)], axis=0)
    line_rows, txt_plane[1] = lax.optimization_barrier((line_rows, txt_plane[1]))
    plane_rows = [line_rows] + [swap(line_rows, flip) for flip in plane[1:]]
    own_texts = jnp.concatenate(txt_plane, axis=0)
    other_texts = swap(own_texts, core)

    normed = jnp.concatenate([normed_b, swap(normed_b, column)], axis=0)
    normed = jnp.concatenate([normed, swap(normed, far)], axis=0)
    normed = jnp.concatenate([normed, swap(normed, near)], axis=0)
    normed_order = sum([[o, o ^ column] for o in order], [])

    grads = []
    for index, value in enumerate(plane_rows):
        grads.append(
            kernel_call(
                functools.partial(grad_body, index * local_rows),
                struct(value.shape),
                flops=4 * local_rows * count * rows * embed,
                name="grad",
            )(value, own_texts, other_texts)
        )
    others = [swap(value, core) for value in grads]

    def add_product(indices, previous, final=False):
        arrays = sum([[grads[i], others[i]] for i in indices], [])
        orders = [[o ^ plane[i] for o in order] for i in indices]
        tiles = 3 if final else 1
        scratch = [
            pltpu.VMEM(proj_weight.shape, jnp.float32),
            pltpu.SemaphoreType.DMA((tiles,)),
        ]
        return kernel_call(
            functools.partial(weight_body, rows, mp_count, normed_order, orders, tiles),
            struct(proj_weight.shape, jnp.float32),
            scratch=scratch if final else (),
            in_specs=[smem] + [vmem] * (1 + len(arrays) + len(previous)),
            out_specs=pl.BlockSpec(memory_space=pl.ANY) if final else vmem,
            flops=4 * width * embed * local_rows * len(indices),
            name="weight",
        )(place, normed, *arrays, *previous)

    grad_features = kernel_call(
        functools.partial(features_body, full_width, rows, mp_count),
        struct(features.shape),
        scratch=[pltpu.VMEM((local_rows, embed), jnp.bfloat16)],
        in_specs=[smem] + [vmem] * (2 + mp_count),
        flops=2 * local_rows * width * embed,
        name="grad_features",
    )(place, proj_weight, weight_sum, grads[0], others[0], grads[2], others[2])
    grad_weight = add_product([0], [])
    grad_weight = add_product([1, 2], [grad_weight])
    grad_weight = add_product([3], [grad_weight], True)
    return grad_features, grad_weight


def shards(features, proj_weight, texts):
    dp_count, mp_count = lax.axis_size("dp"), lax.axis_size("mp")
    count = dp_count * mp_count
    rows = texts.shape[0]
    embed = texts.shape[1]
    fits = (
        count * rows * (embed + LANES) * 2 <= GATHER_BYTES
        and count & (count - 1) == 0
        and mp_count == 4
        and count == 8 * mp_count
        and features.shape[0] == LANES == mp_count * rows
        and embed % LANES == 0
        and 2 * (embed // LANES) + 3 <= rows
        and rows % 16 == 0
    )
    plan = shards_gathered if fits else shards_summed
    return plan(features, proj_weight, texts)


def solution(mesh):
    return jax.shard_map(
        shards,
        mesh=mesh,
        in_specs=(P("dp", "mp"), P("mp", None), P(("dp", "mp"), None)),
        out_specs=(P("dp", "mp"), P("mp", None)),
        check_vma=False,
    )
```

```python
import functools

import jax
import jax.numpy as jnp
from jax import lax
from jax.experimental import pallas as pl
from jax.experimental.pallas import tpu as pltpu
from jax.sharding import PartitionSpec as P

logit_scale = 100.0
logit_bias = -10.0
epsilon = 1e-06
LANES = 128
GATHER_BYTES = 8 << 20
VMEM_BYTES = 40 << 20


def unit_rows(values):
    return values * lax.rsqrt(jnp.sum(values * values, axis=1, keepdims=True) + epsilon)


def add_texts(unit_img_b, image_ids, piece, piece_ids):
    unit_txt_b = unit_rows(piece.astype(jnp.float32)).astype(jnp.bfloat16)
    logits = (
        logit_scale * jnp.dot(unit_img_b, unit_txt_b.T, preferred_element_type=jnp.float32)
        + logit_bias
    )
    labels = jnp.where(image_ids[:, None] == piece_ids[None, :], 1.0, -1.0).astype(jnp.float32)
    slopes = (-labels * jax.nn.sigmoid(-labels * logits)).astype(jnp.bfloat16)
    return logit_scale * jnp.dot(slopes, unit_txt_b, preferred_element_type=jnp.float32)


def shards_summed(features, proj_weight, texts):
    local_rows = features.shape[0]
    width_local = features.shape[1]
    mp_count = lax.axis_size("mp")
    full_width = width_local * mp_count
    mp_index = lax.axis_index("mp")
    dp_index = lax.axis_index("dp")
    text_rows = texts.shape[0]
    inputs = features.astype(jnp.float32)
    mean_in = lax.psum(jnp.sum(inputs, axis=1, keepdims=True), "mp") / full_width
    centred = inputs - mean_in
    normed_b = centred.astype(jnp.bfloat16)
    partial_proj = jnp.dot(normed_b, proj_weight, preferred_element_type=jnp.float32)
    project = lax.psum(partial_proj, "mp")
    inv_norm = lax.rsqrt(jnp.sum(project * project, axis=1, keepdims=True) + epsilon)
    unit_img = project * inv_norm
    unit_img_b = unit_img.astype(jnp.bfloat16)
    image_ids = dp_index * local_rows + jnp.arange(local_rows, dtype=jnp.int32)
    piece = lax.all_gather(texts, "dp", axis=0, tiled=True)
    positions = jnp.arange(piece.shape[0], dtype=jnp.int32)
    shard_of = positions // text_rows
    piece_ids = (shard_of * mp_count + mp_index) * text_rows + positions % text_rows
    grad_unit = add_texts(unit_img_b, image_ids, piece, piece_ids)
    grad_unit = lax.psum(grad_unit, "mp")
    grad_proj = inv_norm * (
        grad_unit - unit_img * jnp.sum(unit_img * grad_unit, axis=1, keepdims=True)
    )
    grad_proj_b = grad_proj.astype(jnp.bfloat16)
    weight_part = jnp.dot(normed_b.T, grad_proj_b, preferred_element_type=jnp.float32)
    grad_weight = lax.psum(weight_part, "dp")
    grad_normed = jnp.dot(grad_proj_b, proj_weight.T, preferred_element_type=jnp.float32)
    grad_total = lax.psum(jnp.sum(grad_normed, axis=1, keepdims=True), "mp")
    grad_in = grad_normed - grad_total / full_width
    return (grad_in.astype(jnp.bfloat16), grad_weight)


def split_terms(value, count):
    terms = []
    for _ in range(count):
        term = value.astype(jnp.bfloat16).astype(jnp.float32)
        terms.append(term)
        value = value - term
    return terms


def kernel_call(body, outs, scratch=(), flops=0, **names):
    return pl.pallas_call(
        body,
        out_shape=outs,
        scratch_shapes=scratch,
        compiler_params=pltpu.CompilerParams(vmem_limit_bytes=VMEM_BYTES),
        cost_estimate=pl.CostEstimate(flops=flops, bytes_accessed=0, transcendentals=0),
        **names,
    )


def texts_body(texts_ref, out_ref):
    out_ref[...] = unit_rows(texts_ref[...].astype(jnp.float32)).astype(jnp.bfloat16)


def store_sums(extra_ref, column_sum, sum_row):
    extra_ref[...] = jnp.zeros_like(extra_ref)
    at = 0
    for term in split_terms(column_sum, 2):
        for i in range(column_sum.shape[1] // LANES):
            extra_ref[at : at + 1, :] = term[:, i * LANES : (i + 1) * LANES]
            at += 1
    for term in split_terms(sum_row, 3):
        extra_ref[at : at + 1, :] = term
        at += 1
    return extra_ref[...].astype(jnp.bfloat16)


def load_sums(extra, embed):
    chunks = embed // LANES
    extra = extra.astype(jnp.float32)
    column_sum = jnp.concatenate(
        [extra[i : i + 1] + extra[chunks + i : chunks + i + 1] for i in range(chunks)], axis=1
    )
    at = 2 * chunks
    return column_sum, extra[at : at + 1] + extra[at + 1 : at + 2] + extra[at + 2 : at + 3]


def pick_rows(sum_row, rows, group):
    row = lax.broadcasted_iota(jnp.int32, (rows, LANES), 0)
    lane = lax.broadcasted_iota(jnp.int32, (rows, LANES), 1)
    return jnp.sum(jnp.where(lane == row + group * rows, sum_row, 0.0), axis=1, keepdims=True)


def project_body(
    rows, mp_count, place_ref, features_ref, weight_ref,
    keep_ref, send_ref, column_sum_ref, sum_row_ref, extra_ref,
):
    embed = weight_ref.shape[1]
    local_rows, width = features_ref.shape
    values = features_ref[...].astype(jnp.float32)
    row_sum = jnp.sum(values, axis=1, keepdims=True)
    column_sum = jnp.sum(weight_ref[...].astype(jnp.float32), axis=0, keepdims=True)
    row = lax.broadcasted_iota(jnp.int32, (local_rows, LANES), 0)
    lane = lax.broadcasted_iota(jnp.int32, (local_rows, LANES), 1)
    sum_row = jnp.sum(jnp.where(row == lane, row_sum, 0.0), axis=0, keepdims=True)
    ordered = []
    for flip in list(range(0, mp_count, 2)) + list(range(1, mp_count, 2)):
        start = pl.multiple_of(((place_ref[0] ^ flip) & (mp_count - 1)) * rows, rows)
        block = features_ref[pl.ds(start, rows), :].astype(jnp.float32)
        ordered.append(block - jnp.sum(block, axis=1, keepdims=True) / width)
    centred = jnp.concatenate(ordered, axis=0).astype(jnp.bfloat16)
    product = jnp.dot(centred, weight_ref[...], preferred_element_type=jnp.float32)
    half = local_rows // 2
    keep_ref[...] = product[:half]
    send_ref[:, :embed] = product[half:].astype(jnp.bfloat16)
    extra = store_sums(extra_ref, column_sum, sum_row)
    for i in range(half // rows):
        send_ref[i * rows : (i + 1) * rows, embed:] = extra
    column_sum_ref[...] = column_sum
    sum_row_ref[...] = sum_row


def chip_body(
    width, mp_count, place_ref, keep_ref, received_ref, column_sum_ref, sum_row_ref,
    own_ref, send_ref, chip_column_ref, chip_row_ref, extra_ref,
):
    rows = own_ref.shape[0]
    embed = own_ref.shape[1]
    columns = [column_sum_ref[...], None]
    sum_rows = [sum_row_ref[...], None]
    columns[1], sum_rows[1] = load_sums(received_ref[:rows, embed:], embed)
    chip_column = columns[0] + columns[1]
    chip_row = sum_rows[0] + sum_rows[1]
    for i in range(2):
        group = (place_ref[0] ^ (2 * i)) & (mp_count - 1)
        mean = pick_rows(chip_row, rows, group) / (2 * width)
        here = slice(i * rows, (i + 1) * rows)
        total = keep_ref[here, :] + received_ref[here, :embed].astype(jnp.float32)
        for column, sum_row in zip(columns, sum_rows):
            total = total + (pick_rows(sum_row, rows, group) / width - mean) * column
        if i == 0:
            own_ref[...] = total
        else:
            send_ref[:, :embed] = total.astype(jnp.bfloat16)
    send_ref[:, embed:] = store_sums(extra_ref, chip_column, chip_row)
    chip_column_ref[...] = chip_column
    chip_row_ref[...] = chip_row


def rows_body(
    full_width, mp_count, place_ref, own_ref, received_ref, column_sum_ref, sum_row_ref,
    project_ref, mean_ref, weight_sum_ref,
):
    rows, embed = own_ref.shape
    columns = [column_sum_ref[...], None]
    sum_rows = [sum_row_ref[...], None]
    columns[1], sum_rows[1] = load_sums(received_ref[:, embed:], embed)
    group = place_ref[0] & (mp_count - 1)
    full_row = sum_rows[0] + sum_rows[1]
    mean = pick_rows(full_row, rows, group) / full_width
    project = own_ref[...] + received_ref[:, :embed].astype(jnp.float32)
    for column, sum_row in zip(columns, sum_rows):
        part_mean = pick_rows(sum_row, rows, group) / (full_width // 2)
        project = project + (part_mean - mean) * column
    project_ref[...] = project.astype(jnp.bfloat16)
    mean_ref[...] = pick_rows(full_row, mean_ref.shape[0], 0) / full_width
    weight_sum_ref[...] = columns[0] + columns[1]


def centre_body(features_ref, mean_ref, out_ref):
    centred = features_ref[...].astype(jnp.float32) - mean_ref[...]
    out_ref[...] = centred.astype(jnp.bfloat16)


def grad_body(first, project_ref, *refs):
    (*texts, out_ref) = refs
    project = project_ref[...].astype(jnp.float32)
    inv_norm = lax.rsqrt(jnp.sum(project * project, axis=1, keepdims=True) + epsilon)
    unit_img = project * inv_norm
    unit_img_b = unit_img.astype(jnp.bfloat16)
    grad_unit = jnp.zeros_like(project)
    at = 0
    for ref in texts:
        unit_txt_b = ref[...]
        logits = (
            logit_scale
            * lax.dot_general(
                unit_img_b,
                unit_txt_b,
                (((1,), (1,)), ((), ())),
                preferred_element_type=jnp.float32,
            )
            + logit_bias
        )
        text = lax.broadcasted_iota(jnp.int32, logits.shape, 1) + at
        image = lax.broadcasted_iota(jnp.int32, logits.shape, 0) + first
        labels = jnp.where(text == image, 1.0, -1.0)
        slopes = (-labels / (1.0 + jnp.exp(labels * logits))).astype(jnp.bfloat16)
        grad_unit = grad_unit + jnp.dot(slopes, unit_txt_b, preferred_element_type=jnp.float32)
        at += unit_txt_b.shape[0]
    grad_unit = logit_scale * grad_unit
    grad_proj = inv_norm * (
        grad_unit - unit_img * jnp.sum(unit_img * grad_unit, axis=1, keepdims=True)
    )
    out_ref[...] = grad_proj.astype(jnp.bfloat16)


def weight_body(
    rows, mp_count, normed_order, orders, tiles, place_ref, normed_ref, *refs
):
    count = 2 * len(orders)
    arrays = refs[:count]
    previous = refs[count : count + 1] if len(refs) - count > (1 if tiles == 1 else 3) else ()
    outs = refs[count + len(previous) :]
    blocks = []
    for order in orders:
        for i in range(2):
            for flip in order:
                group = (place_ref[0] ^ flip ^ i) & (mp_count - 1)
                at = normed_order.index(flip - flip % mp_count) * mp_count
                start = pl.multiple_of((at + group) * rows, rows)
                blocks.append(normed_ref[pl.ds(start, rows), :])
    normed = jnp.concatenate(blocks, axis=0)
    gradient = jnp.concatenate([array[...] for array in arrays], axis=0)
    if tiles == 1:
        total = lax.dot_general(
            normed, gradient, (((0,), (0,)), ((), ())), preferred_element_type=jnp.float32
        )
        for ref in previous:
            total = total + ref[...]
        outs[0][...] = total
        return
    out_hbm, total_ref, sent = outs
    wide = gradient.shape[1] // tiles
    copies = []
    for k in range(tiles):
        here = slice(k * wide, (k + 1) * wide)
        total = lax.dot_general(
            normed, gradient[:, here], (((0,), (0,)), ((), ())), preferred_element_type=jnp.float32
        )
        for ref in previous:
            total = total + ref[:, here]
        total_ref[:, here] = total
        copies.append(
            pltpu.make_async_copy(total_ref.at[:, here], out_hbm.at[:, here], sent.at[k])
        )
        copies[-1].start()
    for copy in copies:
        copy.wait()


def features_body(full_width, rows, mp_count, place_ref, weight_ref, weight_sum_ref, *refs):
    (*parts, out_ref, group_ref) = refs
    for flip, part in enumerate(parts):
        start = pl.multiple_of(((place_ref[0] ^ flip) & (mp_count - 1)) * rows, rows)
        group_ref[pl.ds(start, rows), :] = part[:rows, :]
    group = group_ref[...]
    grad_normed = lax.dot_general(
        group, weight_ref[...], (((1,), (1,)), ((), ())), preferred_element_type=jnp.float32
    )
    grad_total = jnp.sum(group.astype(jnp.float32) * weight_sum_ref[...], axis=1, keepdims=True)
    out_ref[...] = (grad_normed - grad_total / full_width).astype(jnp.bfloat16)


def shards_gathered(features, proj_weight, texts):
    axes = ("dp", "mp")
    dp_count, mp_count = lax.axis_size("dp"), lax.axis_size("mp")
    count = dp_count * mp_count
    plane_count = 2 * mp_count
    local_rows, width = features.shape
    embed = proj_weight.shape[1]
    rows = texts.shape[0]
    half = local_rows // 2
    full_width = width * mp_count
    place = (lax.axis_index("dp") * mp_count + lax.axis_index("mp")).astype(jnp.int32).reshape(1)
    core, across, column = 1, 2, mp_count
    line = list(range(plane_count, count, plane_count))

    def swap(value, flip):
        return lax.ppermute(value, axes, [(i, i ^ flip) for i in range(count)])

    def struct(dims, kind=jnp.bfloat16):
        return jax.ShapeDtypeStruct(dims, kind)

    def along_line(value, order):
        return jnp.concatenate([value] + [swap(value, flip) for flip in order], axis=0)

    smem = pl.BlockSpec(memory_space=pltpu.SMEM)
    vmem = pl.BlockSpec(memory_space=pltpu.VMEM)
    sums = [struct((1, embed), jnp.float32), struct((1, LANES), jnp.float32)]
    extra = pltpu.VMEM((rows, LANES), jnp.float32)

    keep, send, column_sum, sum_row = kernel_call(
        functools.partial(project_body, rows, mp_count),
        [struct((half, embed), jnp.float32), struct((half, embed + LANES))] + sums,
        scratch=[extra],
        in_specs=[smem, vmem, vmem],
        flops=2 * local_rows * width * embed,
        name="project",
    )(place, features, proj_weight)
    own, send, column_sum, sum_row = kernel_call(
        functools.partial(chip_body, width, mp_count),
        [struct((rows, embed), jnp.float32), struct((rows, embed + LANES))] + sums,
        scratch=[extra],
        in_specs=[smem] + [vmem] * 4,
        name="chip_project",
    )(place, keep, swap(send, core), column_sum, sum_row)
    far, near = line[1], line[0]
    order = [0, far, near, far ^ near]
    plane = [0, across, column, column | across]
    unit_txt_b = kernel_call(texts_body, struct(texts.shape), name="unit_texts")(texts)
    txt_line = jnp.concatenate(
        [unit_txt_b] + [swap(unit_txt_b, flip) for flip in order[1:]], axis=0
    )
    send, txt_line = lax.optimization_barrier((send, txt_line))
    txt_plane = [txt_line] + [swap(txt_line, flip) for flip in plane[1:]]

    project, mean, weight_sum = kernel_call(
        functools.partial(rows_body, full_width, mp_count),
        [
            struct((rows, embed)),
            struct((local_rows, 1), jnp.float32),
            struct((1, embed), jnp.float32),
        ],
        in_specs=[smem] + [vmem] * 4,
        name="project_rows",
    )(place, own, swap(send, across), column_sum, sum_row)
    normed_b = kernel_call(centre_body, struct(features.shape), name="centre")(features, mean)

    line_rows = jnp.concatenate([project, swap(project, far)], axis=0)
    line_rows = jnp.concatenate([line_rows, swap(line_rows, near)], axis=0)
    normed = jnp.concatenate([normed_b, swap(normed_b, column)], axis=0)
    normed_far = swap(normed, far)
    line_rows, normed_far, *txt_plane = lax.optimization_barrier(
        (line_rows, normed_far, *txt_plane)
    )
    normed = jnp.concatenate([normed, normed_far], axis=0)
    normed_near = swap(normed, near)
    normed_order = sum([[o, o ^ column] for o in order], [])
    all_texts = [jnp.concatenate(txt_plane, axis=0)]
    all_texts.append(swap(all_texts[0], core))
    plane_rows = [line_rows] + [swap(line_rows, flip) for flip in plane[1:3]]
    last_rows = line_rows
    plane_rows.append(swap(last_rows, plane[3]))

    def gradient(index):
        return kernel_call(
            functools.partial(grad_body, index * local_rows),
            struct(line_rows.shape),
            flops=4 * local_rows * count * rows * embed,
            name="grad",
        )(plane_rows[index], *all_texts)

    grads = [gradient(0)]
    others = [swap(grads[0], core)]
    plane_rows[1], _ = lax.optimization_barrier((plane_rows[1], grads[0]))
    grads.append(gradient(1))
    others.append(swap(grads[1], core))
    plane_rows[3], normed_near = lax.optimization_barrier((plane_rows[3], normed_near))
    normed = jnp.concatenate([normed, normed_near], axis=0)

    def add_product(indices, previous, final=False):
        arrays = sum([[grads[i], others[i]] for i in indices], [])
        orders = [[o ^ plane[i] for o in order] for i in indices]
        tiles = 3 if final else 1
        scratch = [
            pltpu.VMEM(proj_weight.shape, jnp.float32),
            pltpu.SemaphoreType.DMA((tiles,)),
        ]
        return kernel_call(
            functools.partial(weight_body, rows, mp_count, normed_order, orders, tiles),
            struct(proj_weight.shape, jnp.float32),
            scratch=scratch if final else (),
            in_specs=[smem] + [vmem] * (1 + len(arrays) + len(previous)),
            out_specs=pl.BlockSpec(memory_space=pl.ANY) if final else vmem,
            flops=4 * width * embed * local_rows * len(indices),
            name="weight",
        )(place, normed, *arrays, *previous)

    grad_features = kernel_call(
        functools.partial(features_body, full_width, rows, mp_count),
        struct(features.shape),
        scratch=[pltpu.VMEM((local_rows, embed), jnp.bfloat16)],
        in_specs=[smem] + [vmem] * (2 + mp_count),
        flops=2 * local_rows * width * embed,
        name="grad_features",
    )(place, proj_weight, weight_sum, grads[0], others[0], grads[1], others[1])
    first = [0, 1]
    grad_weight = add_product(first, [])
    grads.append(gradient(2))
    others.append(swap(grads[2], core))
    plane_rows[3], _, _ = lax.optimization_barrier((plane_rows[3], grad_weight, grad_features))
    grads.append(gradient(3))
    others.append(swap(grads[3], core))
    grad_weight = add_product([2], [grad_weight])
    grad_weight = add_product([3], [grad_weight], True)
    return grad_features, grad_weight


def shards(features, proj_weight, texts):
    dp_count, mp_count = lax.axis_size("dp"), lax.axis_size("mp")
    count = dp_count * mp_count
    rows = texts.shape[0]
    embed = texts.shape[1]
    fits = (
        count * rows * (embed + LANES) * 2 <= GATHER_BYTES
        and count & (count - 1) == 0
        and mp_count == 4
        and count == 8 * mp_count
        and features.shape[0] == LANES == mp_count * rows
        and embed % LANES == 0
        and 2 * (embed // LANES) + 3 <= rows
        and rows % 16 == 0
    )
    plan = shards_gathered if fits else shards_summed
    return plan(features, proj_weight, texts)


def solution(mesh):
    return jax.shard_map(
        shards,
        mesh=mesh,
        in_specs=(P("dp", "mp"), P("mp", None), P(("dp", "mp"), None)),
        out_specs=(P("dp", "mp"), P("mp", None)),
        check_vma=False,
    )
```

```python
import functools

import jax
import jax.numpy as jnp
from jax import lax
from jax.experimental import pallas as pl
from jax.experimental.pallas import tpu as pltpu
from jax.sharding import PartitionSpec as P

logit_scale = 100.0
logit_bias = -10.0
epsilon = 1e-06
LANES = 128
GATHER_BYTES = 8 << 20
VMEM_BYTES = 40 << 20


def unit_rows(values):
    return values * lax.rsqrt(jnp.sum(values * values, axis=1, keepdims=True) + epsilon)


def add_texts(unit_img_b, image_ids, piece, piece_ids):
    unit_txt_b = unit_rows(piece.astype(jnp.float32)).astype(jnp.bfloat16)
    logits = (
        logit_scale * jnp.dot(unit_img_b, unit_txt_b.T, preferred_element_type=jnp.float32)
        + logit_bias
    )
    labels = jnp.where(image_ids[:, None] == piece_ids[None, :], 1.0, -1.0).astype(jnp.float32)
    slopes = (-labels * jax.nn.sigmoid(-labels * logits)).astype(jnp.bfloat16)
    return logit_scale * jnp.dot(slopes, unit_txt_b, preferred_element_type=jnp.float32)


def shards_summed(features, proj_weight, texts):
    local_rows = features.shape[0]
    width_local = features.shape[1]
    mp_count = lax.axis_size("mp")
    full_width = width_local * mp_count
    mp_index = lax.axis_index("mp")
    dp_index = lax.axis_index("dp")
    text_rows = texts.shape[0]
    inputs = features.astype(jnp.float32)
    mean_in = lax.psum(jnp.sum(inputs, axis=1, keepdims=True), "mp") / full_width
    centred = inputs - mean_in
    normed_b = centred.astype(jnp.bfloat16)
    partial_proj = jnp.dot(normed_b, proj_weight, preferred_element_type=jnp.float32)
    project = lax.psum(partial_proj, "mp")
    inv_norm = lax.rsqrt(jnp.sum(project * project, axis=1, keepdims=True) + epsilon)
    unit_img = project * inv_norm
    unit_img_b = unit_img.astype(jnp.bfloat16)
    image_ids = dp_index * local_rows + jnp.arange(local_rows, dtype=jnp.int32)
    piece = lax.all_gather(texts, "dp", axis=0, tiled=True)
    positions = jnp.arange(piece.shape[0], dtype=jnp.int32)
    shard_of = positions // text_rows
    piece_ids = (shard_of * mp_count + mp_index) * text_rows + positions % text_rows
    grad_unit = add_texts(unit_img_b, image_ids, piece, piece_ids)
    grad_unit = lax.psum(grad_unit, "mp")
    grad_proj = inv_norm * (
        grad_unit - unit_img * jnp.sum(unit_img * grad_unit, axis=1, keepdims=True)
    )
    grad_proj_b = grad_proj.astype(jnp.bfloat16)
    weight_part = jnp.dot(normed_b.T, grad_proj_b, preferred_element_type=jnp.float32)
    grad_weight = lax.psum(weight_part, "dp")
    grad_normed = jnp.dot(grad_proj_b, proj_weight.T, preferred_element_type=jnp.float32)
    grad_total = lax.psum(jnp.sum(grad_normed, axis=1, keepdims=True), "mp")
    grad_in = grad_normed - grad_total / full_width
    return (grad_in.astype(jnp.bfloat16), grad_weight)


def split_terms(value, count):
    terms = []
    for _ in range(count):
        term = value.astype(jnp.bfloat16).astype(jnp.float32)
        terms.append(term)
        value = value - term
    return terms


def kernel_call(body, outs, scratch=(), flops=0, **names):
    return pl.pallas_call(
        body,
        out_shape=outs,
        scratch_shapes=scratch,
        compiler_params=pltpu.CompilerParams(vmem_limit_bytes=VMEM_BYTES),
        cost_estimate=pl.CostEstimate(flops=flops, bytes_accessed=0, transcendentals=0),
        **names,
    )


def texts_body(texts_ref, out_ref):
    out_ref[...] = unit_rows(texts_ref[...].astype(jnp.float32)).astype(jnp.bfloat16)


def store_sums(extra_ref, column_sum, sum_row):
    extra_ref[...] = jnp.zeros_like(extra_ref)
    at = 0
    for term in split_terms(column_sum, 2):
        for i in range(column_sum.shape[1] // LANES):
            extra_ref[at : at + 1, :] = term[:, i * LANES : (i + 1) * LANES]
            at += 1
    for term in split_terms(sum_row, 3):
        extra_ref[at : at + 1, :] = term
        at += 1
    return extra_ref[...].astype(jnp.bfloat16)


def load_sums(extra, embed):
    chunks = embed // LANES
    extra = extra.astype(jnp.float32)
    column_sum = jnp.concatenate(
        [extra[i : i + 1] + extra[chunks + i : chunks + i + 1] for i in range(chunks)], axis=1
    )
    at = 2 * chunks
    return column_sum, extra[at : at + 1] + extra[at + 1 : at + 2] + extra[at + 2 : at + 3]


def pick_rows(sum_row, rows, group):
    row = lax.broadcasted_iota(jnp.int32, (rows, LANES), 0)
    lane = lax.broadcasted_iota(jnp.int32, (rows, LANES), 1)
    return jnp.sum(jnp.where(lane == row + group * rows, sum_row, 0.0), axis=1, keepdims=True)


def project_body(
    rows, mp_count, place_ref, features_ref, weight_ref,
    keep_ref, send_ref, column_sum_ref, sum_row_ref, extra_ref,
):
    embed = weight_ref.shape[1]
    local_rows, width = features_ref.shape
    values = features_ref[...].astype(jnp.float32)
    row_sum = jnp.sum(values, axis=1, keepdims=True)
    column_sum = jnp.sum(weight_ref[...].astype(jnp.float32), axis=0, keepdims=True)
    row = lax.broadcasted_iota(jnp.int32, (local_rows, LANES), 0)
    lane = lax.broadcasted_iota(jnp.int32, (local_rows, LANES), 1)
    sum_row = jnp.sum(jnp.where(row == lane, row_sum, 0.0), axis=0, keepdims=True)
    ordered = []
    for flip in list(range(0, mp_count, 2)) + list(range(1, mp_count, 2)):
        start = pl.multiple_of(((place_ref[0] ^ flip) & (mp_count - 1)) * rows, rows)
        block = features_ref[pl.ds(start, rows), :].astype(jnp.float32)
        ordered.append(block - jnp.sum(block, axis=1, keepdims=True) / width)
    centred = jnp.concatenate(ordered, axis=0).astype(jnp.bfloat16)
    product = jnp.dot(centred, weight_ref[...], preferred_element_type=jnp.float32)
    half = local_rows // 2
    keep_ref[...] = product[:half]
    send_ref[:, :embed] = product[half:].astype(jnp.bfloat16)
    extra = store_sums(extra_ref, column_sum, sum_row)
    for i in range(half // rows):
        send_ref[i * rows : (i + 1) * rows, embed:] = extra
    column_sum_ref[...] = column_sum
    sum_row_ref[...] = sum_row


def chip_body(
    width, mp_count, place_ref, keep_ref, received_ref, column_sum_ref, sum_row_ref,
    own_ref, send_ref, chip_column_ref, chip_row_ref, extra_ref,
):
    rows = own_ref.shape[0]
    embed = own_ref.shape[1]
    columns = [column_sum_ref[...], None]
    sum_rows = [sum_row_ref[...], None]
    columns[1], sum_rows[1] = load_sums(received_ref[:rows, embed:], embed)
    chip_column = columns[0] + columns[1]
    chip_row = sum_rows[0] + sum_rows[1]
    for i in range(2):
        group = (place_ref[0] ^ (2 * i)) & (mp_count - 1)
        mean = pick_rows(chip_row, rows, group) / (2 * width)
        here = slice(i * rows, (i + 1) * rows)
        total = keep_ref[here, :] + received_ref[here, :embed].astype(jnp.float32)
        for column, sum_row in zip(columns, sum_rows):
            total = total + (pick_rows(sum_row, rows, group) / width - mean) * column
        if i == 0:
            own_ref[...] = total
        else:
            send_ref[:, :embed] = total.astype(jnp.bfloat16)
    send_ref[:, embed:] = store_sums(extra_ref, chip_column, chip_row)
    chip_column_ref[...] = chip_column
    chip_row_ref[...] = chip_row


def rows_body(
    full_width, mp_count, place_ref, own_ref, received_ref, column_sum_ref, sum_row_ref,
    project_ref, mean_ref, weight_sum_ref,
):
    rows, embed = own_ref.shape
    columns = [column_sum_ref[...], None]
    sum_rows = [sum_row_ref[...], None]
    columns[1], sum_rows[1] = load_sums(received_ref[:, embed:], embed)
    group = place_ref[0] & (mp_count - 1)
    full_row = sum_rows[0] + sum_rows[1]
    mean = pick_rows(full_row, rows, group) / full_width
    project = own_ref[...] + received_ref[:, :embed].astype(jnp.float32)
    for column, sum_row in zip(columns, sum_rows):
        part_mean = pick_rows(sum_row, rows, group) / (full_width // 2)
        project = project + (part_mean - mean) * column
    project_ref[...] = project.astype(jnp.bfloat16)
    mean_ref[...] = pick_rows(full_row, mean_ref.shape[0], 0) / full_width
    weight_sum_ref[...] = columns[0] + columns[1]


def centre_body(features_ref, mean_ref, out_ref):
    centred = features_ref[...].astype(jnp.float32) - mean_ref[...]
    out_ref[...] = centred.astype(jnp.bfloat16)


def grad_body(first, project_ref, *refs):
    (*texts, out_ref) = refs
    project = project_ref[...].astype(jnp.float32)
    inv_norm = lax.rsqrt(jnp.sum(project * project, axis=1, keepdims=True) + epsilon)
    unit_img = project * inv_norm
    unit_img_b = unit_img.astype(jnp.bfloat16)
    grad_unit = jnp.zeros_like(project)
    at = 0
    for ref in texts:
        unit_txt_b = ref[...]
        logits = (
            logit_scale
            * lax.dot_general(
                unit_img_b,
                unit_txt_b,
                (((1,), (1,)), ((), ())),
                preferred_element_type=jnp.float32,
            )
            + logit_bias
        )
        text = lax.broadcasted_iota(jnp.int32, logits.shape, 1) + at
        image = lax.broadcasted_iota(jnp.int32, logits.shape, 0) + first
        labels = jnp.where(text == image, 1.0, -1.0)
        slopes = (-labels / (1.0 + jnp.exp(labels * logits))).astype(jnp.bfloat16)
        grad_unit = grad_unit + jnp.dot(slopes, unit_txt_b, preferred_element_type=jnp.float32)
        at += unit_txt_b.shape[0]
    grad_unit = logit_scale * grad_unit
    grad_proj = inv_norm * (
        grad_unit - unit_img * jnp.sum(unit_img * grad_unit, axis=1, keepdims=True)
    )
    out_ref[...] = grad_proj.astype(jnp.bfloat16)


def weight_body(
    rows, mp_count, normed_order, orders, tiles, place_ref, normed_ref, *refs
):
    count = 2 * len(orders)
    arrays = refs[:count]
    previous = refs[count : count + 1] if len(refs) - count > (1 if tiles == 1 else 3) else ()
    outs = refs[count + len(previous) :]
    blocks = []
    for order in orders:
        for i in range(2):
            for flip in order:
                group = (place_ref[0] ^ flip ^ i) & (mp_count - 1)
                at = normed_order.index(flip - flip % mp_count) * mp_count
                start = pl.multiple_of((at + group) * rows, rows)
                blocks.append(normed_ref[pl.ds(start, rows), :])
    normed = jnp.concatenate(blocks, axis=0)
    gradient = jnp.concatenate([array[...] for array in arrays], axis=0)
    if tiles == 1:
        total = lax.dot_general(
            normed, gradient, (((0,), (0,)), ((), ())), preferred_element_type=jnp.float32
        )
        for ref in previous:
            total = total + ref[...]
        outs[0][...] = total
        return
    out_hbm, total_ref, sent = outs
    wide = gradient.shape[1] // tiles
    copies = []
    for k in range(tiles):
        here = slice(k * wide, (k + 1) * wide)
        total = lax.dot_general(
            normed, gradient[:, here], (((0,), (0,)), ((), ())), preferred_element_type=jnp.float32
        )
        for ref in previous:
            total = total + ref[:, here]
        total_ref[:, here] = total
        copies.append(
            pltpu.make_async_copy(total_ref.at[:, here], out_hbm.at[:, here], sent.at[k])
        )
        copies[-1].start()
    for copy in copies:
        copy.wait()


def features_body(full_width, rows, mp_count, place_ref, weight_ref, weight_sum_ref, *refs):
    (*parts, out_ref, group_ref) = refs
    for flip, part in enumerate(parts):
        start = pl.multiple_of(((place_ref[0] ^ flip) & (mp_count - 1)) * rows, rows)
        group_ref[pl.ds(start, rows), :] = part[:rows, :]
    group = group_ref[...]
    grad_normed = lax.dot_general(
        group, weight_ref[...], (((1,), (1,)), ((), ())), preferred_element_type=jnp.float32
    )
    grad_total = jnp.sum(group.astype(jnp.float32) * weight_sum_ref[...], axis=1, keepdims=True)
    out_ref[...] = (grad_normed - grad_total / full_width).astype(jnp.bfloat16)


def shards_gathered(features, proj_weight, texts):
    axes = ("dp", "mp")
    dp_count, mp_count = lax.axis_size("dp"), lax.axis_size("mp")
    count = dp_count * mp_count
    plane_count = 2 * mp_count
    local_rows, width = features.shape
    embed = proj_weight.shape[1]
    rows = texts.shape[0]
    half = local_rows // 2
    full_width = width * mp_count
    place = (lax.axis_index("dp") * mp_count + lax.axis_index("mp")).astype(jnp.int32).reshape(1)
    core, across, column = 1, 2, mp_count
    line = list(range(plane_count, count, plane_count))

    def swap(value, flip):
        return lax.ppermute(value, axes, [(i, i ^ flip) for i in range(count)])

    def struct(dims, kind=jnp.bfloat16):
        return jax.ShapeDtypeStruct(dims, kind)

    def along_line(value, order):
        return jnp.concatenate([value] + [swap(value, flip) for flip in order], axis=0)

    smem = pl.BlockSpec(memory_space=pltpu.SMEM)
    vmem = pl.BlockSpec(memory_space=pltpu.VMEM)
    sums = [struct((1, embed), jnp.float32), struct((1, LANES), jnp.float32)]
    extra = pltpu.VMEM((rows, LANES), jnp.float32)

    keep, send, column_sum, sum_row = kernel_call(
        functools.partial(project_body, rows, mp_count),
        [struct((half, embed), jnp.float32), struct((half, embed + LANES))] + sums,
        scratch=[extra],
        in_specs=[smem, vmem, vmem],
        flops=2 * local_rows * width * embed,
        name="project",
    )(place, features, proj_weight)
    own, send, column_sum, sum_row = kernel_call(
        functools.partial(chip_body, width, mp_count),
        [struct((rows, embed), jnp.float32), struct((rows, embed + LANES))] + sums,
        scratch=[extra],
        in_specs=[smem] + [vmem] * 4,
        name="chip_project",
    )(place, keep, swap(send, core), column_sum, sum_row)
    far, near = line[1], line[0]
    order = [0, far, near, far ^ near]
    plane = [0, across, column, column | across]
    unit_txt_b = kernel_call(texts_body, struct(texts.shape), name="unit_texts")(texts)
    txt_line = jnp.concatenate(
        [unit_txt_b] + [swap(unit_txt_b, flip) for flip in order[1:]], axis=0
    )
    send, txt_line = lax.optimization_barrier((send, txt_line))
    middle = local_rows // 2

    def diagonal(by_y, by_x):
        return jnp.concatenate(
            [swap(by_x[:middle], across), swap(by_y[middle:], column)], axis=0
        )

    txt_y, txt_x = swap(txt_line, across), swap(txt_line, column)
    txt_plane = [txt_line, txt_y, txt_x, diagonal(txt_y, txt_x)]

    project, mean, weight_sum = kernel_call(
        functools.partial(rows_body, full_width, mp_count),
        [
            struct((rows, embed)),
            struct((local_rows, 1), jnp.float32),
            struct((1, embed), jnp.float32),
        ],
        in_specs=[smem] + [vmem] * 4,
        name="project_rows",
    )(place, own, swap(send, across), column_sum, sum_row)
    normed_b = kernel_call(centre_body, struct(features.shape), name="centre")(features, mean)

    line_rows = jnp.concatenate([project, swap(project, far)], axis=0)
    line_rows = jnp.concatenate([line_rows, swap(line_rows, near)], axis=0)
    normed = jnp.concatenate([normed_b, swap(normed_b, column)], axis=0)
    normed_far = swap(normed, far)
    line_rows, normed_far, txt_plane[1], txt_plane[2] = lax.optimization_barrier(
        (line_rows, normed_far, txt_plane[1], txt_plane[2])
    )
    normed = jnp.concatenate([normed, normed_far], axis=0)
    normed_near = swap(normed, near)
    normed_order = sum([[o, o ^ column] for o in order], [])
    all_texts = [jnp.concatenate(txt_plane, axis=0)]
    all_texts.append(swap(all_texts[0], core))
    rows_y, rows_x = swap(line_rows, across), swap(line_rows, column)
    diagonal_rows = [swap(rows_x[:middle], across), swap(rows_y[middle:], column)]
    plane_rows = [line_rows, rows_y, rows_x]

    def gradient(index):
        return kernel_call(
            functools.partial(grad_body, index * local_rows),
            struct(line_rows.shape),
            flops=0,
            name="grad",
        )(plane_rows[index], *all_texts)

    grads = [gradient(0)]
    others = [swap(grads[0], core)]
    plane_rows[1], _ = lax.optimization_barrier((plane_rows[1], grads[0]))
    grads.append(gradient(1))
    others.append(swap(grads[1], core))
    normed = jnp.concatenate([normed, normed_near], axis=0)

    def add_product(indices, previous, final=False):
        arrays = sum([[grads[i], others[i]] for i in indices], [])
        orders = [[o ^ plane[i] for o in order] for i in indices]
        tiles = 3 if final else 1
        scratch = [
            pltpu.VMEM(proj_weight.shape, jnp.float32),
            pltpu.SemaphoreType.DMA((tiles,)),
        ]
        return kernel_call(
            functools.partial(weight_body, rows, mp_count, normed_order, orders, tiles),
            struct(proj_weight.shape, jnp.float32),
            scratch=scratch if final else (),
            in_specs=[smem] + [vmem] * (1 + len(arrays) + len(previous)),
            out_specs=pl.BlockSpec(memory_space=pl.ANY) if final else vmem,
            flops=0 * 4 * width * embed * local_rows * len(indices),
            name="weight",
        )(place, normed, *arrays, *previous)

    grad_features = kernel_call(
        functools.partial(features_body, full_width, rows, mp_count),
        struct(features.shape),
        scratch=[pltpu.VMEM((local_rows, embed), jnp.bfloat16)],
        in_specs=[smem] + [vmem] * (2 + mp_count),
        flops=0 * 2 * local_rows * width * embed,
        name="grad_features",
    )(place, proj_weight, weight_sum, grads[0], others[0], grads[1], others[1])
    first = [0]
    grad_weight = add_product(first, [])
    grads.append(gradient(2))
    others.append(swap(grads[2], core))
    *diagonal_rows, _, _, _ = lax.optimization_barrier(
        (*diagonal_rows, grads[2], grad_weight, grad_features)
    )
    plane_rows.append(jnp.concatenate(diagonal_rows, axis=0))
    grads.append(gradient(3))
    others.append(swap(grads[3], core))
    grad_weight = add_product([1, 2], [grad_weight])
    grad_weight = add_product([3], [grad_weight], True)
    return grad_features, grad_weight


def shards(features, proj_weight, texts):
    dp_count, mp_count = lax.axis_size("dp"), lax.axis_size("mp")
    count = dp_count * mp_count
    rows = texts.shape[0]
    embed = texts.shape[1]
    fits = (
        count * rows * (embed + LANES) * 2 <= GATHER_BYTES
        and count & (count - 1) == 0
        and mp_count == 4
        and count == 8 * mp_count
        and features.shape[0] == LANES == mp_count * rows
        and embed % LANES == 0
        and 2 * (embed // LANES) + 3 <= rows
        and rows % 16 == 0
    )
    plan = shards_gathered if fits else shards_summed
    return plan(features, proj_weight, texts)


def solution(mesh):
    return jax.shard_map(
        shards,
        mesh=mesh,
        in_specs=(P("dp", "mp"), P("mp", None), P(("dp", "mp"), None)),
        out_specs=(P("dp", "mp"), P("mp", None)),
        check_vma=False,
    )
```

```python
import functools

import jax
import jax.numpy as jnp
from jax import lax
from jax.experimental import pallas as pl
from jax.experimental.pallas import tpu as pltpu
from jax.sharding import PartitionSpec as P

logit_scale = 100.0
logit_bias = -10.0
epsilon = 1e-06
LANES = 128
GATHER_BYTES = 8 << 20
VMEM_BYTES = 40 << 20


def unit_rows(values):
    return values * lax.rsqrt(jnp.sum(values * values, axis=1, keepdims=True) + epsilon)


def add_texts(unit_img_b, image_ids, piece, piece_ids):
    unit_txt_b = unit_rows(piece.astype(jnp.float32)).astype(jnp.bfloat16)
    logits = (
        logit_scale * jnp.dot(unit_img_b, unit_txt_b.T, preferred_element_type=jnp.float32)
        + logit_bias
    )
    labels = jnp.where(image_ids[:, None] == piece_ids[None, :], 1.0, -1.0).astype(jnp.float32)
    slopes = (-labels * jax.nn.sigmoid(-labels * logits)).astype(jnp.bfloat16)
    return logit_scale * jnp.dot(slopes, unit_txt_b, preferred_element_type=jnp.float32)


def shards_summed(features, proj_weight, texts):
    local_rows = features.shape[0]
    width_local = features.shape[1]
    mp_count = lax.axis_size("mp")
    full_width = width_local * mp_count
    mp_index = lax.axis_index("mp")
    dp_index = lax.axis_index("dp")
    text_rows = texts.shape[0]
    inputs = features.astype(jnp.float32)
    mean_in = lax.psum(jnp.sum(inputs, axis=1, keepdims=True), "mp") / full_width
    centred = inputs - mean_in
    normed_b = centred.astype(jnp.bfloat16)
    partial_proj = jnp.dot(normed_b, proj_weight, preferred_element_type=jnp.float32)
    project = lax.psum(partial_proj, "mp")
    inv_norm = lax.rsqrt(jnp.sum(project * project, axis=1, keepdims=True) + epsilon)
    unit_img = project * inv_norm
    unit_img_b = unit_img.astype(jnp.bfloat16)
    image_ids = dp_index * local_rows + jnp.arange(local_rows, dtype=jnp.int32)
    piece = lax.all_gather(texts, "dp", axis=0, tiled=True)
    positions = jnp.arange(piece.shape[0], dtype=jnp.int32)
    shard_of = positions // text_rows
    piece_ids = (shard_of * mp_count + mp_index) * text_rows + positions % text_rows
    grad_unit = add_texts(unit_img_b, image_ids, piece, piece_ids)
    grad_unit = lax.psum(grad_unit, "mp")
    grad_proj = inv_norm * (
        grad_unit - unit_img * jnp.sum(unit_img * grad_unit, axis=1, keepdims=True)
    )
    grad_proj_b = grad_proj.astype(jnp.bfloat16)
    weight_part = jnp.dot(normed_b.T, grad_proj_b, preferred_element_type=jnp.float32)
    grad_weight = lax.psum(weight_part, "dp")
    grad_normed = jnp.dot(grad_proj_b, proj_weight.T, preferred_element_type=jnp.float32)
    grad_total = lax.psum(jnp.sum(grad_normed, axis=1, keepdims=True), "mp")
    grad_in = grad_normed - grad_total / full_width
    return (grad_in.astype(jnp.bfloat16), grad_weight)


def split_terms(value, count):
    terms = []
    for _ in range(count):
        term = value.astype(jnp.bfloat16).astype(jnp.float32)
        terms.append(term)
        value = value - term
    return terms


def kernel_call(body, outs, scratch=(), flops=0, **names):
    return pl.pallas_call(
        body,
        out_shape=outs,
        scratch_shapes=scratch,
        compiler_params=pltpu.CompilerParams(vmem_limit_bytes=VMEM_BYTES),
        cost_estimate=pl.CostEstimate(flops=flops, bytes_accessed=0, transcendentals=0),
        **names,
    )


def texts_body(texts_ref, out_ref):
    out_ref[...] = unit_rows(texts_ref[...].astype(jnp.float32)).astype(jnp.bfloat16)


def store_sums(extra_ref, column_sum, sum_row):
    extra_ref[...] = jnp.zeros_like(extra_ref)
    at = 0
    for term in split_terms(column_sum, 2):
        for i in range(column_sum.shape[1] // LANES):
            extra_ref[at : at + 1, :] = term[:, i * LANES : (i + 1) * LANES]
            at += 1
    for term in split_terms(sum_row, 3):
        extra_ref[at : at + 1, :] = term
        at += 1
    return extra_ref[...].astype(jnp.bfloat16)


def load_sums(extra, embed):
    chunks = embed // LANES
    extra = extra.astype(jnp.float32)
    column_sum = jnp.concatenate(
        [extra[i : i + 1] + extra[chunks + i : chunks + i + 1] for i in range(chunks)], axis=1
    )
    at = 2 * chunks
    return column_sum, extra[at : at + 1] + extra[at + 1 : at + 2] + extra[at + 2 : at + 3]


def pick_rows(sum_row, rows, group):
    row = lax.broadcasted_iota(jnp.int32, (rows, LANES), 0)
    lane = lax.broadcasted_iota(jnp.int32, (rows, LANES), 1)
    return jnp.sum(jnp.where(lane == row + group * rows, sum_row, 0.0), axis=1, keepdims=True)


def project_body(
    rows, mp_count, place_ref, features_ref, weight_ref,
    keep_ref, send_ref, column_sum_ref, sum_row_ref, extra_ref,
):
    embed = weight_ref.shape[1]
    local_rows, width = features_ref.shape
    values = features_ref[...].astype(jnp.float32)
    row_sum = jnp.sum(values, axis=1, keepdims=True)
    column_sum = jnp.sum(weight_ref[...].astype(jnp.float32), axis=0, keepdims=True)
    row = lax.broadcasted_iota(jnp.int32, (local_rows, LANES), 0)
    lane = lax.broadcasted_iota(jnp.int32, (local_rows, LANES), 1)
    sum_row = jnp.sum(jnp.where(row == lane, row_sum, 0.0), axis=0, keepdims=True)
    ordered = []
    for flip in list(range(0, mp_count, 2)) + list(range(1, mp_count, 2)):
        start = pl.multiple_of(((place_ref[0] ^ flip) & (mp_count - 1)) * rows, rows)
        block = features_ref[pl.ds(start, rows), :].astype(jnp.float32)
        ordered.append(block - jnp.sum(block, axis=1, keepdims=True) / width)
    centred = jnp.concatenate(ordered, axis=0).astype(jnp.bfloat16)
    product = jnp.dot(centred, weight_ref[...], preferred_element_type=jnp.float32)
    half = local_rows // 2
    keep_ref[...] = product[:half]
    send_ref[:, :embed] = product[half:].astype(jnp.bfloat16)
    extra = store_sums(extra_ref, column_sum, sum_row)
    for i in range(half // rows):
        send_ref[i * rows : (i + 1) * rows, embed:] = extra
    column_sum_ref[...] = column_sum
    sum_row_ref[...] = sum_row


def chip_body(
    width, mp_count, place_ref, keep_ref, received_ref, column_sum_ref, sum_row_ref,
    own_ref, send_ref, chip_column_ref, chip_row_ref, extra_ref,
):
    rows = own_ref.shape[0]
    embed = own_ref.shape[1]
    columns = [column_sum_ref[...], None]
    sum_rows = [sum_row_ref[...], None]
    columns[1], sum_rows[1] = load_sums(received_ref[:rows, embed:], embed)
    chip_column = columns[0] + columns[1]
    chip_row = sum_rows[0] + sum_rows[1]
    for i in range(2):
        group = (place_ref[0] ^ (2 * i)) & (mp_count - 1)
        mean = pick_rows(chip_row, rows, group) / (2 * width)
        here = slice(i * rows, (i + 1) * rows)
        total = keep_ref[here, :] + received_ref[here, :embed].astype(jnp.float32)
        for column, sum_row in zip(columns, sum_rows):
            total = total + (pick_rows(sum_row, rows, group) / width - mean) * column
        if i == 0:
            own_ref[...] = total
        else:
            send_ref[:, :embed] = total.astype(jnp.bfloat16)
    send_ref[:, embed:] = store_sums(extra_ref, chip_column, chip_row)
    chip_column_ref[...] = chip_column
    chip_row_ref[...] = chip_row


def rows_body(
    full_width, mp_count, place_ref, own_ref, received_ref, column_sum_ref, sum_row_ref,
    project_ref, weight_sum_ref,
):
    rows, embed = own_ref.shape
    columns = [column_sum_ref[...], None]
    sum_rows = [sum_row_ref[...], None]
    columns[1], sum_rows[1] = load_sums(received_ref[:, embed:], embed)
    group = place_ref[0] & (mp_count - 1)
    mean = pick_rows(sum_rows[0] + sum_rows[1], rows, group) / full_width
    project = own_ref[...] + received_ref[:, :embed].astype(jnp.float32)
    for column, sum_row in zip(columns, sum_rows):
        part_mean = pick_rows(sum_row, rows, group) / (full_width // 2)
        project = project + (part_mean - mean) * column
    project_ref[:, :embed] = project.astype(jnp.bfloat16)
    lane = lax.broadcasted_iota(jnp.int32, (rows, LANES), 1)
    extra = jnp.zeros((rows, LANES), jnp.float32)
    for i, term in enumerate(split_terms(mean, 3)):
        extra = jnp.where(lane == i, term, extra)
    project_ref[:, embed:] = extra.astype(jnp.bfloat16)
    weight_sum_ref[...] = columns[0] + columns[1]


def grad_body(first, project_ref, *refs):
    (*texts, out_ref) = refs
    embed = texts[0].shape[1]
    project = project_ref[:, :embed].astype(jnp.float32)
    inv_norm = lax.rsqrt(jnp.sum(project * project, axis=1, keepdims=True) + epsilon)
    unit_img = project * inv_norm
    unit_img_b = unit_img.astype(jnp.bfloat16)
    grad_unit = jnp.zeros_like(project)
    at = 0
    for ref in texts:
        unit_txt_b = ref[...]
        logits = (
            logit_scale
            * lax.dot_general(
                unit_img_b,
                unit_txt_b,
                (((1,), (1,)), ((), ())),
                preferred_element_type=jnp.float32,
            )
            + logit_bias
        )
        text = lax.broadcasted_iota(jnp.int32, logits.shape, 1) + at
        image = lax.broadcasted_iota(jnp.int32, logits.shape, 0) + first
        labels = jnp.where(text == image, 1.0, -1.0)
        slopes = (-labels / (1.0 + jnp.exp(labels * logits))).astype(jnp.bfloat16)
        grad_unit = grad_unit + jnp.dot(slopes, unit_txt_b, preferred_element_type=jnp.float32)
        at += unit_txt_b.shape[0]
    grad_unit = logit_scale * grad_unit
    grad_proj = inv_norm * (
        grad_unit - unit_img * jnp.sum(unit_img * grad_unit, axis=1, keepdims=True)
    )
    out_ref[:, :embed] = grad_proj.astype(jnp.bfloat16)
    out_ref[:, embed:] = project_ref[:, embed:]


def weight_body(
    rows, mp_count, gather_order, orders, tiles, place_ref, features_ref, *refs
):
    count = 2 * len(orders)
    arrays = refs[:count]
    previous = refs[count : count + 1] if len(refs) - count > (1 if tiles == 1 else 3) else ()
    outs = refs[count + len(previous) :]
    embed = outs[0].shape[1]
    blocks = []
    for at, order in enumerate(orders):
        for i in range(2):
            extra = arrays[2 * at + i][:, embed:].astype(jnp.float32)
            mean = extra[:, 0:1] + extra[:, 1:2] + extra[:, 2:3]
            for k, flip in enumerate(order):
                group = (place_ref[0] ^ flip ^ i) & (mp_count - 1)
                start = (gather_order.index(flip - flip % mp_count) * mp_count + group) * rows
                block = features_ref[pl.ds(pl.multiple_of(start, rows), rows), :]
                blocks.append(block.astype(jnp.float32) - mean[k * rows : (k + 1) * rows])
    normed = jnp.concatenate(blocks, axis=0).astype(jnp.bfloat16)
    gradient = jnp.concatenate([array[:, :embed] for array in arrays], axis=0)
    if tiles == 1:
        total = lax.dot_general(
            normed, gradient, (((0,), (0,)), ((), ())), preferred_element_type=jnp.float32
        )
        for ref in previous:
            total = total + ref[...]
        outs[0][...] = total
        return
    out_hbm, total_ref, sent = outs
    wide = gradient.shape[1] // tiles
    copies = []
    for k in range(tiles):
        here = slice(k * wide, (k + 1) * wide)
        total = lax.dot_general(
            normed, gradient[:, here], (((0,), (0,)), ((), ())), preferred_element_type=jnp.float32
        )
        for ref in previous:
            total = total + ref[:, here]
        total_ref[:, here] = total
        copies.append(
            pltpu.make_async_copy(total_ref.at[:, here], out_hbm.at[:, here], sent.at[k])
        )
        copies[-1].start()
    for copy in copies:
        copy.wait()


def features_body(full_width, rows, mp_count, place_ref, weight_ref, weight_sum_ref, *refs):
    (*parts, out_ref, group_ref) = refs
    for flip, part in enumerate(parts):
        start = pl.multiple_of(((place_ref[0] ^ flip) & (mp_count - 1)) * rows, rows)
        group_ref[pl.ds(start, rows), :] = part[:rows, : group_ref.shape[1]]
    group = group_ref[...]
    grad_normed = lax.dot_general(
        group, weight_ref[...], (((1,), (1,)), ((), ())), preferred_element_type=jnp.float32
    )
    grad_total = jnp.sum(group.astype(jnp.float32) * weight_sum_ref[...], axis=1, keepdims=True)
    out_ref[...] = (grad_normed - grad_total / full_width).astype(jnp.bfloat16)


def shards_gathered(features, proj_weight, texts):
    axes = ("dp", "mp")
    dp_count, mp_count = lax.axis_size("dp"), lax.axis_size("mp")
    count = dp_count * mp_count
    plane_count = 2 * mp_count
    local_rows, width = features.shape
    embed = proj_weight.shape[1]
    rows = texts.shape[0]
    half = local_rows // 2
    full_width = width * mp_count
    place = (lax.axis_index("dp") * mp_count + lax.axis_index("mp")).astype(jnp.int32).reshape(1)
    core, across, column = 1, 2, mp_count
    line = list(range(plane_count, count, plane_count))

    def swap(value, flip):
        return lax.ppermute(value, axes, [(i, i ^ flip) for i in range(count)])

    def struct(dims, kind=jnp.bfloat16):
        return jax.ShapeDtypeStruct(dims, kind)

    def along_line(value, order):
        return jnp.concatenate([value] + [swap(value, flip) for flip in order], axis=0)

    smem = pl.BlockSpec(memory_space=pltpu.SMEM)
    vmem = pl.BlockSpec(memory_space=pltpu.VMEM)
    sums = [struct((1, embed), jnp.float32), struct((1, LANES), jnp.float32)]
    extra = pltpu.VMEM((rows, LANES), jnp.float32)

    keep, send, column_sum, sum_row = kernel_call(
        functools.partial(project_body, rows, mp_count),
        [struct((half, embed), jnp.float32), struct((half, embed + LANES))] + sums,
        scratch=[extra],
        in_specs=[smem, vmem, vmem],
        flops=2 * local_rows * width * embed,
        name="project",
    )(place, features, proj_weight)
    own, send, column_sum, sum_row = kernel_call(
        functools.partial(chip_body, width, mp_count),
        [struct((rows, embed), jnp.float32), struct((rows, embed + LANES))] + sums,
        scratch=[extra],
        in_specs=[smem] + [vmem] * 4,
        name="chip_project",
    )(place, keep, swap(send, core), column_sum, sum_row)
    far, near = line[1], line[0]
    order = [0, far, near, far ^ near]
    plane = [0, across, column, column | across]
    unit_txt_b = kernel_call(texts_body, struct(texts.shape), name="unit_texts")(texts)
    txt_line = jnp.concatenate(
        [unit_txt_b] + [swap(unit_txt_b, flip) for flip in order[1:]], axis=0
    )
    features_x = swap(features, column)
    send, features_x = lax.optimization_barrier((send, features_x))
    send, txt_line = lax.optimization_barrier((send, txt_line))
    middle = local_rows // 2

    def diagonal(by_y, by_x):
        return jnp.concatenate(
            [swap(by_x[:middle], across), swap(by_y[middle:], column)], axis=0
        )

    txt_y, txt_x = swap(txt_line, across), swap(txt_line, column)
    txt_plane = [txt_line, txt_y, txt_x, diagonal(txt_y, txt_x)]

    project, weight_sum = kernel_call(
        functools.partial(rows_body, full_width, mp_count),
        [
            struct((rows, embed + LANES)),
            struct((1, embed), jnp.float32),
        ],
        in_specs=[smem] + [vmem] * 4,
        name="project_rows",
    )(place, own, swap(send, across), column_sum, sum_row)

    line_rows = jnp.concatenate([project, swap(project, far)], axis=0)
    line_rows = jnp.concatenate([line_rows, swap(line_rows, near)], axis=0)
    gathered = jnp.concatenate([features, features_x], axis=0)
    features_far = swap(gathered, far)
    line_rows, features_far, txt_plane[1], txt_plane[2] = lax.optimization_barrier(
        (line_rows, features_far, txt_plane[1], txt_plane[2])
    )
    gathered = jnp.concatenate([gathered, features_far], axis=0)
    features_near = swap(gathered, near)
    gather_order = sum([[o, o ^ column] for o in order], [])
    all_texts = [jnp.concatenate(txt_plane, axis=0)]
    all_texts.append(swap(all_texts[0], core))
    rows_y, rows_x = swap(line_rows, across), swap(line_rows, column)
    diagonal_rows = [swap(rows_x[:middle], across), swap(rows_y[middle:], column)]
    plane_rows = [line_rows, rows_y, rows_x]

    def gradient(index):
        return kernel_call(
            functools.partial(grad_body, index * local_rows),
            struct(line_rows.shape),
            flops=0,
            name="grad",
        )(plane_rows[index], *all_texts)

    grads = [gradient(0)]
    others = [swap(grads[0], core)]
    plane_rows[1], _ = lax.optimization_barrier((plane_rows[1], grads[0]))
    grads.append(gradient(1))
    others.append(swap(grads[1], core))
    gathered = jnp.concatenate([gathered, features_near], axis=0)

    def add_product(indices, previous, final=False):
        arrays = sum([[grads[i], others[i]] for i in indices], [])
        orders = [[o ^ plane[i] for o in order] for i in indices]
        tiles = 3 if final else 1
        scratch = [
            pltpu.VMEM(proj_weight.shape, jnp.float32),
            pltpu.SemaphoreType.DMA((tiles,)),
        ]
        return kernel_call(
            functools.partial(weight_body, rows, mp_count, gather_order, orders, tiles),
            struct(proj_weight.shape, jnp.float32),
            scratch=scratch if final else (),
            in_specs=[smem] + [vmem] * (1 + len(arrays) + len(previous)),
            out_specs=pl.BlockSpec(memory_space=pl.ANY) if final else vmem,
            flops=0 * 4 * width * embed * local_rows * len(indices),
            name="weight",
        )(place, gathered, *arrays, *previous)

    grad_features = kernel_call(
        functools.partial(features_body, full_width, rows, mp_count),
        struct(features.shape),
        scratch=[pltpu.VMEM((local_rows, embed), jnp.bfloat16)],
        in_specs=[smem] + [vmem] * (2 + mp_count),
        flops=0 * 2 * local_rows * width * embed,
        name="grad_features",
    )(place, proj_weight, weight_sum, grads[0], others[0], grads[1], others[1])
    first = [0, 1]
    grad_weight = add_product(first, [])
    grads.append(gradient(2))
    others.append(swap(grads[2], core))
    *diagonal_rows, _, _, _ = lax.optimization_barrier(
        (*diagonal_rows, grads[2], grad_weight, grad_features)
    )
    plane_rows.append(jnp.concatenate(diagonal_rows, axis=0))
    grads.append(gradient(3))
    others.append(swap(grads[3], core))
    grad_weight = add_product([2], [grad_weight])
    grad_weight = add_product([3], [grad_weight], True)
    return grad_features, grad_weight


def shards(features, proj_weight, texts):
    dp_count, mp_count = lax.axis_size("dp"), lax.axis_size("mp")
    count = dp_count * mp_count
    rows = texts.shape[0]
    embed = texts.shape[1]
    fits = (
        count * rows * (embed + LANES) * 2 <= GATHER_BYTES
        and count & (count - 1) == 0
        and mp_count == 4
        and count == 8 * mp_count
        and features.shape[0] == LANES == mp_count * rows
        and embed % LANES == 0
        and 2 * (embed // LANES) + 3 <= rows
        and rows % 16 == 0
    )
    plan = shards_gathered if fits else shards_summed
    return plan(features, proj_weight, texts)


def solution(mesh):
    return jax.shard_map(
        shards,
        mesh=mesh,
        in_specs=(P("dp", "mp"), P("mp", None), P(("dp", "mp"), None)),
        out_specs=(P("dp", "mp"), P("mp", None)),
        check_vma=False,
    )
```

```python
import functools

import jax
import jax.numpy as jnp
from jax import lax
from jax.experimental import pallas as pl
from jax.experimental.pallas import tpu as pltpu
from jax.sharding import PartitionSpec as P

logit_scale = 100.0
logit_bias = -10.0
epsilon = 1e-06
LANES = 128
GATHER_BYTES = 8 << 20
VMEM_BYTES = 40 << 20


def unit_rows(values):
    return values * lax.rsqrt(jnp.sum(values * values, axis=1, keepdims=True) + epsilon)


def add_texts(unit_img_b, image_ids, piece, piece_ids):
    unit_txt_b = unit_rows(piece.astype(jnp.float32)).astype(jnp.bfloat16)
    logits = (
        logit_scale * jnp.dot(unit_img_b, unit_txt_b.T, preferred_element_type=jnp.float32)
        + logit_bias
    )
    labels = jnp.where(image_ids[:, None] == piece_ids[None, :], 1.0, -1.0).astype(jnp.float32)
    slopes = (-labels * jax.nn.sigmoid(-labels * logits)).astype(jnp.bfloat16)
    return logit_scale * jnp.dot(slopes, unit_txt_b, preferred_element_type=jnp.float32)


def shards_summed(features, proj_weight, texts):
    local_rows = features.shape[0]
    width_local = features.shape[1]
    mp_count = lax.axis_size("mp")
    full_width = width_local * mp_count
    mp_index = lax.axis_index("mp")
    dp_index = lax.axis_index("dp")
    text_rows = texts.shape[0]
    inputs = features.astype(jnp.float32)
    mean_in = lax.psum(jnp.sum(inputs, axis=1, keepdims=True), "mp") / full_width
    centred = inputs - mean_in
    normed_b = centred.astype(jnp.bfloat16)
    partial_proj = jnp.dot(normed_b, proj_weight, preferred_element_type=jnp.float32)
    project = lax.psum(partial_proj, "mp")
    inv_norm = lax.rsqrt(jnp.sum(project * project, axis=1, keepdims=True) + epsilon)
    unit_img = project * inv_norm
    unit_img_b = unit_img.astype(jnp.bfloat16)
    image_ids = dp_index * local_rows + jnp.arange(local_rows, dtype=jnp.int32)
    piece = lax.all_gather(texts, "dp", axis=0, tiled=True)
    positions = jnp.arange(piece.shape[0], dtype=jnp.int32)
    shard_of = positions // text_rows
    piece_ids = (shard_of * mp_count + mp_index) * text_rows + positions % text_rows
    grad_unit = add_texts(unit_img_b, image_ids, piece, piece_ids)
    grad_unit = lax.psum(grad_unit, "mp")
    grad_proj = inv_norm * (
        grad_unit - unit_img * jnp.sum(unit_img * grad_unit, axis=1, keepdims=True)
    )
    grad_proj_b = grad_proj.astype(jnp.bfloat16)
    weight_part = jnp.dot(normed_b.T, grad_proj_b, preferred_element_type=jnp.float32)
    grad_weight = lax.psum(weight_part, "dp")
    grad_normed = jnp.dot(grad_proj_b, proj_weight.T, preferred_element_type=jnp.float32)
    grad_total = lax.psum(jnp.sum(grad_normed, axis=1, keepdims=True), "mp")
    grad_in = grad_normed - grad_total / full_width
    return (grad_in.astype(jnp.bfloat16), grad_weight)


def split_terms(value, count):
    terms = []
    for _ in range(count):
        term = value.astype(jnp.bfloat16).astype(jnp.float32)
        terms.append(term)
        value = value - term
    return terms


def kernel_call(body, outs, scratch=(), flops=0, **names):
    return pl.pallas_call(
        body,
        out_shape=outs,
        scratch_shapes=scratch,
        compiler_params=pltpu.CompilerParams(vmem_limit_bytes=VMEM_BYTES),
        cost_estimate=pl.CostEstimate(flops=flops, bytes_accessed=0, transcendentals=0),
        **names,
    )


def texts_body(texts_ref, out_ref):
    out_ref[...] = unit_rows(texts_ref[...].astype(jnp.float32)).astype(jnp.bfloat16)


def store_sums(extra_ref, column_sum, sum_row):
    extra_ref[...] = jnp.zeros_like(extra_ref)
    at = 0
    for term in split_terms(column_sum, 2):
        for i in range(column_sum.shape[1] // LANES):
            extra_ref[at : at + 1, :] = term[:, i * LANES : (i + 1) * LANES]
            at += 1
    for term in split_terms(sum_row, 3):
        extra_ref[at : at + 1, :] = term
        at += 1
    return extra_ref[...].astype(jnp.bfloat16)


def load_sums(extra, embed):
    chunks = embed // LANES
    extra = extra.astype(jnp.float32)
    column_sum = jnp.concatenate(
        [extra[i : i + 1] + extra[chunks + i : chunks + i + 1] for i in range(chunks)], axis=1
    )
    at = 2 * chunks
    return column_sum, extra[at : at + 1] + extra[at + 1 : at + 2] + extra[at + 2 : at + 3]


def pick_rows(sum_row, rows, group):
    row = lax.broadcasted_iota(jnp.int32, (rows, LANES), 0)
    lane = lax.broadcasted_iota(jnp.int32, (rows, LANES), 1)
    return jnp.sum(jnp.where(lane == row + group * rows, sum_row, 0.0), axis=1, keepdims=True)


def project_body(
    rows, mp_count, place_ref, features_ref, weight_ref,
    keep_ref, send_ref, column_sum_ref, sum_row_ref, extra_ref,
):
    embed = weight_ref.shape[1]
    local_rows, width = features_ref.shape
    values = features_ref[...].astype(jnp.float32)
    row_sum = jnp.sum(values, axis=1, keepdims=True)
    column_sum = jnp.sum(weight_ref[...].astype(jnp.float32), axis=0, keepdims=True)
    row = lax.broadcasted_iota(jnp.int32, (local_rows, LANES), 0)
    lane = lax.broadcasted_iota(jnp.int32, (local_rows, LANES), 1)
    sum_row = jnp.sum(jnp.where(row == lane, row_sum, 0.0), axis=0, keepdims=True)
    ordered = []
    for flip in list(range(0, mp_count, 2)) + list(range(1, mp_count, 2)):
        start = pl.multiple_of(((place_ref[0] ^ flip) & (mp_count - 1)) * rows, rows)
        block = features_ref[pl.ds(start, rows), :].astype(jnp.float32)
        ordered.append(block - jnp.sum(block, axis=1, keepdims=True) / width)
    centred = jnp.concatenate(ordered, axis=0).astype(jnp.bfloat16)
    product = jnp.dot(centred, weight_ref[...], preferred_element_type=jnp.float32)
    half = local_rows // 2
    keep_ref[...] = product[:half]
    send_ref[:, :embed] = product[half:].astype(jnp.bfloat16)
    extra = store_sums(extra_ref, column_sum, sum_row)
    for i in range(half // rows):
        send_ref[i * rows : (i + 1) * rows, embed:] = extra
    column_sum_ref[...] = column_sum
    sum_row_ref[...] = sum_row


def chip_body(
    width, mp_count, place_ref, keep_ref, received_ref, column_sum_ref, sum_row_ref,
    own_ref, send_ref, chip_column_ref, chip_row_ref, extra_ref,
):
    rows = own_ref.shape[0]
    embed = own_ref.shape[1]
    columns = [column_sum_ref[...], None]
    sum_rows = [sum_row_ref[...], None]
    columns[1], sum_rows[1] = load_sums(received_ref[:rows, embed:], embed)
    chip_column = columns[0] + columns[1]
    chip_row = sum_rows[0] + sum_rows[1]
    for i in range(2):
        group = (place_ref[0] ^ (2 * i)) & (mp_count - 1)
        mean = pick_rows(chip_row, rows, group) / (2 * width)
        here = slice(i * rows, (i + 1) * rows)
        total = keep_ref[here, :] + received_ref[here, :embed].astype(jnp.float32)
        for column, sum_row in zip(columns, sum_rows):
            total = total + (pick_rows(sum_row, rows, group) / width - mean) * column
        if i == 0:
            own_ref[...] = total
        else:
            send_ref[:, :embed] = total.astype(jnp.bfloat16)
    send_ref[:, embed:] = store_sums(extra_ref, chip_column, chip_row)
    chip_column_ref[...] = chip_column
    chip_row_ref[...] = chip_row


def rows_body(
    full_width, mp_count, place_ref, own_ref, received_ref, column_sum_ref, sum_row_ref,
    project_ref, weight_sum_ref,
):
    rows, embed = own_ref.shape
    columns = [column_sum_ref[...], None]
    sum_rows = [sum_row_ref[...], None]
    columns[1], sum_rows[1] = load_sums(received_ref[:, embed:], embed)
    group = place_ref[0] & (mp_count - 1)
    mean = pick_rows(sum_rows[0] + sum_rows[1], rows, group) / full_width
    project = own_ref[...] + received_ref[:, :embed].astype(jnp.float32)
    for column, sum_row in zip(columns, sum_rows):
        part_mean = pick_rows(sum_row, rows, group) / (full_width // 2)
        project = project + (part_mean - mean) * column
    project_ref[:, :embed] = project.astype(jnp.bfloat16)
    lane = lax.broadcasted_iota(jnp.int32, (rows, LANES), 1)
    extra = jnp.zeros((rows, LANES), jnp.float32)
    for i, term in enumerate(split_terms(mean, 3)):
        extra = jnp.where(lane == i, term, extra)
    project_ref[:, embed:] = extra.astype(jnp.bfloat16)
    weight_sum_ref[...] = columns[0] + columns[1]


def grad_body(first, project_ref, *refs):
    (*texts, out_ref) = refs
    embed = texts[0].shape[1]
    project = project_ref[:, :embed].astype(jnp.float32)
    inv_norm = lax.rsqrt(jnp.sum(project * project, axis=1, keepdims=True) + epsilon)
    unit_img = project * inv_norm
    unit_img_b = unit_img.astype(jnp.bfloat16)
    grad_unit = jnp.zeros_like(project)
    at = 0
    for ref in texts:
        unit_txt_b = ref[...]
        logits = (
            logit_scale
            * lax.dot_general(
                unit_img_b,
                unit_txt_b,
                (((1,), (1,)), ((), ())),
                preferred_element_type=jnp.float32,
            )
            + logit_bias
        )
        text = lax.broadcasted_iota(jnp.int32, logits.shape, 1) + at
        image = lax.broadcasted_iota(jnp.int32, logits.shape, 0) + first
        labels = jnp.where(text == image, 1.0, -1.0)
        slopes = (-labels / (1.0 + jnp.exp(labels * logits))).astype(jnp.bfloat16)
        grad_unit = grad_unit + jnp.dot(slopes, unit_txt_b, preferred_element_type=jnp.float32)
        at += unit_txt_b.shape[0]
    grad_unit = logit_scale * grad_unit
    grad_proj = inv_norm * (
        grad_unit - unit_img * jnp.sum(unit_img * grad_unit, axis=1, keepdims=True)
    )
    out_ref[:, :embed] = grad_proj.astype(jnp.bfloat16)
    out_ref[:, embed:] = project_ref[:, embed:]


def weight_body(
    rows, mp_count, gather_order, orders, tiles, place_ref, features_ref, *refs
):
    count = 2 * len(orders)
    arrays = refs[:count]
    previous = refs[count : count + 1] if len(refs) - count > (1 if tiles == 1 else 3) else ()
    outs = refs[count + len(previous) :]
    embed = outs[0].shape[1]
    blocks = []
    for at, order in enumerate(orders):
        for i in range(2):
            extra = arrays[2 * at + i][:, embed:].astype(jnp.float32)
            mean = extra[:, 0:1] + extra[:, 1:2] + extra[:, 2:3]
            for k, flip in enumerate(order):
                group = (place_ref[0] ^ flip ^ i) & (mp_count - 1)
                start = (gather_order.index(flip - flip % mp_count) * mp_count + group) * rows
                block = features_ref[pl.ds(pl.multiple_of(start, rows), rows), :]
                blocks.append(block.astype(jnp.float32) - mean[k * rows : (k + 1) * rows])
    normed = jnp.concatenate(blocks, axis=0).astype(jnp.bfloat16)
    gradient = jnp.concatenate([array[:, :embed] for array in arrays], axis=0)
    if tiles == 1:
        total = lax.dot_general(
            normed, gradient, (((0,), (0,)), ((), ())), preferred_element_type=jnp.float32
        )
        for ref in previous:
            total = total + ref[...]
        outs[0][...] = total
        return
    out_hbm, total_ref, sent = outs
    wide = gradient.shape[1] // tiles
    copies = []
    for k in range(tiles):
        here = slice(k * wide, (k + 1) * wide)
        total = lax.dot_general(
            normed, gradient[:, here], (((0,), (0,)), ((), ())), preferred_element_type=jnp.float32
        )
        for ref in previous:
            total = total + ref[:, here]
        total_ref[:, here] = total
        copies.append(
            pltpu.make_async_copy(total_ref.at[:, here], out_hbm.at[:, here], sent.at[k])
        )
        copies[-1].start()
    for copy in copies:
        copy.wait()


def features_body(full_width, rows, mp_count, place_ref, weight_ref, weight_sum_ref, *refs):
    (*parts, out_ref, group_ref) = refs
    for flip, part in enumerate(parts):
        start = pl.multiple_of(((place_ref[0] ^ flip) & (mp_count - 1)) * rows, rows)
        group_ref[pl.ds(start, rows), :] = part[:rows, : group_ref.shape[1]]
    group = group_ref[...]
    grad_normed = lax.dot_general(
        group, weight_ref[...], (((1,), (1,)), ((), ())), preferred_element_type=jnp.float32
    )
    grad_total = jnp.sum(group.astype(jnp.float32) * weight_sum_ref[...], axis=1, keepdims=True)
    out_ref[...] = (grad_normed - grad_total / full_width).astype(jnp.bfloat16)


def shards_gathered(features, proj_weight, texts):
    axes = ("dp", "mp")
    dp_count, mp_count = lax.axis_size("dp"), lax.axis_size("mp")
    count = dp_count * mp_count
    plane_count = 2 * mp_count
    local_rows, width = features.shape
    embed = proj_weight.shape[1]
    rows = texts.shape[0]
    half = local_rows // 2
    full_width = width * mp_count
    place = (lax.axis_index("dp") * mp_count + lax.axis_index("mp")).astype(jnp.int32).reshape(1)
    core, across, column = 1, 2, mp_count
    line = list(range(plane_count, count, plane_count))

    def swap(value, flip):
        return lax.ppermute(value, axes, [(i, i ^ flip) for i in range(count)])

    def struct(dims, kind=jnp.bfloat16):
        return jax.ShapeDtypeStruct(dims, kind)

    def along_line(value, order):
        return jnp.concatenate([value] + [swap(value, flip) for flip in order], axis=0)

    smem = pl.BlockSpec(memory_space=pltpu.SMEM)
    vmem = pl.BlockSpec(memory_space=pltpu.VMEM)
    sums = [struct((1, embed), jnp.float32), struct((1, LANES), jnp.float32)]
    extra = pltpu.VMEM((rows, LANES), jnp.float32)

    keep, send, column_sum, sum_row = kernel_call(
        functools.partial(project_body, rows, mp_count),
        [struct((half, embed), jnp.float32), struct((half, embed + LANES))] + sums,
        scratch=[extra],
        in_specs=[smem, vmem, vmem],
        flops=2 * local_rows * width * embed,
        name="project",
    )(place, features, proj_weight)
    own, send, column_sum, sum_row = kernel_call(
        functools.partial(chip_body, width, mp_count),
        [struct((rows, embed), jnp.float32), struct((rows, embed + LANES))] + sums,
        scratch=[extra],
        in_specs=[smem] + [vmem] * 4,
        name="chip_project",
    )(place, keep, swap(send, core), column_sum, sum_row)
    far, near = line[1], line[0]
    order = [0, far, near, far ^ near]
    plane = [0, across, column, column | across]
    unit_txt_b = kernel_call(texts_body, struct(texts.shape), name="unit_texts")(texts)
    txt_line = jnp.concatenate(
        [unit_txt_b] + [swap(unit_txt_b, flip) for flip in order[1:]], axis=0
    )
    features_x = swap(features, column)
    send, features_x = lax.optimization_barrier((send, features_x))
    send, txt_line = lax.optimization_barrier((send, txt_line))
    middle = local_rows // 2

    def diagonal(by_y, by_x):
        return jnp.concatenate(
            [swap(by_x[:middle], across), swap(by_y[middle:], column)], axis=0
        )

    txt_y, txt_x = swap(txt_line, across), swap(txt_line, column)
    txt_plane = [txt_line, txt_y, txt_x, diagonal(txt_y, txt_x)]

    project, weight_sum = kernel_call(
        functools.partial(rows_body, full_width, mp_count),
        [
            struct((rows, embed + LANES)),
            struct((1, embed), jnp.float32),
        ],
        in_specs=[smem] + [vmem] * 4,
        name="project_rows",
    )(place, own, swap(send, across), column_sum, sum_row)

    gathered = jnp.concatenate([features, features_x], axis=0)
    far_rows = swap(project, far)
    far_rows, gathered = lax.optimization_barrier((far_rows, gathered))
    line_rows = jnp.concatenate([project, far_rows], axis=0)
    line_rows = jnp.concatenate([line_rows, swap(line_rows, near)], axis=0)
    features_far = swap(gathered, far)
    line_rows, features_far, txt_plane[1], txt_plane[2] = lax.optimization_barrier(
        (line_rows, features_far, txt_plane[1], txt_plane[2])
    )
    gathered = jnp.concatenate([gathered, features_far], axis=0)
    features_near = swap(gathered, near)
    gather_order = sum([[o, o ^ column] for o in order], [])
    all_texts = [jnp.concatenate(txt_plane, axis=0)]
    all_texts.append(swap(all_texts[0], core))
    rows_y, rows_x = swap(line_rows, across), swap(line_rows, column)
    diagonal_rows = [swap(rows_x[:middle], across), swap(rows_y[middle:], column)]
    plane_rows = [line_rows, rows_y, rows_x]

    def gradient(index):
        return kernel_call(
            functools.partial(grad_body, index * local_rows),
            struct(line_rows.shape),
            flops=4 * local_rows * count * rows * embed,
            name="grad",
        )(plane_rows[index], *all_texts)

    grads = [gradient(0)]
    others = [swap(grads[0], core)]
    grads.append(gradient(1))
    others.append(swap(grads[1], core))
    gathered = jnp.concatenate([gathered, features_near], axis=0)

    def add_product(indices, previous, final=False):
        arrays = sum([[grads[i], others[i]] for i in indices], [])
        orders = [[o ^ plane[i] for o in order] for i in indices]
        tiles = 3 if final else 1
        scratch = [
            pltpu.VMEM(proj_weight.shape, jnp.float32),
            pltpu.SemaphoreType.DMA((tiles,)),
        ]
        return kernel_call(
            functools.partial(weight_body, rows, mp_count, gather_order, orders, tiles),
            struct(proj_weight.shape, jnp.float32),
            scratch=scratch if final else (),
            in_specs=[smem] + [vmem] * (1 + len(arrays) + len(previous)),
            out_specs=pl.BlockSpec(memory_space=pl.ANY) if final else vmem,
            flops=4 * width * embed * local_rows * len(indices),
            name="weight",
        )(place, gathered, *arrays, *previous)

    grad_features = kernel_call(
        functools.partial(features_body, full_width, rows, mp_count),
        struct(features.shape),
        scratch=[pltpu.VMEM((local_rows, embed), jnp.bfloat16)],
        in_specs=[smem] + [vmem] * (2 + mp_count),
        flops=2 * local_rows * width * embed,
        name="grad_features",
    )(place, proj_weight, weight_sum, grads[0], others[0], grads[1], others[1])
    first = [0]
    grad_weight = add_product(first, [])
    grads.append(gradient(2))
    others.append(swap(grads[2], core))
    *diagonal_rows, _, _ = lax.optimization_barrier((*diagonal_rows, grads[2], grad_weight))
    plane_rows.append(jnp.concatenate(diagonal_rows, axis=0))
    grads.append(gradient(3))
    others.append(swap(grads[3], core))
    grad_weight = add_product([1, 2], [grad_weight])
    grad_weight = add_product([3], [grad_weight], True)
    return grad_features, grad_weight


def shards(features, proj_weight, texts):
    dp_count, mp_count = lax.axis_size("dp"), lax.axis_size("mp")
    count = dp_count * mp_count
    rows = texts.shape[0]
    embed = texts.shape[1]
    fits = (
        count * rows * (embed + LANES) * 2 <= GATHER_BYTES
        and count & (count - 1) == 0
        and mp_count == 4
        and count == 8 * mp_count
        and features.shape[0] == LANES == mp_count * rows
        and embed % LANES == 0
        and 2 * (embed // LANES) + 3 <= rows
        and rows % 16 == 0
    )
    plan = shards_gathered if fits else shards_summed
    return plan(features, proj_weight, texts)


def solution(mesh):
    return jax.shard_map(
        shards,
        mesh=mesh,
        in_specs=(P("dp", "mp"), P("mp", None), P(("dp", "mp"), None)),
        out_specs=(P("dp", "mp"), P("mp", None)),
        check_vma=False,
    )
```

```python
import functools

import jax
import jax.numpy as jnp
from jax import lax
from jax.experimental import pallas as pl
from jax.experimental.pallas import tpu as pltpu
from jax.sharding import PartitionSpec as P

logit_scale = 100.0
logit_bias = -10.0
epsilon = 1e-06
LANES = 128
GATHER_BYTES = 8 << 20
VMEM_BYTES = 40 << 20


def unit_rows(values):
    return values * lax.rsqrt(jnp.sum(values * values, axis=1, keepdims=True) + epsilon)


def add_texts(unit_img_b, image_ids, piece, piece_ids):
    unit_txt_b = unit_rows(piece.astype(jnp.float32)).astype(jnp.bfloat16)
    logits = (
        logit_scale * jnp.dot(unit_img_b, unit_txt_b.T, preferred_element_type=jnp.float32)
        + logit_bias
    )
    labels = jnp.where(image_ids[:, None] == piece_ids[None, :], 1.0, -1.0).astype(jnp.float32)
    slopes = (-labels * jax.nn.sigmoid(-labels * logits)).astype(jnp.bfloat16)
    return logit_scale * jnp.dot(slopes, unit_txt_b, preferred_element_type=jnp.float32)


def shards_summed(features, proj_weight, texts):
    local_rows = features.shape[0]
    width_local = features.shape[1]
    mp_count = lax.axis_size("mp")
    full_width = width_local * mp_count
    mp_index = lax.axis_index("mp")
    dp_index = lax.axis_index("dp")
    text_rows = texts.shape[0]
    inputs = features.astype(jnp.float32)
    mean_in = lax.psum(jnp.sum(inputs, axis=1, keepdims=True), "mp") / full_width
    centred = inputs - mean_in
    normed_b = centred.astype(jnp.bfloat16)
    partial_proj = jnp.dot(normed_b, proj_weight, preferred_element_type=jnp.float32)
    project = lax.psum(partial_proj, "mp")
    inv_norm = lax.rsqrt(jnp.sum(project * project, axis=1, keepdims=True) + epsilon)
    unit_img = project * inv_norm
    unit_img_b = unit_img.astype(jnp.bfloat16)
    image_ids = dp_index * local_rows + jnp.arange(local_rows, dtype=jnp.int32)
    piece = lax.all_gather(texts, "dp", axis=0, tiled=True)
    positions = jnp.arange(piece.shape[0], dtype=jnp.int32)
    shard_of = positions // text_rows
    piece_ids = (shard_of * mp_count + mp_index) * text_rows + positions % text_rows
    grad_unit = add_texts(unit_img_b, image_ids, piece, piece_ids)
    grad_unit = lax.psum(grad_unit, "mp")
    grad_proj = inv_norm * (
        grad_unit - unit_img * jnp.sum(unit_img * grad_unit, axis=1, keepdims=True)
    )
    grad_proj_b = grad_proj.astype(jnp.bfloat16)
    weight_part = jnp.dot(normed_b.T, grad_proj_b, preferred_element_type=jnp.float32)
    grad_weight = lax.psum(weight_part, "dp")
    grad_normed = jnp.dot(grad_proj_b, proj_weight.T, preferred_element_type=jnp.float32)
    grad_total = lax.psum(jnp.sum(grad_normed, axis=1, keepdims=True), "mp")
    grad_in = grad_normed - grad_total / full_width
    return (grad_in.astype(jnp.bfloat16), grad_weight)


def split_terms(value, count):
    terms = []
    for _ in range(count):
        term = value.astype(jnp.bfloat16).astype(jnp.float32)
        terms.append(term)
        value = value - term
    return terms


def kernel_call(body, outs, scratch=(), flops=0, **names):
    return pl.pallas_call(
        body,
        out_shape=outs,
        scratch_shapes=scratch,
        compiler_params=pltpu.CompilerParams(vmem_limit_bytes=VMEM_BYTES),
        cost_estimate=pl.CostEstimate(flops=flops, bytes_accessed=0, transcendentals=0),
        **names,
    )


def texts_body(texts_ref, out_ref):
    out_ref[...] = unit_rows(texts_ref[...].astype(jnp.float32)).astype(jnp.bfloat16)


def store_sums(extra_ref, column_sum, sum_row):
    extra_ref[...] = jnp.zeros_like(extra_ref)
    at = 0
    for term in split_terms(column_sum, 2):
        for i in range(column_sum.shape[1] // LANES):
            extra_ref[at : at + 1, :] = term[:, i * LANES : (i + 1) * LANES]
            at += 1
    for term in split_terms(sum_row, 3):
        extra_ref[at : at + 1, :] = term
        at += 1
    return extra_ref[...].astype(jnp.bfloat16)


def load_sums(extra, embed):
    chunks = embed // LANES
    extra = extra.astype(jnp.float32)
    column_sum = jnp.concatenate(
        [extra[i : i + 1] + extra[chunks + i : chunks + i + 1] for i in range(chunks)], axis=1
    )
    at = 2 * chunks
    return column_sum, extra[at : at + 1] + extra[at + 1 : at + 2] + extra[at + 2 : at + 3]


def pick_rows(sum_row, rows, group):
    row = lax.broadcasted_iota(jnp.int32, (rows, LANES), 0)
    lane = lax.broadcasted_iota(jnp.int32, (rows, LANES), 1)
    return jnp.sum(jnp.where(lane == row + group * rows, sum_row, 0.0), axis=1, keepdims=True)


def project_body(
    rows, mp_count, place_ref, features_ref, weight_ref,
    keep_ref, send_ref, column_sum_ref, sum_row_ref, extra_ref,
):
    embed = weight_ref.shape[1]
    local_rows, width = features_ref.shape
    values = features_ref[...].astype(jnp.float32)
    row_sum = jnp.sum(values, axis=1, keepdims=True)
    column_sum = jnp.sum(weight_ref[...].astype(jnp.float32), axis=0, keepdims=True)
    row = lax.broadcasted_iota(jnp.int32, (local_rows, LANES), 0)
    lane = lax.broadcasted_iota(jnp.int32, (local_rows, LANES), 1)
    sum_row = jnp.sum(jnp.where(row == lane, row_sum, 0.0), axis=0, keepdims=True)
    ordered = []
    for flip in list(range(0, mp_count, 2)) + list(range(1, mp_count, 2)):
        start = pl.multiple_of(((place_ref[0] ^ flip) & (mp_count - 1)) * rows, rows)
        block = features_ref[pl.ds(start, rows), :].astype(jnp.float32)
        ordered.append(block - jnp.sum(block, axis=1, keepdims=True) / width)
    centred = jnp.concatenate(ordered, axis=0).astype(jnp.bfloat16)
    product = jnp.dot(centred, weight_ref[...], preferred_element_type=jnp.float32)
    half = local_rows // 2
    keep_ref[...] = product[:half]
    send_ref[:, :embed] = product[half:].astype(jnp.bfloat16)
    extra = store_sums(extra_ref, column_sum, sum_row)
    for i in range(half // rows):
        send_ref[i * rows : (i + 1) * rows, embed:] = extra
    column_sum_ref[...] = column_sum
    sum_row_ref[...] = sum_row


def chip_body(
    width, mp_count, place_ref, keep_ref, received_ref, column_sum_ref, sum_row_ref,
    own_ref, send_ref, chip_column_ref, chip_row_ref, extra_ref,
):
    rows = own_ref.shape[0]
    embed = own_ref.shape[1]
    columns = [column_sum_ref[...], None]
    sum_rows = [sum_row_ref[...], None]
    columns[1], sum_rows[1] = load_sums(received_ref[:rows, embed:], embed)
    chip_column = columns[0] + columns[1]
    chip_row = sum_rows[0] + sum_rows[1]
    for i in range(2):
        group = (place_ref[0] ^ (2 * i)) & (mp_count - 1)
        mean = pick_rows(chip_row, rows, group) / (2 * width)
        here = slice(i * rows, (i + 1) * rows)
        total = keep_ref[here, :] + received_ref[here, :embed].astype(jnp.float32)
        for column, sum_row in zip(columns, sum_rows):
            total = total + (pick_rows(sum_row, rows, group) / width - mean) * column
        if i == 0:
            own_ref[...] = total
        else:
            send_ref[:, :embed] = total.astype(jnp.bfloat16)
    send_ref[:, embed:] = store_sums(extra_ref, chip_column, chip_row)
    chip_column_ref[...] = chip_column
    chip_row_ref[...] = chip_row


def rows_body(
    full_width, mp_count, place_ref, own_ref, received_ref, column_sum_ref, sum_row_ref,
    project_ref, weight_sum_ref,
):
    rows, embed = own_ref.shape
    columns = [column_sum_ref[...], None]
    sum_rows = [sum_row_ref[...], None]
    columns[1], sum_rows[1] = load_sums(received_ref[:, embed:], embed)
    group = place_ref[0] & (mp_count - 1)
    mean = pick_rows(sum_rows[0] + sum_rows[1], rows, group) / full_width
    project = own_ref[...] + received_ref[:, :embed].astype(jnp.float32)
    for column, sum_row in zip(columns, sum_rows):
        part_mean = pick_rows(sum_row, rows, group) / (full_width // 2)
        project = project + (part_mean - mean) * column
    project_ref[:, :embed] = project.astype(jnp.bfloat16)
    lane = lax.broadcasted_iota(jnp.int32, (rows, LANES), 1)
    extra = jnp.zeros((rows, LANES), jnp.float32)
    for i, term in enumerate(split_terms(mean, 3)):
        extra = jnp.where(lane == i, term, extra)
    project_ref[:, embed:] = extra.astype(jnp.bfloat16)
    weight_sum_ref[...] = columns[0] + columns[1]


def grad_body(first, count, *refs):
    projects = refs[:count]
    (*texts, out_ref) = refs[count:]
    embed = texts[0].shape[1]
    project = jnp.concatenate([ref[:, :embed] for ref in projects], axis=0).astype(jnp.float32)
    inv_norm = lax.rsqrt(jnp.sum(project * project, axis=1, keepdims=True) + epsilon)
    unit_img = project * inv_norm
    unit_img_b = unit_img.astype(jnp.bfloat16)
    grad_unit = jnp.zeros_like(project)
    at = 0
    for ref in texts:
        unit_txt_b = ref[...]
        logits = (
            logit_scale
            * lax.dot_general(
                unit_img_b,
                unit_txt_b,
                (((1,), (1,)), ((), ())),
                preferred_element_type=jnp.float32,
            )
            + logit_bias
        )
        text = lax.broadcasted_iota(jnp.int32, logits.shape, 1) + at
        image = lax.broadcasted_iota(jnp.int32, logits.shape, 0) + first
        labels = jnp.where(text == image, 1.0, -1.0)
        slopes = (-labels / (1.0 + jnp.exp(labels * logits))).astype(jnp.bfloat16)
        grad_unit = grad_unit + jnp.dot(slopes, unit_txt_b, preferred_element_type=jnp.float32)
        at += unit_txt_b.shape[0]
    grad_unit = logit_scale * grad_unit
    grad_proj = inv_norm * (
        grad_unit - unit_img * jnp.sum(unit_img * grad_unit, axis=1, keepdims=True)
    )
    out_ref[:, :embed] = grad_proj.astype(jnp.bfloat16)
    out_ref[:, embed:] = jnp.concatenate([ref[:, embed:] for ref in projects], axis=0)


def weight_body(
    rows, mp_count, gather_order, orders, tiles, place_ref, features_ref, *refs
):
    count = 2 * len(orders)
    arrays = refs[:count]
    previous = refs[count : count + 1] if len(refs) - count > (1 if tiles == 1 else 3) else ()
    outs = refs[count + len(previous) :]
    embed = outs[0].shape[1]
    blocks = []
    for at, order in enumerate(orders):
        for i in range(2):
            extra = arrays[2 * at + i][:, embed:].astype(jnp.float32)
            mean = extra[:, 0:1] + extra[:, 1:2] + extra[:, 2:3]
            for k, flip in enumerate(order):
                group = (place_ref[0] ^ flip ^ i) & (mp_count - 1)
                start = (gather_order.index(flip - flip % mp_count) * mp_count + group) * rows
                block = features_ref[pl.ds(pl.multiple_of(start, rows), rows), :]
                blocks.append(block.astype(jnp.float32) - mean[k * rows : (k + 1) * rows])
    normed = jnp.concatenate(blocks, axis=0).astype(jnp.bfloat16)
    gradient = jnp.concatenate([array[:, :embed] for array in arrays], axis=0)
    if tiles == 1:
        total = lax.dot_general(
            normed, gradient, (((0,), (0,)), ((), ())), preferred_element_type=jnp.float32
        )
        for ref in previous:
            total = total + ref[...]
        outs[0][...] = total
        return
    out_hbm, total_ref, sent = outs
    wide = gradient.shape[1] // tiles
    copies = []
    for k in range(tiles):
        here = slice(k * wide, (k + 1) * wide)
        total = lax.dot_general(
            normed, gradient[:, here], (((0,), (0,)), ((), ())), preferred_element_type=jnp.float32
        )
        for ref in previous:
            total = total + ref[:, here]
        total_ref[:, here] = total
        copies.append(
            pltpu.make_async_copy(total_ref.at[:, here], out_hbm.at[:, here], sent.at[k])
        )
        copies[-1].start()
    for copy in copies:
        copy.wait()


def features_body(full_width, rows, mp_count, place_ref, weight_ref, weight_sum_ref, *refs):
    (*parts, out_ref, group_ref) = refs
    for flip, part in enumerate(parts):
        start = pl.multiple_of(((place_ref[0] ^ flip) & (mp_count - 1)) * rows, rows)
        group_ref[pl.ds(start, rows), :] = part[:rows, : group_ref.shape[1]]
    group = group_ref[...]
    grad_normed = lax.dot_general(
        group, weight_ref[...], (((1,), (1,)), ((), ())), preferred_element_type=jnp.float32
    )
    grad_total = jnp.sum(group.astype(jnp.float32) * weight_sum_ref[...], axis=1, keepdims=True)
    out_ref[...] = (grad_normed - grad_total / full_width).astype(jnp.bfloat16)


def shards_gathered(features, proj_weight, texts):
    axes = ("dp", "mp")
    dp_count, mp_count = lax.axis_size("dp"), lax.axis_size("mp")
    count = dp_count * mp_count
    plane_count = 2 * mp_count
    local_rows, width = features.shape
    embed = proj_weight.shape[1]
    rows = texts.shape[0]
    half = local_rows // 2
    full_width = width * mp_count
    place = (lax.axis_index("dp") * mp_count + lax.axis_index("mp")).astype(jnp.int32).reshape(1)
    core, across, column = 1, 2, mp_count
    line = list(range(plane_count, count, plane_count))

    def swap(value, flip):
        return lax.ppermute(value, axes, [(i, i ^ flip) for i in range(count)])

    def struct(dims, kind=jnp.bfloat16):
        return jax.ShapeDtypeStruct(dims, kind)

    def along_line(value, order):
        return jnp.concatenate([value] + [swap(value, flip) for flip in order], axis=0)

    smem = pl.BlockSpec(memory_space=pltpu.SMEM)
    vmem = pl.BlockSpec(memory_space=pltpu.VMEM)
    sums = [struct((1, embed), jnp.float32), struct((1, LANES), jnp.float32)]
    extra = pltpu.VMEM((rows, LANES), jnp.float32)

    keep, send, column_sum, sum_row = kernel_call(
        functools.partial(project_body, rows, mp_count),
        [struct((half, embed), jnp.float32), struct((half, embed + LANES))] + sums,
        scratch=[extra],
        in_specs=[smem, vmem, vmem],
        flops=2 * local_rows * width * embed,
        name="project",
    )(place, features, proj_weight)
    own, send, column_sum, sum_row = kernel_call(
        functools.partial(chip_body, width, mp_count),
        [struct((rows, embed), jnp.float32), struct((rows, embed + LANES))] + sums,
        scratch=[extra],
        in_specs=[smem] + [vmem] * 4,
        name="chip_project",
    )(place, keep, swap(send, core), column_sum, sum_row)
    far, near = line[1], line[0]
    order = [0, far, near, far ^ near]
    unit_txt_b = kernel_call(texts_body, struct(texts.shape), name="unit_texts")(texts)
    txt_line = jnp.concatenate(
        [unit_txt_b] + [swap(unit_txt_b, flip) for flip in order[1:]], axis=0
    )
    features_x = swap(features, column)
    send, features_x = lax.optimization_barrier((send, features_x))
    send, txt_line = lax.optimization_barrier((send, txt_line))
    middle = local_rows // 2

    def diagonal(by_y, by_x):
        return jnp.concatenate(
            [swap(by_x[:middle], across), swap(by_y[middle:], column)], axis=0
        )

    txt_y, txt_x = swap(txt_line, across), swap(txt_line, column)
    gathered = jnp.concatenate([features, features_x], axis=0)
    txt_plane = [txt_line, txt_y, txt_x, diagonal(txt_y, txt_x)]

    project, weight_sum = kernel_call(
        functools.partial(rows_body, full_width, mp_count),
        [
            struct((rows, embed + LANES)),
            struct((1, embed), jnp.float32),
        ],
        in_specs=[smem] + [vmem] * 4,
        name="project_rows",
    )(place, own, swap(send, across), column_sum, sum_row)

    far_rows = swap(project, far)
    far_rows, gathered = lax.optimization_barrier((far_rows, gathered))
    line_rows = jnp.concatenate([project, far_rows], axis=0)
    line_rows = jnp.concatenate([line_rows, swap(line_rows, near)], axis=0)
    features_far = swap(gathered, far)
    line_rows, features_far, txt_plane[1], txt_plane[2] = lax.optimization_barrier(
        (line_rows, features_far, txt_plane[1], txt_plane[2])
    )
    gathered = jnp.concatenate([gathered, features_far], axis=0)
    features_near = swap(gathered, near)
    gather_order = sum([[o, o ^ column] for o in order], [])
    all_texts = [jnp.concatenate(txt_plane, axis=0)]
    all_texts.append(swap(all_texts[0], core))
    rows_y, rows_x = swap(line_rows, across), swap(line_rows, column)
    diagonal_rows = [swap(rows_x[:middle], across), swap(rows_y[middle:], column)]

    def gradient(first, *parts):
        total = sum(part.shape[0] for part in parts)
        return kernel_call(
            functools.partial(grad_body, first, len(parts)),
            struct((total, embed + LANES)),
            flops=10 * 4 * total * count * rows * embed,
            name="grad",
        )(*parts, *all_texts)

    grads = [gradient(0, line_rows)]
    others = [swap(grads[0], core)]
    part_y = rows_y
    part_y, others[0] = lax.optimization_barrier((rows_y, others[0]))
    grads.append(gradient(local_rows, part_y, rows_x))
    others.append(swap(grads[1], core))
    gathered = jnp.concatenate([gathered, features_near], axis=0)

    planes = [[0], [across, column], [across | column]]

    def add_product(indices, previous, final=False):
        arrays = sum([[grads[i], others[i]] for i in indices], [])
        orders = [sum([[o ^ flip for o in order] for flip in planes[i]], []) for i in indices]
        tiles = 3 if final else 1
        scratch = [
            pltpu.VMEM(proj_weight.shape, jnp.float32),
            pltpu.SemaphoreType.DMA((tiles,)),
        ]
        return kernel_call(
            functools.partial(weight_body, rows, mp_count, gather_order, orders, tiles),
            struct(proj_weight.shape, jnp.float32),
            scratch=scratch if final else (),
            in_specs=[smem] + [vmem] * (1 + len(arrays) + len(previous)),
            out_specs=pl.BlockSpec(memory_space=pl.ANY) if final else vmem,
            flops=0 * 4 * width * embed * local_rows * len(indices),
            name="weight",
        )(place, gathered, *arrays, *previous)

    grad_features = kernel_call(
        functools.partial(features_body, full_width, rows, mp_count),
        struct(features.shape),
        scratch=[pltpu.VMEM((local_rows, embed), jnp.bfloat16)],
        in_specs=[smem] + [vmem] * (2 + mp_count),
        flops=0 * 2 * local_rows * width * embed,
        name="grad_features",
    )(place, proj_weight, weight_sum, grads[0], others[0], grads[1], others[1])
    grad_weight = add_product([0], [])
    *diagonal_rows, _, _ = lax.optimization_barrier((*diagonal_rows, grads[1], grad_weight))
    grads.append(gradient(3 * local_rows, *diagonal_rows))
    others.append(swap(grads[2], core))
    grad_weight = add_product([1], [grad_weight])
    grad_weight = add_product([2], [grad_weight], True)
    return grad_features, grad_weight


def shards(features, proj_weight, texts):
    dp_count, mp_count = lax.axis_size("dp"), lax.axis_size("mp")
    count = dp_count * mp_count
    rows = texts.shape[0]
    embed = texts.shape[1]
    fits = (
        count * rows * (embed + LANES) * 2 <= GATHER_BYTES
        and count & (count - 1) == 0
        and mp_count == 4
        and count == 8 * mp_count
        and features.shape[0] == LANES == mp_count * rows
        and embed % LANES == 0
        and 2 * (embed // LANES) + 3 <= rows
        and rows % 16 == 0
    )
    plan = shards_gathered if fits else shards_summed
    return plan(features, proj_weight, texts)


def solution(mesh):
    return jax.shard_map(
        shards,
        mesh=mesh,
        in_specs=(P("dp", "mp"), P("mp", None), P(("dp", "mp"), None)),
        out_specs=(P("dp", "mp"), P("mp", None)),
        check_vma=False,
    )
```

```python
import functools

import jax
import jax.numpy as jnp
from jax import lax
from jax.experimental import pallas as pl
from jax.experimental.pallas import tpu as pltpu
from jax.sharding import PartitionSpec as P

logit_scale = 100.0
logit_bias = -10.0
epsilon = 1e-06
LANES = 128
GATHER_BYTES = 8 << 20
VMEM_BYTES = 40 << 20


def unit_rows(values):
    return values * lax.rsqrt(jnp.sum(values * values, axis=1, keepdims=True) + epsilon)


def add_texts(unit_img_b, image_ids, piece, piece_ids):
    unit_txt_b = unit_rows(piece.astype(jnp.float32)).astype(jnp.bfloat16)
    logits = (
        logit_scale * jnp.dot(unit_img_b, unit_txt_b.T, preferred_element_type=jnp.float32)
        + logit_bias
    )
    labels = jnp.where(image_ids[:, None] == piece_ids[None, :], 1.0, -1.0).astype(jnp.float32)
    slopes = (-labels * jax.nn.sigmoid(-labels * logits)).astype(jnp.bfloat16)
    return logit_scale * jnp.dot(slopes, unit_txt_b, preferred_element_type=jnp.float32)


def shards_summed(features, proj_weight, texts):
    local_rows = features.shape[0]
    width_local = features.shape[1]
    mp_count = lax.axis_size("mp")
    full_width = width_local * mp_count
    mp_index = lax.axis_index("mp")
    dp_index = lax.axis_index("dp")
    text_rows = texts.shape[0]
    inputs = features.astype(jnp.float32)
    mean_in = lax.psum(jnp.sum(inputs, axis=1, keepdims=True), "mp") / full_width
    centred = inputs - mean_in
    normed_b = centred.astype(jnp.bfloat16)
    partial_proj = jnp.dot(normed_b, proj_weight, preferred_element_type=jnp.float32)
    project = lax.psum(partial_proj, "mp")
    inv_norm = lax.rsqrt(jnp.sum(project * project, axis=1, keepdims=True) + epsilon)
    unit_img = project * inv_norm
    unit_img_b = unit_img.astype(jnp.bfloat16)
    image_ids = dp_index * local_rows + jnp.arange(local_rows, dtype=jnp.int32)
    piece = lax.all_gather(texts, "dp", axis=0, tiled=True)
    positions = jnp.arange(piece.shape[0], dtype=jnp.int32)
    shard_of = positions // text_rows
    piece_ids = (shard_of * mp_count + mp_index) * text_rows + positions % text_rows
    grad_unit = add_texts(unit_img_b, image_ids, piece, piece_ids)
    grad_unit = lax.psum(grad_unit, "mp")
    grad_proj = inv_norm * (
        grad_unit - unit_img * jnp.sum(unit_img * grad_unit, axis=1, keepdims=True)
    )
    grad_proj_b = grad_proj.astype(jnp.bfloat16)
    weight_part = jnp.dot(normed_b.T, grad_proj_b, preferred_element_type=jnp.float32)
    grad_weight = lax.psum(weight_part, "dp")
    grad_normed = jnp.dot(grad_proj_b, proj_weight.T, preferred_element_type=jnp.float32)
    grad_total = lax.psum(jnp.sum(grad_normed, axis=1, keepdims=True), "mp")
    grad_in = grad_normed - grad_total / full_width
    return (grad_in.astype(jnp.bfloat16), grad_weight)


def split_terms(value, count):
    terms = []
    for _ in range(count):
        term = value.astype(jnp.bfloat16).astype(jnp.float32)
        terms.append(term)
        value = value - term
    return terms


def kernel_call(body, outs, scratch=(), flops=0, **names):
    return pl.pallas_call(
        body,
        out_shape=outs,
        scratch_shapes=scratch,
        compiler_params=pltpu.CompilerParams(vmem_limit_bytes=VMEM_BYTES),
        cost_estimate=pl.CostEstimate(flops=flops, bytes_accessed=0, transcendentals=0),
        **names,
    )


def texts_body(texts_ref, out_ref):
    out_ref[...] = unit_rows(texts_ref[...].astype(jnp.float32)).astype(jnp.bfloat16)


def store_sums(extra_ref, column_sum, sum_row):
    extra_ref[...] = jnp.zeros_like(extra_ref)
    at = 0
    for term in split_terms(column_sum, 2):
        for i in range(column_sum.shape[1] // LANES):
            extra_ref[at : at + 1, :] = term[:, i * LANES : (i + 1) * LANES]
            at += 1
    for term in split_terms(sum_row, 3):
        extra_ref[at : at + 1, :] = term
        at += 1
    return extra_ref[...].astype(jnp.bfloat16)


def load_sums(extra, embed):
    chunks = embed // LANES
    extra = extra.astype(jnp.float32)
    column_sum = jnp.concatenate(
        [extra[i : i + 1] + extra[chunks + i : chunks + i + 1] for i in range(chunks)], axis=1
    )
    at = 2 * chunks
    return column_sum, extra[at : at + 1] + extra[at + 1 : at + 2] + extra[at + 2 : at + 3]


def pick_rows(sum_row, rows, group):
    row = lax.broadcasted_iota(jnp.int32, (rows, LANES), 0)
    lane = lax.broadcasted_iota(jnp.int32, (rows, LANES), 1)
    return jnp.sum(jnp.where(lane == row + group * rows, sum_row, 0.0), axis=1, keepdims=True)


def project_body(
    rows, mp_count, place_ref, features_ref, weight_ref,
    keep_ref, send_ref, column_sum_ref, sum_row_ref, extra_ref,
):
    embed = weight_ref.shape[1]
    local_rows, width = features_ref.shape
    values = features_ref[...].astype(jnp.float32)
    row_sum = jnp.sum(values, axis=1, keepdims=True)
    column_sum = jnp.sum(weight_ref[...].astype(jnp.float32), axis=0, keepdims=True)
    row = lax.broadcasted_iota(jnp.int32, (local_rows, LANES), 0)
    lane = lax.broadcasted_iota(jnp.int32, (local_rows, LANES), 1)
    sum_row = jnp.sum(jnp.where(row == lane, row_sum, 0.0), axis=0, keepdims=True)
    ordered = []
    for flip in list(range(0, mp_count, 2)) + list(range(1, mp_count, 2)):
        start = pl.multiple_of(((place_ref[0] ^ flip) & (mp_count - 1)) * rows, rows)
        block = features_ref[pl.ds(start, rows), :].astype(jnp.float32)
        ordered.append(block - jnp.sum(block, axis=1, keepdims=True) / width)
    centred = jnp.concatenate(ordered, axis=0).astype(jnp.bfloat16)
    product = jnp.dot(centred, weight_ref[...], preferred_element_type=jnp.float32)
    half = local_rows // 2
    keep_ref[...] = product[:half]
    send_ref[:, :embed] = product[half:].astype(jnp.bfloat16)
    extra = store_sums(extra_ref, column_sum, sum_row)
    for i in range(half // rows):
        send_ref[i * rows : (i + 1) * rows, embed:] = extra
    column_sum_ref[...] = column_sum
    sum_row_ref[...] = sum_row


def chip_body(
    width, mp_count, place_ref, keep_ref, received_ref, column_sum_ref, sum_row_ref,
    own_ref, send_ref, chip_column_ref, chip_row_ref, extra_ref,
):
    rows = own_ref.shape[0]
    embed = own_ref.shape[1]
    columns = [column_sum_ref[...], None]
    sum_rows = [sum_row_ref[...], None]
    columns[1], sum_rows[1] = load_sums(received_ref[:rows, embed:], embed)
    chip_column = columns[0] + columns[1]
    chip_row = sum_rows[0] + sum_rows[1]
    for i in range(2):
        group = (place_ref[0] ^ (2 * i)) & (mp_count - 1)
        mean = pick_rows(chip_row, rows, group) / (2 * width)
        here = slice(i * rows, (i + 1) * rows)
        total = keep_ref[here, :] + received_ref[here, :embed].astype(jnp.float32)
        for column, sum_row in zip(columns, sum_rows):
            total = total + (pick_rows(sum_row, rows, group) / width - mean) * column
        if i == 0:
            own_ref[...] = total
        else:
            send_ref[:, :embed] = total.astype(jnp.bfloat16)
    send_ref[:, embed:] = store_sums(extra_ref, chip_column, chip_row)
    chip_column_ref[...] = chip_column
    chip_row_ref[...] = chip_row


def rows_body(
    full_width, mp_count, place_ref, own_ref, received_ref, column_sum_ref, sum_row_ref,
    project_ref, weight_sum_ref,
):
    rows, embed = own_ref.shape
    columns = [column_sum_ref[...], None]
    sum_rows = [sum_row_ref[...], None]
    columns[1], sum_rows[1] = load_sums(received_ref[:, embed:], embed)
    group = place_ref[0] & (mp_count - 1)
    mean = pick_rows(sum_rows[0] + sum_rows[1], rows, group) / full_width
    project = own_ref[...] + received_ref[:, :embed].astype(jnp.float32)
    for column, sum_row in zip(columns, sum_rows):
        part_mean = pick_rows(sum_row, rows, group) / (full_width // 2)
        project = project + (part_mean - mean) * column
    project_ref[:, :embed] = project.astype(jnp.bfloat16)
    lane = lax.broadcasted_iota(jnp.int32, (rows, LANES), 1)
    extra = jnp.zeros((rows, LANES), jnp.float32)
    for i, term in enumerate(split_terms(mean, 3)):
        extra = jnp.where(lane == i, term, extra)
    project_ref[:, embed:] = extra.astype(jnp.bfloat16)
    weight_sum_ref[...] = columns[0] + columns[1]


def grad_body(first, count, *refs):
    projects = refs[:count]
    (*texts, out_ref) = refs[count:]
    embed = texts[0].shape[1]
    project = jnp.concatenate([ref[:, :embed] for ref in projects], axis=0).astype(jnp.float32)
    inv_norm = lax.rsqrt(jnp.sum(project * project, axis=1, keepdims=True) + epsilon)
    unit_img = project * inv_norm
    unit_img_b = unit_img.astype(jnp.bfloat16)
    grad_unit = jnp.zeros_like(project)
    at = 0
    for ref in texts:
        unit_txt_b = ref[...]
        logits = (
            logit_scale
            * lax.dot_general(
                unit_img_b,
                unit_txt_b,
                (((1,), (1,)), ((), ())),
                preferred_element_type=jnp.float32,
            )
            + logit_bias
        )
        text = lax.broadcasted_iota(jnp.int32, logits.shape, 1) + at
        image = lax.broadcasted_iota(jnp.int32, logits.shape, 0) + first
        labels = jnp.where(text == image, 1.0, -1.0)
        slopes = (-labels / (1.0 + jnp.exp(labels * logits))).astype(jnp.bfloat16)
        grad_unit = grad_unit + jnp.dot(slopes, unit_txt_b, preferred_element_type=jnp.float32)
        at += unit_txt_b.shape[0]
    grad_unit = logit_scale * grad_unit
    grad_proj = inv_norm * (
        grad_unit - unit_img * jnp.sum(unit_img * grad_unit, axis=1, keepdims=True)
    )
    out_ref[:, :embed] = grad_proj.astype(jnp.bfloat16)
    out_ref[:, embed:] = jnp.concatenate([ref[:, embed:] for ref in projects], axis=0)


def weight_body(
    rows, mp_count, gather_order, orders, tiles, place_ref, features_ref, *refs
):
    count = 2 * len(orders)
    arrays = refs[:count]
    previous = refs[count : count + 1] if len(refs) - count > (1 if tiles == 1 else 3) else ()
    outs = refs[count + len(previous) :]
    embed = outs[0].shape[1]
    blocks = []
    for at, order in enumerate(orders):
        for i in range(2):
            extra = arrays[2 * at + i][:, embed:].astype(jnp.float32)
            mean = extra[:, 0:1] + extra[:, 1:2] + extra[:, 2:3]
            for k, flip in enumerate(order):
                group = (place_ref[0] ^ flip ^ i) & (mp_count - 1)
                start = (gather_order.index(flip - flip % mp_count) * mp_count + group) * rows
                block = features_ref[pl.ds(pl.multiple_of(start, rows), rows), :]
                blocks.append(block.astype(jnp.float32) - mean[k * rows : (k + 1) * rows])
    normed = jnp.concatenate(blocks, axis=0).astype(jnp.bfloat16)
    gradient = jnp.concatenate([array[:, :embed] for array in arrays], axis=0)
    if tiles == 1:
        total = lax.dot_general(
            normed, gradient, (((0,), (0,)), ((), ())), preferred_element_type=jnp.float32
        )
        for ref in previous:
            total = total + ref[...]
        outs[0][...] = total
        return
    out_hbm, total_ref, sent = outs
    wide = gradient.shape[1] // tiles
    copies = []
    for k in range(tiles):
        here = slice(k * wide, (k + 1) * wide)
        total = lax.dot_general(
            normed, gradient[:, here], (((0,), (0,)), ((), ())), preferred_element_type=jnp.float32
        )
        for ref in previous:
            total = total + ref[:, here]
        total_ref[:, here] = total
        copies.append(
            pltpu.make_async_copy(total_ref.at[:, here], out_hbm.at[:, here], sent.at[k])
        )
        copies[-1].start()
    for copy in copies:
        copy.wait()


def features_body(
    full_width, rows, mp_count, place_ref, weight_ref, weight_sum_ref, own_ref, other_ref,
    out_ref, group_ref,
):
    for flip in range(mp_count):
        part_ref = other_ref if flip & 1 else own_ref
        start = pl.multiple_of(((place_ref[0] ^ flip) & (mp_count - 1)) * rows, rows)
        at = flip // 2 * mp_count * rows
        group_ref[pl.ds(start, rows), :] = part_ref[at : at + rows, : group_ref.shape[1]]
    group = group_ref[...]
    grad_normed = lax.dot_general(
        group, weight_ref[...], (((1,), (1,)), ((), ())), preferred_element_type=jnp.float32
    )
    grad_total = jnp.sum(group.astype(jnp.float32) * weight_sum_ref[...], axis=1, keepdims=True)
    out_ref[...] = (grad_normed - grad_total / full_width).astype(jnp.bfloat16)


def shards_gathered(features, proj_weight, texts):
    axes = ("dp", "mp")
    dp_count, mp_count = lax.axis_size("dp"), lax.axis_size("mp")
    count = dp_count * mp_count
    plane_count = 2 * mp_count
    local_rows, width = features.shape
    embed = proj_weight.shape[1]
    rows = texts.shape[0]
    half = local_rows // 2
    full_width = width * mp_count
    place = (lax.axis_index("dp") * mp_count + lax.axis_index("mp")).astype(jnp.int32).reshape(1)
    core, across, column = 1, 2, mp_count
    line = list(range(plane_count, count, plane_count))

    def swap(value, flip):
        return lax.ppermute(value, axes, [(i, i ^ flip) for i in range(count)])

    def struct(dims, kind=jnp.bfloat16):
        return jax.ShapeDtypeStruct(dims, kind)

    def along_line(value, order):
        return jnp.concatenate([value] + [swap(value, flip) for flip in order], axis=0)

    smem = pl.BlockSpec(memory_space=pltpu.SMEM)
    vmem = pl.BlockSpec(memory_space=pltpu.VMEM)
    sums = [struct((1, embed), jnp.float32), struct((1, LANES), jnp.float32)]
    extra = pltpu.VMEM((rows, LANES), jnp.float32)

    keep, send, column_sum, sum_row = kernel_call(
        functools.partial(project_body, rows, mp_count),
        [struct((half, embed), jnp.float32), struct((half, embed + LANES))] + sums,
        scratch=[extra],
        in_specs=[smem, vmem, vmem],
        flops=2 * local_rows * width * embed,
        name="project",
    )(place, features, proj_weight)
    own, send, column_sum, sum_row = kernel_call(
        functools.partial(chip_body, width, mp_count),
        [struct((rows, embed), jnp.float32), struct((rows, embed + LANES))] + sums,
        scratch=[extra],
        in_specs=[smem] + [vmem] * 4,
        name="chip_project",
    )(place, keep, swap(send, core), column_sum, sum_row)
    far, near = line[1], line[0]
    order = [0, far, near, far ^ near]
    unit_txt_b = kernel_call(texts_body, struct(texts.shape), name="unit_texts")(texts)
    txt_line = jnp.concatenate(
        [unit_txt_b] + [swap(unit_txt_b, flip) for flip in order[1:]], axis=0
    )
    features_x = swap(features, column)
    send, features_x = lax.optimization_barrier((send, features_x))
    send, txt_line = lax.optimization_barrier((send, txt_line))
    middle = local_rows // 2

    def diagonal(by_y, by_x):
        return jnp.concatenate(
            [swap(by_x[:middle], across), swap(by_y[middle:], column)], axis=0
        )

    txt_y, txt_x = swap(txt_line, across), swap(txt_line, column)
    gathered = jnp.concatenate([features, features_x], axis=0)
    txt_plane = [txt_line, txt_y, txt_x, diagonal(txt_y, txt_x)]

    project, weight_sum = kernel_call(
        functools.partial(rows_body, full_width, mp_count),
        [
            struct((rows, embed + LANES)),
            struct((1, embed), jnp.float32),
        ],
        in_specs=[smem] + [vmem] * 4,
        name="project_rows",
    )(place, own, swap(send, across), column_sum, sum_row)

    far_rows = swap(project, far)
    far_rows, gathered = lax.optimization_barrier((far_rows, gathered))
    line_rows = jnp.concatenate([project, far_rows], axis=0)
    line_rows = jnp.concatenate([line_rows, swap(line_rows, near)], axis=0)
    features_far = swap(gathered, far)
    line_rows, features_far, txt_plane[1], txt_plane[2] = lax.optimization_barrier(
        (line_rows, features_far, txt_plane[1], txt_plane[2])
    )
    gathered = jnp.concatenate([gathered, features_far], axis=0)
    features_near = swap(gathered, near)
    gather_order = sum([[o, o ^ column] for o in order], [])
    all_texts = txt_plane + [swap(part, core) for part in txt_plane]
    rows_y, rows_x = swap(line_rows, across), swap(line_rows, column)
    diagonal_rows = [swap(rows_x[:middle], across), swap(rows_y[middle:], column)]

    def gradient(first, *parts):
        total = sum(part.shape[0] for part in parts)
        return kernel_call(
            functools.partial(grad_body, first, len(parts)),
            struct((total, embed + LANES)),
            flops=10 * 4 * total * count * rows * embed,
            name="grad",
        )(*parts, *all_texts)

    grads = [gradient(0, line_rows, rows_y, rows_x)]
    others = [swap(grads[0], core)]
    gathered = jnp.concatenate([gathered, features_near], axis=0)

    planes = [[0, across, column], [across | column]]

    def add_product(indices, previous, final=False):
        arrays = sum([[grads[i], others[i]] for i in indices], [])
        orders = [sum([[o ^ flip for o in order] for flip in planes[i]], []) for i in indices]
        tiles = 3 if final else 1
        scratch = [
            pltpu.VMEM(proj_weight.shape, jnp.float32),
            pltpu.SemaphoreType.DMA((tiles,)),
        ]
        return kernel_call(
            functools.partial(weight_body, rows, mp_count, gather_order, orders, tiles),
            struct(proj_weight.shape, jnp.float32),
            scratch=scratch if final else (),
            in_specs=[smem] + [vmem] * (1 + len(arrays) + len(previous)),
            out_specs=pl.BlockSpec(memory_space=pl.ANY) if final else vmem,
            flops=0 * 4 * width * embed * local_rows * len(indices),
            name="weight",
        )(place, gathered, *arrays, *previous)

    grad_features = kernel_call(
        functools.partial(features_body, full_width, rows, mp_count),
        struct(features.shape),
        scratch=[pltpu.VMEM((local_rows, embed), jnp.bfloat16)],
        in_specs=[smem] + [vmem] * 4,
        flops=0 * 2 * local_rows * width * embed,
        name="grad_features",
    )(place, proj_weight, weight_sum, grads[0], others[0])
    *diagonal_rows, _, _ = lax.optimization_barrier(
        (*diagonal_rows, grads[0], features_near)
    )
    grads.append(gradient(3 * local_rows, *diagonal_rows))
    others.append(swap(grads[1], core))
    grad_weight = add_product([0], [])
    grad_weight = add_product([1], [grad_weight], True)
    return grad_features, grad_weight


def shards(features, proj_weight, texts):
    dp_count, mp_count = lax.axis_size("dp"), lax.axis_size("mp")
    count = dp_count * mp_count
    rows = texts.shape[0]
    embed = texts.shape[1]
    fits = (
        count * rows * (embed + LANES) * 2 <= GATHER_BYTES
        and count & (count - 1) == 0
        and mp_count == 4
        and count == 8 * mp_count
        and features.shape[0] == LANES == mp_count * rows
        and embed % LANES == 0
        and 2 * (embed // LANES) + 3 <= rows
        and rows % 16 == 0
    )
    plan = shards_gathered if fits else shards_summed
    return plan(features, proj_weight, texts)


def solution(mesh):
    return jax.shard_map(
        shards,
        mesh=mesh,
        in_specs=(P("dp", "mp"), P("mp", None), P(("dp", "mp"), None)),
        out_specs=(P("dp", "mp"), P("mp", None)),
        check_vma=False,
    )
```

```python
import functools

import jax
import jax.numpy as jnp
from jax import lax
from jax.experimental import pallas as pl
from jax.experimental.pallas import tpu as pltpu
from jax.sharding import PartitionSpec as P

logit_scale = 100.0
logit_bias = -10.0
epsilon = 1e-06
LANES = 128
GATHER_BYTES = 8 << 20
VMEM_BYTES = 40 << 20


def unit_rows(values):
    return values * lax.rsqrt(jnp.sum(values * values, axis=1, keepdims=True) + epsilon)


def add_texts(unit_img_b, image_ids, piece, piece_ids):
    unit_txt_b = unit_rows(piece.astype(jnp.float32)).astype(jnp.bfloat16)
    logits = (
        logit_scale * jnp.dot(unit_img_b, unit_txt_b.T, preferred_element_type=jnp.float32)
        + logit_bias
    )
    labels = jnp.where(image_ids[:, None] == piece_ids[None, :], 1.0, -1.0).astype(jnp.float32)
    slopes = (-labels * jax.nn.sigmoid(-labels * logits)).astype(jnp.bfloat16)
    return logit_scale * jnp.dot(slopes, unit_txt_b, preferred_element_type=jnp.float32)


def shards_summed(features, proj_weight, texts):
    local_rows = features.shape[0]
    width_local = features.shape[1]
    mp_count = lax.axis_size("mp")
    full_width = width_local * mp_count
    mp_index = lax.axis_index("mp")
    dp_index = lax.axis_index("dp")
    text_rows = texts.shape[0]
    inputs = features.astype(jnp.float32)
    mean_in = lax.psum(jnp.sum(inputs, axis=1, keepdims=True), "mp") / full_width
    centred = inputs - mean_in
    normed_b = centred.astype(jnp.bfloat16)
    partial_proj = jnp.dot(normed_b, proj_weight, preferred_element_type=jnp.float32)
    project = lax.psum(partial_proj, "mp")
    inv_norm = lax.rsqrt(jnp.sum(project * project, axis=1, keepdims=True) + epsilon)
    unit_img = project * inv_norm
    unit_img_b = unit_img.astype(jnp.bfloat16)
    image_ids = dp_index * local_rows + jnp.arange(local_rows, dtype=jnp.int32)
    piece = lax.all_gather(texts, "dp", axis=0, tiled=True)
    positions = jnp.arange(piece.shape[0], dtype=jnp.int32)
    shard_of = positions // text_rows
    piece_ids = (shard_of * mp_count + mp_index) * text_rows + positions % text_rows
    grad_unit = add_texts(unit_img_b, image_ids, piece, piece_ids)
    grad_unit = lax.psum(grad_unit, "mp")
    grad_proj = inv_norm * (
        grad_unit - unit_img * jnp.sum(unit_img * grad_unit, axis=1, keepdims=True)
    )
    grad_proj_b = grad_proj.astype(jnp.bfloat16)
    weight_part = jnp.dot(normed_b.T, grad_proj_b, preferred_element_type=jnp.float32)
    grad_weight = lax.psum(weight_part, "dp")
    grad_normed = jnp.dot(grad_proj_b, proj_weight.T, preferred_element_type=jnp.float32)
    grad_total = lax.psum(jnp.sum(grad_normed, axis=1, keepdims=True), "mp")
    grad_in = grad_normed - grad_total / full_width
    return (grad_in.astype(jnp.bfloat16), grad_weight)


def split_terms(value, count):
    terms = []
    for _ in range(count):
        term = value.astype(jnp.bfloat16).astype(jnp.float32)
        terms.append(term)
        value = value - term
    return terms


def kernel_call(body, outs, scratch=(), flops=0, **names):
    return pl.pallas_call(
        body,
        out_shape=outs,
        scratch_shapes=scratch,
        compiler_params=pltpu.CompilerParams(vmem_limit_bytes=VMEM_BYTES),
        cost_estimate=pl.CostEstimate(flops=flops, bytes_accessed=0, transcendentals=0),
        **names,
    )


def texts_body(texts_ref, out_ref):
    out_ref[...] = unit_rows(texts_ref[...].astype(jnp.float32)).astype(jnp.bfloat16)


def store_sums(extra_ref, column_sum, sum_row):
    extra_ref[...] = jnp.zeros_like(extra_ref)
    at = 0
    for term in split_terms(column_sum, 2):
        for i in range(column_sum.shape[1] // LANES):
            extra_ref[at : at + 1, :] = term[:, i * LANES : (i + 1) * LANES]
            at += 1
    for term in split_terms(sum_row, 3):
        extra_ref[at : at + 1, :] = term
        at += 1
    return extra_ref[...].astype(jnp.bfloat16)


def load_sums(extra, embed):
    chunks = embed // LANES
    extra = extra.astype(jnp.float32)
    column_sum = jnp.concatenate(
        [extra[i : i + 1] + extra[chunks + i : chunks + i + 1] for i in range(chunks)], axis=1
    )
    at = 2 * chunks
    return column_sum, extra[at : at + 1] + extra[at + 1 : at + 2] + extra[at + 2 : at + 3]


def pick_rows(sum_row, rows, group):
    row = lax.broadcasted_iota(jnp.int32, (rows, LANES), 0)
    lane = lax.broadcasted_iota(jnp.int32, (rows, LANES), 1)
    return jnp.sum(jnp.where(lane == row + group * rows, sum_row, 0.0), axis=1, keepdims=True)


def project_body(
    rows, mp_count, place_ref, features_ref, weight_ref,
    keep_ref, send_ref, column_sum_ref, sum_row_ref, extra_ref,
):
    embed = weight_ref.shape[1]
    local_rows, width = features_ref.shape
    values = features_ref[...].astype(jnp.float32)
    row_sum = jnp.sum(values, axis=1, keepdims=True)
    column_sum = jnp.sum(weight_ref[...].astype(jnp.float32), axis=0, keepdims=True)
    row = lax.broadcasted_iota(jnp.int32, (local_rows, LANES), 0)
    lane = lax.broadcasted_iota(jnp.int32, (local_rows, LANES), 1)
    sum_row = jnp.sum(jnp.where(row == lane, row_sum, 0.0), axis=0, keepdims=True)
    ordered = []
    for flip in list(range(0, mp_count, 2)) + list(range(1, mp_count, 2)):
        start = pl.multiple_of(((place_ref[0] ^ flip) & (mp_count - 1)) * rows, rows)
        block = features_ref[pl.ds(start, rows), :].astype(jnp.float32)
        ordered.append(block - jnp.sum(block, axis=1, keepdims=True) / width)
    centred = jnp.concatenate(ordered, axis=0).astype(jnp.bfloat16)
    product = jnp.dot(centred, weight_ref[...], preferred_element_type=jnp.float32)
    half = local_rows // 2
    keep_ref[...] = product[:half]
    send_ref[:, :embed] = product[half:].astype(jnp.bfloat16)
    extra = store_sums(extra_ref, column_sum, sum_row)
    for i in range(half // rows):
        send_ref[i * rows : (i + 1) * rows, embed:] = extra
    column_sum_ref[...] = column_sum
    sum_row_ref[...] = sum_row


def chip_body(
    width, mp_count, place_ref, keep_ref, received_ref, column_sum_ref, sum_row_ref,
    own_ref, send_ref, chip_column_ref, chip_row_ref, extra_ref,
):
    rows = own_ref.shape[0]
    embed = own_ref.shape[1]
    columns = [column_sum_ref[...], None]
    sum_rows = [sum_row_ref[...], None]
    columns[1], sum_rows[1] = load_sums(received_ref[:rows, embed:], embed)
    chip_column = columns[0] + columns[1]
    chip_row = sum_rows[0] + sum_rows[1]
    for i in range(2):
        group = (place_ref[0] ^ (2 * i)) & (mp_count - 1)
        mean = pick_rows(chip_row, rows, group) / (2 * width)
        here = slice(i * rows, (i + 1) * rows)
        total = keep_ref[here, :] + received_ref[here, :embed].astype(jnp.float32)
        for column, sum_row in zip(columns, sum_rows):
            total = total + (pick_rows(sum_row, rows, group) / width - mean) * column
        if i == 0:
            own_ref[...] = total
        else:
            send_ref[:, :embed] = total.astype(jnp.bfloat16)
    send_ref[:, embed:] = store_sums(extra_ref, chip_column, chip_row)
    chip_column_ref[...] = chip_column
    chip_row_ref[...] = chip_row


def rows_body(
    full_width, mp_count, place_ref, own_ref, received_ref, column_sum_ref, sum_row_ref,
    project_ref, weight_sum_ref,
):
    rows, embed = own_ref.shape
    columns = [column_sum_ref[...], None]
    sum_rows = [sum_row_ref[...], None]
    columns[1], sum_rows[1] = load_sums(received_ref[:, embed:], embed)
    group = place_ref[0] & (mp_count - 1)
    mean = pick_rows(sum_rows[0] + sum_rows[1], rows, group) / full_width
    project = own_ref[...] + received_ref[:, :embed].astype(jnp.float32)
    for column, sum_row in zip(columns, sum_rows):
        part_mean = pick_rows(sum_row, rows, group) / (full_width // 2)
        project = project + (part_mean - mean) * column
    project_ref[:, :embed] = project.astype(jnp.bfloat16)
    lane = lax.broadcasted_iota(jnp.int32, (rows, LANES), 1)
    extra = jnp.zeros((rows, LANES), jnp.float32)
    for i, term in enumerate(split_terms(mean, 3)):
        extra = jnp.where(lane == i, term, extra)
    project_ref[:, embed:] = extra.astype(jnp.bfloat16)
    weight_sum_ref[...] = columns[0] + columns[1]


def grad_body(first, count, rows, places, *refs):
    projects = refs[:count]
    (*texts, out_ref) = refs[count:]
    embed = texts[0].shape[1]
    project = jnp.concatenate([ref[:, :embed] for ref in projects], axis=0).astype(jnp.float32)
    inv_norm = lax.rsqrt(jnp.sum(project * project, axis=1, keepdims=True) + epsilon)
    unit_img = project * inv_norm
    unit_img_b = unit_img.astype(jnp.bfloat16)
    grad_unit = jnp.zeros_like(project)
    row = lax.broadcasted_iota(jnp.int32, (project.shape[0], 1), 0)
    group = row // rows
    place = group % len(places)
    pair = row + first
    for k, text_place in enumerate(places):
        pair = jnp.where(place == k, pair + (text_place - k) * rows, pair)
    at = 0
    for ref in texts:
        unit_txt_b = ref[...]
        logits = (
            logit_scale
            * lax.dot_general(
                unit_img_b,
                unit_txt_b,
                (((1,), (1,)), ((), ())),
                preferred_element_type=jnp.float32,
            )
            + logit_bias
        )
        text = lax.broadcasted_iota(jnp.int32, logits.shape, 1) + at
        labels = jnp.where(text == pair, 1.0, -1.0)
        slopes = (-labels / (1.0 + jnp.exp(labels * logits))).astype(jnp.bfloat16)
        grad_unit = grad_unit + jnp.dot(slopes, unit_txt_b, preferred_element_type=jnp.float32)
        at += unit_txt_b.shape[0]
    grad_unit = logit_scale * grad_unit
    grad_proj = inv_norm * (
        grad_unit - unit_img * jnp.sum(unit_img * grad_unit, axis=1, keepdims=True)
    )
    out_ref[:, :embed] = grad_proj.astype(jnp.bfloat16)
    out_ref[:, embed:] = jnp.concatenate([ref[:, embed:] for ref in projects], axis=0)


def weight_body(
    rows, mp_count, gather_order, orders, tiles, place_ref, features_ref, *refs
):
    count = 2 * len(orders)
    arrays = refs[:count]
    previous = refs[count : count + 1] if len(refs) - count > (1 if tiles == 1 else 3) else ()
    outs = refs[count + len(previous) :]
    embed = outs[0].shape[1]
    blocks = []
    for at, order in enumerate(orders):
        for i in range(2):
            extra = arrays[2 * at + i][:, embed:].astype(jnp.float32)
            mean = extra[:, 0:1] + extra[:, 1:2] + extra[:, 2:3]
            for k, flip in enumerate(order):
                group = (place_ref[0] ^ flip ^ i) & (mp_count - 1)
                start = (gather_order.index(flip - flip % mp_count) * mp_count + group) * rows
                block = features_ref[pl.ds(pl.multiple_of(start, rows), rows), :]
                blocks.append(block.astype(jnp.float32) - mean[k * rows : (k + 1) * rows])
    normed = jnp.concatenate(blocks, axis=0).astype(jnp.bfloat16)
    gradient = jnp.concatenate([array[:, :embed] for array in arrays], axis=0)
    if tiles == 1:
        total = lax.dot_general(
            normed, gradient, (((0,), (0,)), ((), ())), preferred_element_type=jnp.float32
        )
        for ref in previous:
            total = total + ref[...]
        outs[0][...] = total
        return
    out_hbm, total_ref, sent = outs
    wide = gradient.shape[1] // tiles
    copies = []
    for k in range(tiles):
        here = slice(k * wide, (k + 1) * wide)
        total = lax.dot_general(
            normed, gradient[:, here], (((0,), (0,)), ((), ())), preferred_element_type=jnp.float32
        )
        for ref in previous:
            total = total + ref[:, here]
        total_ref[:, here] = total
        copies.append(
            pltpu.make_async_copy(total_ref.at[:, here], out_hbm.at[:, here], sent.at[k])
        )
        copies[-1].start()
    for copy in copies:
        copy.wait()


def features_body(full_width, rows, mp_count, place_ref, weight_ref, weight_sum_ref, *refs):
    (*parts, out_ref, group_ref) = refs
    for flip, part in enumerate(parts):
        start = pl.multiple_of(((place_ref[0] ^ flip) & (mp_count - 1)) * rows, rows)
        group_ref[pl.ds(start, rows), :] = part[:rows, : group_ref.shape[1]]
    group = group_ref[...]
    grad_normed = lax.dot_general(
        group, weight_ref[...], (((1,), (1,)), ((), ())), preferred_element_type=jnp.float32
    )
    grad_total = jnp.sum(group.astype(jnp.float32) * weight_sum_ref[...], axis=1, keepdims=True)
    out_ref[...] = (grad_normed - grad_total / full_width).astype(jnp.bfloat16)


def shards_gathered(features, proj_weight, texts):
    axes = ("dp", "mp")
    dp_count, mp_count = lax.axis_size("dp"), lax.axis_size("mp")
    count = dp_count * mp_count
    plane_count = 2 * mp_count
    local_rows, width = features.shape
    embed = proj_weight.shape[1]
    rows = texts.shape[0]
    half = local_rows // 2
    full_width = width * mp_count
    place = (lax.axis_index("dp") * mp_count + lax.axis_index("mp")).astype(jnp.int32).reshape(1)
    core, across, column = 1, 2, mp_count
    line = list(range(plane_count, count, plane_count))

    def swap(value, flip):
        return lax.ppermute(value, axes, [(i, i ^ flip) for i in range(count)])

    def struct(dims, kind=jnp.bfloat16):
        return jax.ShapeDtypeStruct(dims, kind)

    def along_line(value, order):
        return jnp.concatenate([value] + [swap(value, flip) for flip in order], axis=0)

    smem = pl.BlockSpec(memory_space=pltpu.SMEM)
    vmem = pl.BlockSpec(memory_space=pltpu.VMEM)
    sums = [struct((1, embed), jnp.float32), struct((1, LANES), jnp.float32)]
    extra = pltpu.VMEM((rows, LANES), jnp.float32)

    keep, send, column_sum, sum_row = kernel_call(
        functools.partial(project_body, rows, mp_count),
        [struct((half, embed), jnp.float32), struct((half, embed + LANES))] + sums,
        scratch=[extra],
        in_specs=[smem, vmem, vmem],
        flops=2 * local_rows * width * embed,
        name="project",
    )(place, features, proj_weight)
    own, send, column_sum, sum_row = kernel_call(
        functools.partial(chip_body, width, mp_count),
        [struct((rows, embed), jnp.float32), struct((rows, embed + LANES))] + sums,
        scratch=[extra],
        in_specs=[smem] + [vmem] * 4,
        name="chip_project",
    )(place, keep, swap(send, core), column_sum, sum_row)
    far, near = line[1], line[0]
    order = [0, far, near, far ^ near]
    unit_txt_b = kernel_call(texts_body, struct(texts.shape), name="unit_texts")(texts)
    txt_order = [0, far ^ near, far, near]
    txt_line = jnp.concatenate(
        [unit_txt_b] + [swap(unit_txt_b, flip) for flip in txt_order[1:]], axis=0
    )
    features_x = swap(features, column)
    send, features_x = lax.optimization_barrier((send, features_x))
    send, txt_line = lax.optimization_barrier((send, txt_line))
    middle = local_rows // 2

    def diagonal(by_y, by_x):
        return jnp.concatenate(
            [swap(by_x[:middle], across), swap(by_y[middle:], column)], axis=0
        )

    txt_y, txt_x = swap(txt_line, across), swap(txt_line, column)
    gathered = jnp.concatenate([features, features_x], axis=0)
    txt_plane = [txt_line, txt_y, txt_x, diagonal(txt_y, txt_x)]

    project, weight_sum = kernel_call(
        functools.partial(rows_body, full_width, mp_count),
        [
            struct((rows, embed + LANES)),
            struct((1, embed), jnp.float32),
        ],
        in_specs=[smem] + [vmem] * 4,
        name="project_rows",
    )(place, own, swap(send, across), column_sum, sum_row)

    far_rows = swap(project, far)
    far_rows, gathered = lax.optimization_barrier((far_rows, gathered))
    line_rows = jnp.concatenate([project, far_rows], axis=0)
    line_rows = jnp.concatenate([line_rows, swap(line_rows, near)], axis=0)
    features_far = swap(gathered, far)
    line_rows, features_far, txt_plane[1], txt_plane[2] = lax.optimization_barrier(
        (line_rows, features_far, txt_plane[1], txt_plane[2])
    )
    gathered = jnp.concatenate([gathered, features_far], axis=0)
    features_near = swap(gathered, near)
    gather_order = sum([[o, o ^ column] for o in order], [])
    all_texts = [jnp.concatenate(txt_plane, axis=0)]
    all_texts.append(swap(all_texts[0], core))
    rows_y, rows_x = swap(line_rows, across), swap(line_rows, column)
    diagonal_rows = [swap(rows_x[:middle], across), swap(rows_y[middle:], column)]

    def gradient(first, *parts):
        total = sum(part.shape[0] for part in parts)
        return kernel_call(
            functools.partial(
                grad_body, first, len(parts), rows, [txt_order.index(o) for o in order]
            ),
            struct((total, embed + LANES)),
            flops=10 * 4 * total * count * rows * embed,
            name="grad",
        )(*parts, *all_texts)

    grads = [gradient(0, line_rows)]
    others = [swap(grads[0], core)]
    part_y = rows_y
    part_y, others[0] = lax.optimization_barrier((rows_y, others[0]))
    grads.append(gradient(local_rows, part_y, rows_x))
    others.append(swap(grads[1], core))
    gathered = jnp.concatenate([gathered, features_near], axis=0)

    planes = [[0], [across, column], [across | column]]

    def add_product(indices, previous, final=False):
        arrays = sum([[grads[i], others[i]] for i in indices], [])
        orders = [sum([[o ^ flip for o in order] for flip in planes[i]], []) for i in indices]
        tiles = 3 if final else 1
        scratch = [
            pltpu.VMEM(proj_weight.shape, jnp.float32),
            pltpu.SemaphoreType.DMA((tiles,)),
        ]
        return kernel_call(
            functools.partial(weight_body, rows, mp_count, gather_order, orders, tiles),
            struct(proj_weight.shape, jnp.float32),
            scratch=scratch if final else (),
            in_specs=[smem] + [vmem] * (1 + len(arrays) + len(previous)),
            out_specs=pl.BlockSpec(memory_space=pl.ANY) if final else vmem,
            flops=0 * 4 * width * embed * local_rows * len(indices),
            name="weight",
        )(place, gathered, *arrays, *previous)

    grad_features = kernel_call(
        functools.partial(features_body, full_width, rows, mp_count),
        struct(features.shape),
        scratch=[pltpu.VMEM((local_rows, embed), jnp.bfloat16)],
        in_specs=[smem] + [vmem] * (2 + mp_count),
        flops=0 * 2 * local_rows * width * embed,
        name="grad_features",
    )(place, proj_weight, weight_sum, grads[0], others[0], grads[1], others[1])
    grad_weight = add_product([0], [])
    *diagonal_rows, _, _ = lax.optimization_barrier((*diagonal_rows, grads[1], grad_weight))
    grads.append(gradient(3 * local_rows, *diagonal_rows))
    others.append(swap(grads[2], core))
    grad_weight = add_product([1], [grad_weight])
    grad_weight = add_product([2], [grad_weight], True)
    return grad_features, grad_weight


def shards(features, proj_weight, texts):
    dp_count, mp_count = lax.axis_size("dp"), lax.axis_size("mp")
    count = dp_count * mp_count
    rows = texts.shape[0]
    embed = texts.shape[1]
    fits = (
        count * rows * (embed + LANES) * 2 <= GATHER_BYTES
        and count & (count - 1) == 0
        and mp_count == 4
        and count == 8 * mp_count
        and features.shape[0] == LANES == mp_count * rows
        and embed % LANES == 0
        and 2 * (embed // LANES) + 3 <= rows
        and rows % 16 == 0
    )
    plan = shards_gathered if fits else shards_summed
    return plan(features, proj_weight, texts)


def solution(mesh):
    return jax.shard_map(
        shards,
        mesh=mesh,
        in_specs=(P("dp", "mp"), P("mp", None), P(("dp", "mp"), None)),
        out_specs=(P("dp", "mp"), P("mp", None)),
        check_vma=False,
    )
```

```python
import functools

import jax
import jax.numpy as jnp
from jax import lax
from jax.experimental import pallas as pl
from jax.experimental.pallas import tpu as pltpu
from jax.sharding import PartitionSpec as P

logit_scale = 100.0
logit_bias = -10.0
epsilon = 1e-06
LANES = 128
GATHER_BYTES = 8 << 20
VMEM_BYTES = 40 << 20


def unit_rows(values):
    return values * lax.rsqrt(jnp.sum(values * values, axis=1, keepdims=True) + epsilon)


def add_texts(unit_img_b, image_ids, piece, piece_ids):
    unit_txt_b = unit_rows(piece.astype(jnp.float32)).astype(jnp.bfloat16)
    logits = (
        logit_scale * jnp.dot(unit_img_b, unit_txt_b.T, preferred_element_type=jnp.float32)
        + logit_bias
    )
    labels = jnp.where(image_ids[:, None] == piece_ids[None, :], 1.0, -1.0).astype(jnp.float32)
    slopes = (-labels * jax.nn.sigmoid(-labels * logits)).astype(jnp.bfloat16)
    return logit_scale * jnp.dot(slopes, unit_txt_b, preferred_element_type=jnp.float32)


def shards_summed(features, proj_weight, texts):
    local_rows = features.shape[0]
    width_local = features.shape[1]
    mp_count = lax.axis_size("mp")
    full_width = width_local * mp_count
    mp_index = lax.axis_index("mp")
    dp_index = lax.axis_index("dp")
    text_rows = texts.shape[0]
    inputs = features.astype(jnp.float32)
    mean_in = lax.psum(jnp.sum(inputs, axis=1, keepdims=True), "mp") / full_width
    centred = inputs - mean_in
    normed_b = centred.astype(jnp.bfloat16)
    partial_proj = jnp.dot(normed_b, proj_weight, preferred_element_type=jnp.float32)
    project = lax.psum(partial_proj, "mp")
    inv_norm = lax.rsqrt(jnp.sum(project * project, axis=1, keepdims=True) + epsilon)
    unit_img = project * inv_norm
    unit_img_b = unit_img.astype(jnp.bfloat16)
    image_ids = dp_index * local_rows + jnp.arange(local_rows, dtype=jnp.int32)
    piece = lax.all_gather(texts, "dp", axis=0, tiled=True)
    positions = jnp.arange(piece.shape[0], dtype=jnp.int32)
    shard_of = positions // text_rows
    piece_ids = (shard_of * mp_count + mp_index) * text_rows + positions % text_rows
    grad_unit = add_texts(unit_img_b, image_ids, piece, piece_ids)
    grad_unit = lax.psum(grad_unit, "mp")
    grad_proj = inv_norm * (
        grad_unit - unit_img * jnp.sum(unit_img * grad_unit, axis=1, keepdims=True)
    )
    grad_proj_b = grad_proj.astype(jnp.bfloat16)
    weight_part = jnp.dot(normed_b.T, grad_proj_b, preferred_element_type=jnp.float32)
    grad_weight = lax.psum(weight_part, "dp")
    grad_normed = jnp.dot(grad_proj_b, proj_weight.T, preferred_element_type=jnp.float32)
    grad_total = lax.psum(jnp.sum(grad_normed, axis=1, keepdims=True), "mp")
    grad_in = grad_normed - grad_total / full_width
    return (grad_in.astype(jnp.bfloat16), grad_weight)


def split_terms(value, count):
    terms = []
    for _ in range(count):
        term = value.astype(jnp.bfloat16).astype(jnp.float32)
        terms.append(term)
        value = value - term
    return terms


def kernel_call(body, outs, scratch=(), flops=0, **names):
    return pl.pallas_call(
        body,
        out_shape=outs,
        scratch_shapes=scratch,
        compiler_params=pltpu.CompilerParams(vmem_limit_bytes=VMEM_BYTES),
        cost_estimate=pl.CostEstimate(flops=flops, bytes_accessed=0, transcendentals=0),
        **names,
    )


def texts_body(texts_ref, out_ref):
    out_ref[...] = unit_rows(texts_ref[...].astype(jnp.float32)).astype(jnp.bfloat16)


def store_sums(extra_ref, column_sum, sum_row):
    extra_ref[...] = jnp.zeros_like(extra_ref)
    at = 0
    for term in split_terms(column_sum, 2):
        for i in range(column_sum.shape[1] // LANES):
            extra_ref[at : at + 1, :] = term[:, i * LANES : (i + 1) * LANES]
            at += 1
    for term in split_terms(sum_row, 3):
        extra_ref[at : at + 1, :] = term
        at += 1
    return extra_ref[...].astype(jnp.bfloat16)


def load_sums(extra, embed):
    chunks = embed // LANES
    extra = extra.astype(jnp.float32)
    column_sum = jnp.concatenate(
        [extra[i : i + 1] + extra[chunks + i : chunks + i + 1] for i in range(chunks)], axis=1
    )
    at = 2 * chunks
    return column_sum, extra[at : at + 1] + extra[at + 1 : at + 2] + extra[at + 2 : at + 3]


def pick_rows(sum_row, rows, group):
    row = lax.broadcasted_iota(jnp.int32, (rows, LANES), 0)
    lane = lax.broadcasted_iota(jnp.int32, (rows, LANES), 1)
    return jnp.sum(jnp.where(lane == row + group * rows, sum_row, 0.0), axis=1, keepdims=True)


def project_body(
    rows, mp_count, place_ref, features_ref, weight_ref,
    keep_ref, send_ref, column_sum_ref, sum_row_ref, extra_ref,
):
    embed = weight_ref.shape[1]
    local_rows, width = features_ref.shape
    values = features_ref[...].astype(jnp.float32)
    row_sum = jnp.sum(values, axis=1, keepdims=True)
    column_sum = jnp.sum(weight_ref[...].astype(jnp.float32), axis=0, keepdims=True)
    row = lax.broadcasted_iota(jnp.int32, (local_rows, LANES), 0)
    lane = lax.broadcasted_iota(jnp.int32, (local_rows, LANES), 1)
    sum_row = jnp.sum(jnp.where(row == lane, row_sum, 0.0), axis=0, keepdims=True)
    ordered = []
    for flip in list(range(0, mp_count, 2)) + list(range(1, mp_count, 2)):
        start = pl.multiple_of(((place_ref[0] ^ flip) & (mp_count - 1)) * rows, rows)
        block = features_ref[pl.ds(start, rows), :].astype(jnp.float32)
        ordered.append(block - jnp.sum(block, axis=1, keepdims=True) / width)
    centred = jnp.concatenate(ordered, axis=0).astype(jnp.bfloat16)
    product = jnp.dot(centred, weight_ref[...], preferred_element_type=jnp.float32)
    half = local_rows // 2
    keep_ref[...] = product[:half]
    send_ref[:, :embed] = product[half:].astype(jnp.bfloat16)
    extra = store_sums(extra_ref, column_sum, sum_row)
    for i in range(half // rows):
        send_ref[i * rows : (i + 1) * rows, embed:] = extra
    column_sum_ref[...] = column_sum
    sum_row_ref[...] = sum_row


def chip_body(
    width, mp_count, place_ref, keep_ref, received_ref, column_sum_ref, sum_row_ref,
    own_ref, send_ref, chip_column_ref, chip_row_ref, extra_ref,
):
    rows = own_ref.shape[0]
    embed = own_ref.shape[1]
    columns = [column_sum_ref[...], None]
    sum_rows = [sum_row_ref[...], None]
    columns[1], sum_rows[1] = load_sums(received_ref[:rows, embed:], embed)
    chip_column = columns[0] + columns[1]
    chip_row = sum_rows[0] + sum_rows[1]
    for i in range(2):
        group = (place_ref[0] ^ (2 * i)) & (mp_count - 1)
        mean = pick_rows(chip_row, rows, group) / (2 * width)
        here = slice(i * rows, (i + 1) * rows)
        total = keep_ref[here, :] + received_ref[here, :embed].astype(jnp.float32)
        for column, sum_row in zip(columns, sum_rows):
            total = total + (pick_rows(sum_row, rows, group) / width - mean) * column
        if i == 0:
            own_ref[...] = total
        else:
            send_ref[:, :embed] = total.astype(jnp.bfloat16)
    send_ref[:, embed:] = store_sums(extra_ref, chip_column, chip_row)
    chip_column_ref[...] = chip_column
    chip_row_ref[...] = chip_row


def rows_body(
    full_width, mp_count, place_ref, own_ref, received_ref, column_sum_ref, sum_row_ref,
    project_ref, weight_sum_ref,
):
    rows, embed = own_ref.shape
    columns = [column_sum_ref[...], None]
    sum_rows = [sum_row_ref[...], None]
    columns[1], sum_rows[1] = load_sums(received_ref[:, embed:], embed)
    group = place_ref[0] & (mp_count - 1)
    mean = pick_rows(sum_rows[0] + sum_rows[1], rows, group) / full_width
    project = own_ref[...] + received_ref[:, :embed].astype(jnp.float32)
    for column, sum_row in zip(columns, sum_rows):
        part_mean = pick_rows(sum_row, rows, group) / (full_width // 2)
        project = project + (part_mean - mean) * column
    project_ref[:, :embed] = project.astype(jnp.bfloat16)
    lane = lax.broadcasted_iota(jnp.int32, (rows, LANES), 1)
    extra = jnp.zeros((rows, LANES), jnp.float32)
    for i, term in enumerate(split_terms(mean, 3)):
        extra = jnp.where(lane == i, term, extra)
    project_ref[:, embed:] = extra.astype(jnp.bfloat16)
    weight_sum_ref[...] = columns[0] + columns[1]


def grad_body(first, count, *refs):
    projects = refs[:count]
    (*texts, out_ref) = refs[count:]
    embed = texts[0].shape[1]
    project = jnp.concatenate([ref[:, :embed] for ref in projects], axis=0).astype(jnp.float32)
    inv_norm = lax.rsqrt(jnp.sum(project * project, axis=1, keepdims=True) + epsilon)
    unit_img = project * inv_norm
    unit_img_b = unit_img.astype(jnp.bfloat16)
    grad_unit = jnp.zeros_like(project)
    at = 0
    for ref in texts:
        unit_txt_b = ref[...]
        logits = (
            logit_scale
            * lax.dot_general(
                unit_img_b,
                unit_txt_b,
                (((1,), (1,)), ((), ())),
                preferred_element_type=jnp.float32,
            )
            + logit_bias
        )
        text = lax.broadcasted_iota(jnp.int32, logits.shape, 1) + at
        image = lax.broadcasted_iota(jnp.int32, logits.shape, 0) + first
        labels = jnp.where(text == image, 1.0, -1.0)
        slopes = (-labels / (1.0 + jnp.exp(labels * logits))).astype(jnp.bfloat16)
        grad_unit = grad_unit + jnp.dot(slopes, unit_txt_b, preferred_element_type=jnp.float32)
        at += unit_txt_b.shape[0]
    grad_unit = logit_scale * grad_unit
    grad_proj = inv_norm * (
        grad_unit - unit_img * jnp.sum(unit_img * grad_unit, axis=1, keepdims=True)
    )
    out_ref[:, :embed] = grad_proj.astype(jnp.bfloat16)
    out_ref[:, embed:] = jnp.concatenate([ref[:, embed:] for ref in projects], axis=0)


def weight_body(
    rows, mp_count, gather_order, orders, tiles, place_ref, features_ref, *refs
):
    count = 2 * len(orders)
    arrays = refs[:count]
    previous = refs[count : count + 1] if len(refs) - count > (1 if tiles == 1 else 3) else ()
    outs = refs[count + len(previous) :]
    embed = outs[0].shape[1]
    blocks = []
    for at, order in enumerate(orders):
        for i in range(2):
            extra = arrays[2 * at + i][:, embed:].astype(jnp.float32)
            mean = extra[:, 0:1] + extra[:, 1:2] + extra[:, 2:3]
            for k, flip in enumerate(order):
                group = (place_ref[0] ^ flip ^ i) & (mp_count - 1)
                start = (gather_order.index(flip - flip % mp_count) * mp_count + group) * rows
                block = features_ref[pl.ds(pl.multiple_of(start, rows), rows), :]
                blocks.append(block.astype(jnp.float32) - mean[k * rows : (k + 1) * rows])
    normed = jnp.concatenate(blocks, axis=0).astype(jnp.bfloat16)
    gradient = jnp.concatenate([array[:, :embed] for array in arrays], axis=0)
    if tiles == 1:
        total = lax.dot_general(
            normed, gradient, (((0,), (0,)), ((), ())), preferred_element_type=jnp.float32
        )
        for ref in previous:
            total = total + ref[...]
        outs[0][...] = total
        return
    out_hbm, total_ref, sent = outs
    wide = gradient.shape[1] // tiles
    copies = []
    for k in range(tiles):
        here = slice(k * wide, (k + 1) * wide)
        total = lax.dot_general(
            normed, gradient[:, here], (((0,), (0,)), ((), ())), preferred_element_type=jnp.float32
        )
        for ref in previous:
            total = total + ref[:, here]
        total_ref[:, here] = total
        copies.append(
            pltpu.make_async_copy(total_ref.at[:, here], out_hbm.at[:, here], sent.at[k])
        )
        copies[-1].start()
    for copy in copies:
        copy.wait()


def features_body(full_width, rows, mp_count, place_ref, weight_ref, weight_sum_ref, *refs):
    (*parts, out_ref, group_ref) = refs
    for flip, part in enumerate(parts):
        start = pl.multiple_of(((place_ref[0] ^ flip) & (mp_count - 1)) * rows, rows)
        group_ref[pl.ds(start, rows), :] = part[:rows, : group_ref.shape[1]]
    group = group_ref[...]
    grad_normed = lax.dot_general(
        group, weight_ref[...], (((1,), (1,)), ((), ())), preferred_element_type=jnp.float32
    )
    grad_total = jnp.sum(group.astype(jnp.float32) * weight_sum_ref[...], axis=1, keepdims=True)
    out_ref[...] = (grad_normed - grad_total / full_width).astype(jnp.bfloat16)


def shards_gathered(features, proj_weight, texts):
    axes = ("dp", "mp")
    dp_count, mp_count = lax.axis_size("dp"), lax.axis_size("mp")
    count = dp_count * mp_count
    plane_count = 2 * mp_count
    local_rows, width = features.shape
    embed = proj_weight.shape[1]
    rows = texts.shape[0]
    half = local_rows // 2
    full_width = width * mp_count
    place = (lax.axis_index("dp") * mp_count + lax.axis_index("mp")).astype(jnp.int32).reshape(1)
    core, across, column = 1, 2, mp_count
    line = list(range(plane_count, count, plane_count))

    def swap(value, flip):
        return lax.ppermute(value, axes, [(i, i ^ flip) for i in range(count)])

    def struct(dims, kind=jnp.bfloat16):
        return jax.ShapeDtypeStruct(dims, kind)

    def along_line(value, order):
        return jnp.concatenate([value] + [swap(value, flip) for flip in order], axis=0)

    smem = pl.BlockSpec(memory_space=pltpu.SMEM)
    vmem = pl.BlockSpec(memory_space=pltpu.VMEM)
    sums = [struct((1, embed), jnp.float32), struct((1, LANES), jnp.float32)]
    extra = pltpu.VMEM((rows, LANES), jnp.float32)

    keep, send, column_sum, sum_row = kernel_call(
        functools.partial(project_body, rows, mp_count),
        [struct((half, embed), jnp.float32), struct((half, embed + LANES))] + sums,
        scratch=[extra],
        in_specs=[smem, vmem, vmem],
        flops=2 * local_rows * width * embed,
        name="project",
    )(place, features, proj_weight)
    own, send, column_sum, sum_row = kernel_call(
        functools.partial(chip_body, width, mp_count),
        [struct((rows, embed), jnp.float32), struct((rows, embed + LANES))] + sums,
        scratch=[extra],
        in_specs=[smem] + [vmem] * 4,
        name="chip_project",
    )(place, keep, swap(send, core), column_sum, sum_row)
    far, near = line[1], line[0]
    order = [0, far, near, far ^ near]
    unit_txt_b = kernel_call(texts_body, struct(texts.shape), name="unit_texts")(texts)
    txt_line = jnp.concatenate(
        [unit_txt_b] + [swap(unit_txt_b, flip) for flip in order[1:]], axis=0
    )
    features_x = swap(features, column)
    send, features_x = lax.optimization_barrier((send, features_x))
    send, txt_line = lax.optimization_barrier((send, txt_line))
    middle = local_rows // 2

    def diagonal(by_y, by_x):
        return jnp.concatenate(
            [swap(by_x[:middle], across), swap(by_y[middle:], column)], axis=0
        )

    txt_y, txt_x = swap(txt_line, across), swap(txt_line, column)
    gathered = jnp.concatenate([features, features_x], axis=0)
    txt_plane = [txt_line, txt_y, txt_x, diagonal(txt_y, txt_x)]

    project, weight_sum = kernel_call(
        functools.partial(rows_body, full_width, mp_count),
        [
            struct((rows, embed + LANES)),
            struct((1, embed), jnp.float32),
        ],
        in_specs=[smem] + [vmem] * 4,
        name="project_rows",
    )(place, own, swap(send, across), column_sum, sum_row)

    far_rows = swap(project, far)
    far_rows, gathered = lax.optimization_barrier((far_rows, gathered))
    line_rows = jnp.concatenate([project, far_rows], axis=0)
    line_rows = jnp.concatenate([line_rows, swap(line_rows, near)], axis=0)
    features_far = swap(gathered, far)
    line_rows, features_far, txt_plane[1], txt_plane[2] = lax.optimization_barrier(
        (line_rows, features_far, txt_plane[1], txt_plane[2])
    )
    gathered = jnp.concatenate([gathered, features_far], axis=0)
    features_near = swap(gathered, near)
    gather_order = sum([[o, o ^ column] for o in order], [])
    all_texts = [jnp.concatenate(txt_plane, axis=0)]
    all_texts.append(swap(all_texts[0], core))
    rows_y, rows_x = swap(line_rows, across), swap(line_rows, column)
    diagonal_rows = [swap(rows_x[:middle], across), swap(rows_y[middle:], column)]

    def gradient(first, *parts):
        total = sum(part.shape[0] for part in parts)
        return kernel_call(
            functools.partial(grad_body, first, len(parts)),
            struct((total, embed + LANES)),
            flops=10 * 4 * total * count * rows * embed,
            name="grad",
        )(*parts, *all_texts)

    grads = [gradient(0, line_rows)]
    others = [swap(grads[0], core)]
    part_y = rows_y
    part_y, others[0] = lax.optimization_barrier((rows_y, others[0]))
    grads.append(gradient(local_rows, part_y, rows_x))
    others.append(swap(grads[1], core))
    gathered = jnp.concatenate([gathered, features_near], axis=0)

    planes = [[0], [across, column], [across | column]]

    def add_product(indices, previous, final=False):
        arrays = sum([[grads[i], others[i]] for i in indices], [])
        orders = [sum([[o ^ flip for o in order] for flip in planes[i]], []) for i in indices]
        tiles = 3 if final else 1
        scratch = [
            pltpu.VMEM(proj_weight.shape, jnp.float32),
            pltpu.SemaphoreType.DMA((tiles,)),
        ]
        return kernel_call(
            functools.partial(weight_body, rows, mp_count, gather_order, orders, tiles),
            struct(proj_weight.shape, jnp.float32),
            scratch=scratch if final else (),
            in_specs=[smem] + [vmem] * (1 + len(arrays) + len(previous)),
            out_specs=pl.BlockSpec(memory_space=pl.ANY) if final else vmem,
            flops=0 * 4 * width * embed * local_rows * len(indices),
            name="weight",
        )(place, gathered, *arrays, *previous)

    grad_features = kernel_call(
        functools.partial(features_body, full_width, rows, mp_count),
        struct(features.shape),
        scratch=[pltpu.VMEM((local_rows, embed), jnp.bfloat16)],
        in_specs=[smem] + [vmem] * (2 + mp_count),
        flops=0 * 2 * local_rows * width * embed,
        name="grad_features",
    )(place, proj_weight, weight_sum, grads[0], others[0], grads[1], others[1])
    grad_weight = add_product([0], [])
    *diagonal_rows, _, _ = lax.optimization_barrier((*diagonal_rows, grads[1], grad_weight))
    grads.append(gradient(3 * local_rows, *diagonal_rows))
    others.append(swap(grads[2], core))
    grad_weight, grad_features = lax.optimization_barrier((grad_weight, grad_features))
    grad_weight = add_product([1, 2], [grad_weight], True)
    return grad_features, grad_weight


def shards(features, proj_weight, texts):
    dp_count, mp_count = lax.axis_size("dp"), lax.axis_size("mp")
    count = dp_count * mp_count
    rows = texts.shape[0]
    embed = texts.shape[1]
    fits = (
        count * rows * (embed + LANES) * 2 <= GATHER_BYTES
        and count & (count - 1) == 0
        and mp_count == 4
        and count == 8 * mp_count
        and features.shape[0] == LANES == mp_count * rows
        and embed % LANES == 0
        and 2 * (embed // LANES) + 3 <= rows
        and rows % 16 == 0
    )
    plan = shards_gathered if fits else shards_summed
    return plan(features, proj_weight, texts)


def solution(mesh):
    return jax.shard_map(
        shards,
        mesh=mesh,
        in_specs=(P("dp", "mp"), P("mp", None), P(("dp", "mp"), None)),
        out_specs=(P("dp", "mp"), P("mp", None)),
        check_vma=False,
    )
```

```python
import functools

import jax
import jax.numpy as jnp
from jax import lax
from jax.experimental import pallas as pl
from jax.experimental.pallas import tpu as pltpu
from jax.sharding import PartitionSpec as P

logit_scale = 100.0
logit_bias = -10.0
epsilon = 1e-06
LANES = 128
GATHER_BYTES = 8 << 20
VMEM_BYTES = 40 << 20


def unit_rows(values):
    return values * lax.rsqrt(jnp.sum(values * values, axis=1, keepdims=True) + epsilon)


def add_texts(unit_img_b, image_ids, piece, piece_ids):
    unit_txt_b = unit_rows(piece.astype(jnp.float32)).astype(jnp.bfloat16)
    logits = (
        logit_scale * jnp.dot(unit_img_b, unit_txt_b.T, preferred_element_type=jnp.float32)
        + logit_bias
    )
    labels = jnp.where(image_ids[:, None] == piece_ids[None, :], 1.0, -1.0).astype(jnp.float32)
    slopes = (-labels * jax.nn.sigmoid(-labels * logits)).astype(jnp.bfloat16)
    return logit_scale * jnp.dot(slopes, unit_txt_b, preferred_element_type=jnp.float32)


def shards_summed(features, proj_weight, texts):
    local_rows = features.shape[0]
    width_local = features.shape[1]
    mp_count = lax.axis_size("mp")
    full_width = width_local * mp_count
    mp_index = lax.axis_index("mp")
    dp_index = lax.axis_index("dp")
    text_rows = texts.shape[0]
    inputs = features.astype(jnp.float32)
    mean_in = lax.psum(jnp.sum(inputs, axis=1, keepdims=True), "mp") / full_width
    centred = inputs - mean_in
    normed_b = centred.astype(jnp.bfloat16)
    partial_proj = jnp.dot(normed_b, proj_weight, preferred_element_type=jnp.float32)
    project = lax.psum(partial_proj, "mp")
    inv_norm = lax.rsqrt(jnp.sum(project * project, axis=1, keepdims=True) + epsilon)
    unit_img = project * inv_norm
    unit_img_b = unit_img.astype(jnp.bfloat16)
    image_ids = dp_index * local_rows + jnp.arange(local_rows, dtype=jnp.int32)
    piece = lax.all_gather(texts, "dp", axis=0, tiled=True)
    positions = jnp.arange(piece.shape[0], dtype=jnp.int32)
    shard_of = positions // text_rows
    piece_ids = (shard_of * mp_count + mp_index) * text_rows + positions % text_rows
    grad_unit = add_texts(unit_img_b, image_ids, piece, piece_ids)
    grad_unit = lax.psum(grad_unit, "mp")
    grad_proj = inv_norm * (
        grad_unit - unit_img * jnp.sum(unit_img * grad_unit, axis=1, keepdims=True)
    )
    grad_proj_b = grad_proj.astype(jnp.bfloat16)
    weight_part = jnp.dot(normed_b.T, grad_proj_b, preferred_element_type=jnp.float32)
    grad_weight = lax.psum(weight_part, "dp")
    grad_normed = jnp.dot(grad_proj_b, proj_weight.T, preferred_element_type=jnp.float32)
    grad_total = lax.psum(jnp.sum(grad_normed, axis=1, keepdims=True), "mp")
    grad_in = grad_normed - grad_total / full_width
    return (grad_in.astype(jnp.bfloat16), grad_weight)


def split_terms(value, count):
    terms = []
    for _ in range(count):
        term = value.astype(jnp.bfloat16).astype(jnp.float32)
        terms.append(term)
        value = value - term
    return terms


def kernel_call(body, outs, scratch=(), flops=0, **names):
    return pl.pallas_call(
        body,
        out_shape=outs,
        scratch_shapes=scratch,
        compiler_params=pltpu.CompilerParams(vmem_limit_bytes=VMEM_BYTES),
        cost_estimate=pl.CostEstimate(flops=flops, bytes_accessed=0, transcendentals=0),
        **names,
    )


def texts_body(texts_ref, out_ref):
    out_ref[...] = unit_rows(texts_ref[...].astype(jnp.float32)).astype(jnp.bfloat16)


def store_sums(extra_ref, column_sum, sum_row):
    extra_ref[...] = jnp.zeros_like(extra_ref)
    at = 0
    for term in split_terms(column_sum, 2):
        for i in range(column_sum.shape[1] // LANES):
            extra_ref[at : at + 1, :] = term[:, i * LANES : (i + 1) * LANES]
            at += 1
    for term in split_terms(sum_row, 3):
        extra_ref[at : at + 1, :] = term
        at += 1
    return extra_ref[...].astype(jnp.bfloat16)


def load_sums(extra, embed):
    chunks = embed // LANES
    extra = extra.astype(jnp.float32)
    column_sum = jnp.concatenate(
        [extra[i : i + 1] + extra[chunks + i : chunks + i + 1] for i in range(chunks)], axis=1
    )
    at = 2 * chunks
    return column_sum, extra[at : at + 1] + extra[at + 1 : at + 2] + extra[at + 2 : at + 3]


def pick_rows(sum_row, rows, group):
    row = lax.broadcasted_iota(jnp.int32, (rows, LANES), 0)
    lane = lax.broadcasted_iota(jnp.int32, (rows, LANES), 1)
    return jnp.sum(jnp.where(lane == row + group * rows, sum_row, 0.0), axis=1, keepdims=True)


def project_body(
    rows, mp_count, place_ref, features_ref, weight_ref,
    keep_ref, send_ref, column_sum_ref, sum_row_ref, extra_ref,
):
    embed = weight_ref.shape[1]
    local_rows, width = features_ref.shape
    values = features_ref[...].astype(jnp.float32)
    row_sum = jnp.sum(values, axis=1, keepdims=True)
    column_sum = jnp.sum(weight_ref[...].astype(jnp.float32), axis=0, keepdims=True)
    row = lax.broadcasted_iota(jnp.int32, (local_rows, LANES), 0)
    lane = lax.broadcasted_iota(jnp.int32, (local_rows, LANES), 1)
    sum_row = jnp.sum(jnp.where(row == lane, row_sum, 0.0), axis=0, keepdims=True)
    ordered = []
    for flip in list(range(0, mp_count, 2)) + list(range(1, mp_count, 2)):
        start = pl.multiple_of(((place_ref[0] ^ flip) & (mp_count - 1)) * rows, rows)
        block = features_ref[pl.ds(start, rows), :].astype(jnp.float32)
        ordered.append(block - jnp.sum(block, axis=1, keepdims=True) / width)
    centred = jnp.concatenate(ordered, axis=0).astype(jnp.bfloat16)
    product = jnp.dot(centred, weight_ref[...], preferred_element_type=jnp.float32)
    half = local_rows // 2
    keep_ref[...] = product[:half]
    send_ref[:, :embed] = product[half:].astype(jnp.bfloat16)
    extra = store_sums(extra_ref, column_sum, sum_row)
    for i in range(half // rows):
        send_ref[i * rows : (i + 1) * rows, embed:] = extra
    column_sum_ref[...] = column_sum
    sum_row_ref[...] = sum_row


def chip_body(
    width, mp_count, place_ref, keep_ref, received_ref, column_sum_ref, sum_row_ref,
    own_ref, send_ref, chip_column_ref, chip_row_ref, extra_ref,
):
    rows = own_ref.shape[0]
    embed = own_ref.shape[1]
    columns = [column_sum_ref[...], None]
    sum_rows = [sum_row_ref[...], None]
    columns[1], sum_rows[1] = load_sums(received_ref[:rows, embed:], embed)
    chip_column = columns[0] + columns[1]
    chip_row = sum_rows[0] + sum_rows[1]
    for i in range(2):
        group = (place_ref[0] ^ (2 * i)) & (mp_count - 1)
        mean = pick_rows(chip_row, rows, group) / (2 * width)
        here = slice(i * rows, (i + 1) * rows)
        total = keep_ref[here, :] + received_ref[here, :embed].astype(jnp.float32)
        for column, sum_row in zip(columns, sum_rows):
            total = total + (pick_rows(sum_row, rows, group) / width - mean) * column
        if i == 0:
            own_ref[...] = total
        else:
            send_ref[:, :embed] = total.astype(jnp.bfloat16)
    send_ref[:, embed:] = store_sums(extra_ref, chip_column, chip_row)
    chip_column_ref[...] = chip_column
    chip_row_ref[...] = chip_row


def rows_body(
    full_width, mp_count, place_ref, own_ref, received_ref, column_sum_ref, sum_row_ref,
    project_ref, weight_sum_ref,
):
    rows, embed = own_ref.shape
    columns = [column_sum_ref[...], None]
    sum_rows = [sum_row_ref[...], None]
    columns[1], sum_rows[1] = load_sums(received_ref[:, embed:], embed)
    group = place_ref[0] & (mp_count - 1)
    mean = pick_rows(sum_rows[0] + sum_rows[1], rows, group) / full_width
    project = own_ref[...] + received_ref[:, :embed].astype(jnp.float32)
    for column, sum_row in zip(columns, sum_rows):
        part_mean = pick_rows(sum_row, rows, group) / (full_width // 2)
        project = project + (part_mean - mean) * column
    project_ref[:, :embed] = project.astype(jnp.bfloat16)
    lane = lax.broadcasted_iota(jnp.int32, (rows, LANES), 1)
    extra = jnp.zeros((rows, LANES), jnp.float32)
    for i, term in enumerate(split_terms(mean, 3)):
        extra = jnp.where(lane == i, term, extra)
    project_ref[:, embed:] = extra.astype(jnp.bfloat16)
    weight_sum_ref[...] = columns[0] + columns[1]


def grad_body(first, count, *refs):
    projects = refs[:count]
    (*texts, out_ref) = refs[count:]
    embed = texts[0].shape[1]
    project = jnp.concatenate([ref[:, :embed] for ref in projects], axis=0).astype(jnp.float32)
    inv_norm = lax.rsqrt(jnp.sum(project * project, axis=1, keepdims=True) + epsilon)
    unit_img = project * inv_norm
    unit_img_b = unit_img.astype(jnp.bfloat16)
    grad_unit = jnp.zeros_like(project)
    at = 0
    for ref in texts:
        unit_txt_b = ref[...]
        logits = (
            logit_scale
            * lax.dot_general(
                unit_img_b,
                unit_txt_b,
                (((1,), (1,)), ((), ())),
                preferred_element_type=jnp.float32,
            )
            + logit_bias
        )
        text = lax.broadcasted_iota(jnp.int32, logits.shape, 1) + at
        image = lax.broadcasted_iota(jnp.int32, logits.shape, 0) + first
        labels = jnp.where(text == image, 1.0, -1.0)
        slopes = (-labels / (1.0 + jnp.exp(labels * logits))).astype(jnp.bfloat16)
        grad_unit = grad_unit + jnp.dot(slopes, unit_txt_b, preferred_element_type=jnp.float32)
        at += unit_txt_b.shape[0]
    grad_unit = logit_scale * grad_unit
    grad_proj = inv_norm * (
        grad_unit - unit_img * jnp.sum(unit_img * grad_unit, axis=1, keepdims=True)
    )
    out_ref[:, :embed] = grad_proj.astype(jnp.bfloat16)
    out_ref[:, embed:] = jnp.concatenate([ref[:, embed:] for ref in projects], axis=0)


def weight_body(
    rows, mp_count, gather_order, orders, tiles, place_ref, features_ref, *refs
):
    count = 2 * len(orders)
    arrays = refs[:count]
    previous = refs[count : count + 1] if len(refs) - count > (1 if tiles == 1 else 3) else ()
    outs = refs[count + len(previous) :]
    embed = outs[0].shape[1]
    blocks = []
    for at, order in enumerate(orders):
        for i in range(2):
            extra = arrays[2 * at + i][:, embed:].astype(jnp.float32)
            mean = extra[:, 0:1] + extra[:, 1:2] + extra[:, 2:3]
            for k, flip in enumerate(order):
                group = (place_ref[0] ^ flip ^ i) & (mp_count - 1)
                start = (gather_order.index(flip - flip % mp_count) * mp_count + group) * rows
                block = features_ref[pl.ds(pl.multiple_of(start, rows), rows), :]
                blocks.append(block.astype(jnp.float32) - mean[k * rows : (k + 1) * rows])
    normed = jnp.concatenate(blocks, axis=0).astype(jnp.bfloat16)
    gradient = jnp.concatenate([array[:, :embed] for array in arrays], axis=0)
    if tiles == 1:
        total = lax.dot_general(
            normed, gradient, (((0,), (0,)), ((), ())), preferred_element_type=jnp.float32
        )
        for ref in previous:
            total = total + ref[...]
        outs[0][...] = total
        return
    out_hbm, total_ref, sent = outs
    high = normed.shape[1] // tiles
    copies = []
    for k in range(tiles):
        here = slice(k * high, (k + 1) * high)
        total = lax.dot_general(
            normed[:, here], gradient, (((0,), (0,)), ((), ())), preferred_element_type=jnp.float32
        )
        for ref in previous:
            total = total + ref[here, :]
        total_ref[here, :] = total
        copies.append(
            pltpu.make_async_copy(total_ref.at[here, :], out_hbm.at[here, :], sent.at[k])
        )
        copies[-1].start()
    for copy in copies:
        copy.wait()


def features_body(full_width, rows, mp_count, place_ref, weight_ref, weight_sum_ref, *refs):
    (*parts, out_ref, group_ref) = refs
    for flip, part in enumerate(parts):
        start = pl.multiple_of(((place_ref[0] ^ flip) & (mp_count - 1)) * rows, rows)
        group_ref[pl.ds(start, rows), :] = part[:rows, : group_ref.shape[1]]
    group = group_ref[...]
    grad_normed = lax.dot_general(
        group, weight_ref[...], (((1,), (1,)), ((), ())), preferred_element_type=jnp.float32
    )
    grad_total = jnp.sum(group.astype(jnp.float32) * weight_sum_ref[...], axis=1, keepdims=True)
    out_ref[...] = (grad_normed - grad_total / full_width).astype(jnp.bfloat16)


def shards_gathered(features, proj_weight, texts):
    axes = ("dp", "mp")
    dp_count, mp_count = lax.axis_size("dp"), lax.axis_size("mp")
    count = dp_count * mp_count
    plane_count = 2 * mp_count
    local_rows, width = features.shape
    embed = proj_weight.shape[1]
    rows = texts.shape[0]
    half = local_rows // 2
    full_width = width * mp_count
    place = (lax.axis_index("dp") * mp_count + lax.axis_index("mp")).astype(jnp.int32).reshape(1)
    core, across, column = 1, 2, mp_count
    line = list(range(plane_count, count, plane_count))

    def swap(value, flip):
        return lax.ppermute(value, axes, [(i, i ^ flip) for i in range(count)])

    def struct(dims, kind=jnp.bfloat16):
        return jax.ShapeDtypeStruct(dims, kind)

    def along_line(value, order):
        return jnp.concatenate([value] + [swap(value, flip) for flip in order], axis=0)

    smem = pl.BlockSpec(memory_space=pltpu.SMEM)
    vmem = pl.BlockSpec(memory_space=pltpu.VMEM)
    sums = [struct((1, embed), jnp.float32), struct((1, LANES), jnp.float32)]
    extra = pltpu.VMEM((rows, LANES), jnp.float32)

    keep, send, column_sum, sum_row = kernel_call(
        functools.partial(project_body, rows, mp_count),
        [struct((half, embed), jnp.float32), struct((half, embed + LANES))] + sums,
        scratch=[extra],
        in_specs=[smem, vmem, vmem],
        flops=2 * local_rows * width * embed,
        name="project",
    )(place, features, proj_weight)
    own, send, column_sum, sum_row = kernel_call(
        functools.partial(chip_body, width, mp_count),
        [struct((rows, embed), jnp.float32), struct((rows, embed + LANES))] + sums,
        scratch=[extra],
        in_specs=[smem] + [vmem] * 4,
        name="chip_project",
    )(place, keep, swap(send, core), column_sum, sum_row)
    far, near = line[1], line[0]
    order = [0, far, near, far ^ near]
    unit_txt_b = kernel_call(texts_body, struct(texts.shape), name="unit_texts")(texts)
    txt_line = jnp.concatenate(
        [unit_txt_b] + [swap(unit_txt_b, flip) for flip in order[1:]], axis=0
    )
    features_x = swap(features, column)
    send, features_x = lax.optimization_barrier((send, features_x))
    send, txt_line = lax.optimization_barrier((send, txt_line))
    middle = local_rows // 2

    def diagonal(by_y, by_x):
        return jnp.concatenate(
            [swap(by_x[:middle], across), swap(by_y[middle:], column)], axis=0
        )

    txt_y, txt_x = swap(txt_line, across), swap(txt_line, column)
    gathered = jnp.concatenate([features, features_x], axis=0)
    txt_plane = [txt_line, txt_y, txt_x, diagonal(txt_y, txt_x)]

    project, weight_sum = kernel_call(
        functools.partial(rows_body, full_width, mp_count),
        [
            struct((rows, embed + LANES)),
            struct((1, embed), jnp.float32),
        ],
        in_specs=[smem] + [vmem] * 4,
        name="project_rows",
    )(place, own, swap(send, across), column_sum, sum_row)

    far_rows = swap(project, far)
    far_rows, gathered = lax.optimization_barrier((far_rows, gathered))
    line_rows = jnp.concatenate([project, far_rows], axis=0)
    line_rows = jnp.concatenate([line_rows, swap(line_rows, near)], axis=0)
    features_far = swap(gathered, far)
    line_rows, features_far, txt_plane[1], txt_plane[2] = lax.optimization_barrier(
        (line_rows, features_far, txt_plane[1], txt_plane[2])
    )
    gathered = jnp.concatenate([gathered, features_far], axis=0)
    features_near = swap(gathered, near)
    gather_order = sum([[o, o ^ column] for o in order], [])
    all_texts = [jnp.concatenate(txt_plane, axis=0)]
    all_texts.append(swap(all_texts[0], core))
    rows_y, rows_x = swap(line_rows, across), swap(line_rows, column)
    diagonal_rows = [swap(rows_x[:middle], across), swap(rows_y[middle:], column)]

    def gradient(first, *parts):
        total = sum(part.shape[0] for part in parts)
        return kernel_call(
            functools.partial(grad_body, first, len(parts)),
            struct((total, embed + LANES)),
            flops=10 * 4 * total * count * rows * embed,
            name="grad",
        )(*parts, *all_texts)

    grads = [gradient(0, line_rows)]
    others = [swap(grads[0], core)]
    part_y = rows_y
    part_y, others[0] = lax.optimization_barrier((rows_y, others[0]))
    grads.append(gradient(local_rows, part_y, rows_x))
    others.append(swap(grads[1], core))
    gathered = jnp.concatenate([gathered, features_near], axis=0)

    planes = [[0], [across, column], [across | column]]

    def add_product(indices, previous, final=False):
        arrays = sum([[grads[i], others[i]] for i in indices], [])
        orders = [sum([[o ^ flip for o in order] for flip in planes[i]], []) for i in indices]
        tiles = 3 if final else 1
        scratch = [
            pltpu.VMEM(proj_weight.shape, jnp.float32),
            pltpu.SemaphoreType.DMA((tiles,)),
        ]
        return kernel_call(
            functools.partial(weight_body, rows, mp_count, gather_order, orders, tiles),
            struct(proj_weight.shape, jnp.float32),
            scratch=scratch if final else (),
            in_specs=[smem] + [vmem] * (1 + len(arrays) + len(previous)),
            out_specs=pl.BlockSpec(memory_space=pl.ANY) if final else vmem,
            flops=0 * 4 * width * embed * local_rows * len(indices),
            name="weight",
        )(place, gathered, *arrays, *previous)

    grad_features = kernel_call(
        functools.partial(features_body, full_width, rows, mp_count),
        struct(features.shape),
        scratch=[pltpu.VMEM((local_rows, embed), jnp.bfloat16)],
        in_specs=[smem] + [vmem] * (2 + mp_count),
        flops=0 * 2 * local_rows * width * embed,
        name="grad_features",
    )(place, proj_weight, weight_sum, grads[0], others[0], grads[1], others[1])
    grad_weight = add_product([0], [])
    *diagonal_rows, _, _ = lax.optimization_barrier((*diagonal_rows, grads[1], grad_weight))
    grads.append(gradient(3 * local_rows, *diagonal_rows))
    others.append(swap(grads[2], core))
    grad_weight = add_product([1], [grad_weight])
    grad_weight = add_product([2], [grad_weight], True)
    return grad_features, grad_weight


def shards(features, proj_weight, texts):
    dp_count, mp_count = lax.axis_size("dp"), lax.axis_size("mp")
    count = dp_count * mp_count
    rows = texts.shape[0]
    embed = texts.shape[1]
    fits = (
        count * rows * (embed + LANES) * 2 <= GATHER_BYTES
        and count & (count - 1) == 0
        and mp_count == 4
        and count == 8 * mp_count
        and features.shape[0] == LANES == mp_count * rows
        and embed % LANES == 0
        and 2 * (embed // LANES) + 3 <= rows
        and rows % 16 == 0
    )
    plan = shards_gathered if fits else shards_summed
    return plan(features, proj_weight, texts)


def solution(mesh):
    return jax.shard_map(
        shards,
        mesh=mesh,
        in_specs=(P("dp", "mp"), P("mp", None), P(("dp", "mp"), None)),
        out_specs=(P("dp", "mp"), P("mp", None)),
        check_vma=False,
    )
```
